32 devices in a mesh: dp: 8 (over z, x), seq: 4 (over y, core).
Axes of the slice: x: 2, y: 2, z: 4, core: 2. Of those that a mesh axis runs over, the one named last changes fastest.
Arguments:
- frames: float32 [8192, 1024], P(('dp', 'seq')), may hold values from -6 to 6
- time_embed: float32 [8, 1024], P('dp'), may hold values from -6 to 6
- clip_len: int32 [8, 6], P('dp'), may hold values from 1 to 512, 1024 in all within a row
- w_qkv: bfloat16 [1024, 3072], P('dp'), may hold values from -0.1875 to 0.1875
- b_qkv: bfloat16 [3072], P('dp'), may hold values from -1.75 to 1.75
- w_out: bfloat16 [1024, 1024], P('dp'), may hold values from -1.5 to 1.5
- b_out: bfloat16 [1024], P('dp'), may hold values from -1.75 to 1.75
- w_up: bfloat16 [1024, 2048], P('dp'), may hold values from -0.1875 to 0.1875
- b_up: bfloat16 [2048], P('dp'), may hold values from -1.75 to 1.75
- w_down: bfloat16 [2048, 1024], P('dp'), may hold values from -0.25 to 0.25
- b_down: bfloat16 [1024], P('dp'), may hold values from -1.75 to 1.75
- w_mod: bfloat16 [1024, 6144], P('dp'), may hold values from -0.1875 to 0.1875
- b_mod: bfloat16 [6144], P('dp'), may hold values from -2.5 to 2.5
- cotangent: float32 [8192, 1024], P(('dp', 'seq')), may hold values from -6 to 6
Outputs:
- block_out: float32 [8192, 1024], P(('dp', 'seq'))
- grad_input: float32 [8192, 1024], P(('dp', 'seq'))
- grad_time: float32 [8, 1024], P('dp')
- grad_w_qkv: float32 [1024, 3072], P('dp')
- grad_b_qkv: float32 [3072], P('dp')
- grad_w_out: float32 [1024, 1024], P('dp')
- grad_b_out: float32 [1024], P('dp')
- grad_w_up: float32 [1024, 2048], P('dp')
- grad_b_up: float32 [2048], P('dp')
- grad_w_down: float32 [2048, 1024], P('dp')
- grad_b_down: float32 [1024], P('dp')
- grad_w_mod: float32 [1024, 6144], P('dp')
- grad_b_mod: float32 [6144], P('dp')
The draws below stay inside these ranges and needn't reach their ends.
Inputs may be any that keep to these rules, and one draw needn't show every extreme that they name: `clip_len`: each row sums to 1024; each row's longest clip has exactly 512 frames.
All inputs are finite; a program needn't handle non-finite values.
Results may differ from the reference program's by a relative error of at most 0.015.
The reference program's roundings to bfloat16 on the way count: a program that leaves them out, or rounds other values in their place, can miss the bound.
Values may be sent and summed in bfloat16 or wider, within the bound.
A program may use at most 192 MiB of HBM per device.

```python
import math
import jax
import jax.numpy as jnp
import numpy as np
from jax import lax

D = 1024
FF = 2048
HEADS = 16
HEAD = 64
CLIPS = 6
ITEMS = 8
ITEM_LEN = 1024
TOKENS = 8192


def level_of(key, shape, cuts, smallest, top_value):
    factor_of, own = 1.0, jax.random.fold_in(key, 6)
    for position, shards_of in cuts:
        steps = jnp.exp(jax.random.uniform(jax.random.fold_in(own, position), (shards_of,), jnp.float32, smallest / len(cuts), top_value / len(cuts)))
        factor_of = factor_of * jnp.repeat(steps, shape[position] // shards_of).reshape([-1 if axis == position else 1 for axis in range(len(shape))])
    return factor_of


def length_profile(number_of, total, limit, skew):
    weights = [(1 << 20) // math.isqrt(rank ** skew) + 1 for rank in range(2, number_of + 1)]
    surplus, counts = total - limit - (number_of - 1), [1] * (number_of - 1)
    while surplus > 0:
        movable = [i for i in range(number_of - 1) if counts[i] < limit]
        mass, budget = sum([weights[i] for i in movable]), surplus
        for i in movable:
            extra = min(limit - counts[i], max(1, budget * weights[i] // mass), surplus)
            counts[i] = counts[i] + extra
            surplus = surplus - extra
    return np.array([limit] + counts)


def uneven_parts(rng, count, total, reach, slope):
    if count == 2:
        one = jax.random.randint(rng, (), max(1, total - reach), min(reach, total - 1) + 1)
        return jnp.stack([one, total - one])
    sizes = jnp.asarray(length_profile(count, total, reach, slope), jnp.int32)
    twos = (count - 1) // 2
    giver, sink = sizes[1:1 + 2 * twos:2], sizes[2:2 + 2 * twos:2]
    margin = jnp.minimum(giver - 1, reach - sink)
    shifted = jax.random.randint(jax.random.fold_in(rng, 1), (twos,), 0, 1 << 20) % (margin + 1)
    sizes = sizes.at[1:1 + 2 * twos:2].set(giver - shifted).at[2:2 + 2 * twos:2].set(sink + shifted)
    return sizes[jax.random.permutation(jax.random.fold_in(rng, 2), count)]


def gaussian(key, shape, spread, reach, cuts=(), kind=jnp.bfloat16):
    entries = spread * jax.random.normal(key, shape, jnp.float32)
    if cuts:
        entries = entries * level_of(key, shape, cuts, -0.22, 0.18)
    return jnp.clip(entries, -reach, reach).astype(kind)


def setup_inputs(seed: int = 0) -> dict:
    keys = jax.random.split(jax.random.key(seed), 15)
    return {
        "frames": gaussian(keys[0], (TOKENS, D), 1.0, 6.0, ((0, 32),), jnp.float32),
        "time_embed": gaussian(keys[1], (ITEMS, D), 1.0, 6.0, ((0, 8),), jnp.float32),
        "clip_len": jax.vmap(lambda own: uneven_parts(own, CLIPS, ITEM_LEN, ITEM_LEN // 2, 2))(jax.random.split(keys[2], ITEMS)).reshape((ITEMS, CLIPS)).astype(jnp.int32),
        "w_qkv": gaussian(keys[3], (D, 3 * D), D ** -0.5, 0.1875, ((0, 8),)),
        "b_qkv": gaussian(keys[4], (3 * D,), 0.3, 1.75, ((0, 8),)),
        "w_out": gaussian(keys[5], (D, D), (D // 64) ** -0.5, 1.5, ((0, 8),)),
        "b_out": gaussian(keys[6], (D,), 0.3, 1.75, ((0, 8),)),
        "w_up": gaussian(keys[7], (D, FF), D ** -0.5, 0.1875, ((0, 8),)),
        "b_up": gaussian(keys[8], (FF,), 0.3, 1.75, ((0, 8),)),
        "w_down": gaussian(keys[9], (FF, D), (FF // 4) ** -0.5, 0.25, ((0, 8),)),
        "b_down": gaussian(keys[10], (D,), 0.3, 1.75, ((0, 8),)),
        "w_mod": gaussian(keys[11], (D, 6 * D), D ** -0.5, 0.1875, ((0, 8),)),
        "b_mod": gaussian(keys[12], (6 * D,), 0.4, 2.5, ((0, 8),)),
        "cotangent": gaussian(keys[13], (TOKENS, D), 1.0, 6.0, ((0, 32),), jnp.float32),
    }


@jax.custom_vjp
def low(v):
    return lax.optimization_barrier(v.astype(jnp.bfloat16)).astype(jnp.float32)

@jax.custom_vjp
def low_back(v):
    return v

def low_keep(v):
    return (low(v), None)

def low_pass(kept, grad):
    return (grad,)

def back_keep(v):
    return (v, None)

def back_low(kept, grad):
    return (low(grad),)
low.defvjp(low_keep, low_pass)
low_back.defvjp(back_keep, back_low)
precise = lax.Precision.HIGHEST
norm_eps = 1e-06

def product(left_side, right_side):
    return jnp.dot(left_side, right_side, precision=precise)

def layer_norm(values):
    mean_val = lax.optimization_barrier(jnp.mean(values, axis=-1, keepdims=True))
    centred = values - mean_val
    variance = lax.optimization_barrier(jnp.mean(centred * centred, axis=-1, keepdims=True))
    return centred * lax.rsqrt(variance + norm_eps)

def rotate(values, cosine_tab, sine_tab):
    half_dim = values.shape[-1] // 2
    lower_half = values[..., :half_dim]
    upper_half = values[..., half_dim:]
    return jnp.concatenate([lower_half * cosine_tab - upper_half * sine_tab, upper_half * cosine_tab + lower_half * sine_tab], axis=-1)

def angles(positions):
    half_dim = HEAD // 2
    inv_rate = jnp.exp(jnp.arange(half_dim, dtype=jnp.float32) * (-2.0 * math.log(10000.0) / HEAD))
    phases = positions.astype(jnp.float32)[:, None] * inv_rate[None, :]
    return (jnp.cos(phases)[:, None, :], jnp.sin(phases)[:, None, :])

def layout(lengths):
    clip_end = jnp.cumsum(lengths).astype(jnp.int32)
    clip_start = (clip_end - lengths).astype(jnp.int32)
    frame_pos = jnp.arange(ITEM_LEN, dtype=jnp.int32)
    inside = (frame_pos[:, None] >= clip_start[None, :]) & (frame_pos[:, None] < clip_end[None, :])
    clip_ids = lax.optimization_barrier(jnp.sum(jnp.where(inside, jnp.arange(CLIPS, dtype=jnp.int32)[None, :], 0), axis=1)).astype(jnp.int32)
    positions = (frame_pos - lax.optimization_barrier(jnp.sum(jnp.where(inside, clip_start[None, :], 0), axis=1))).astype(jnp.int32)
    return (clip_ids, positions)

def attend(query, keys_all, values_all, clip_ids):
    block_rows = min(512, ITEM_LEN)
    block_count = ITEM_LEN // block_rows
    factor = HEAD ** (-0.5)

    def one_block(inputs):
        query_blk, clip_blk = inputs
        raw_scores = jnp.einsum('qhe,khe->hqk', query_blk, keys_all, precision=precise) * factor
        same_clip = clip_blk[:, None] == clip_ids[None, :]
        scores = low_back(jnp.where(same_clip[None], raw_scores, -1e+30))
        attn_prob = low(jax.nn.softmax(scores, axis=-1))
        return jnp.einsum('hqk,khe->qhe', attn_prob, values_all, precision=precise)
    blocks_out = lax.map(jax.checkpoint(one_block), (query.reshape(block_count, block_rows, HEADS, HEAD), clip_ids.reshape(block_count, block_rows)))
    return blocks_out.reshape(ITEM_LEN, HEADS * HEAD)

def layer(weights_all, x_item, t_item, lengths):
    w_qkv, b_qkv, w_out, b_out, w_up, b_up, w_down, b_down, w_mod, b_mod = weights_all
    clip_ids, positions = layout(lengths)
    cosine_tab, sine_tab = angles(positions)
    time_act = low(jax.nn.silu(t_item))[None, :]
    modulation = low_back(product(time_act, w_mod) + b_mod)
    shift_a, scale_a, gate_a, shift_f, scale_f, gate_f = jnp.split(modulation, 6, axis=1)
    x_a = low(layer_norm(x_item) * (1.0 + scale_a) + shift_a)
    projected = low_back(product(x_a, w_qkv) + b_qkv)
    pieces = projected.reshape(ITEM_LEN, 3, HEADS, HEAD)
    query = low_back(low(rotate(pieces[:, 0], cosine_tab, sine_tab)))
    keys_all = low_back(low(rotate(pieces[:, 1], cosine_tab, sine_tab)))
    values_all = low_back(low(pieces[:, 2]))
    attn_out = low_back(low(attend(query, keys_all, values_all, clip_ids)))
    attn_branch = low_back(product(attn_out, w_out) + b_out)
    x_mid = x_item + gate_a * attn_branch
    x_f = low(layer_norm(x_mid) * (1.0 + scale_f) + shift_f)
    hidden = low_back(product(x_f, w_up) + b_up)
    gelu_act = low(jax.nn.gelu(hidden, approximate=True))
    ffn_branch = low_back(product(gelu_act, w_down) + b_down)
    return x_mid + gate_f * ffn_branch

def reference(frames, time_embed, clip_len, w_qkv, b_qkv, w_out, b_out, w_up, b_up, w_down, b_down, w_mod, b_mod, cotangent):
    weights_all = tuple((w.astype(jnp.float32) for w in (w_qkv, b_qkv, w_out, b_out, w_up, b_up, w_down, b_down, w_mod, b_mod)))

    def forward(weights_in, frames_in, time_in):

        def item_step(running, inputs):
            x_item, t_item, lengths = inputs
            return (running, jax.checkpoint(layer)(weights_in, x_item, t_item, lengths))
        _, stacked = lax.scan(item_step, jnp.zeros((), jnp.float32), (frames_in.reshape(ITEMS, ITEM_LEN, D), time_in, clip_len))
        return stacked.reshape(ITEMS * ITEM_LEN, D)
    block_out, pullback = jax.vjp(forward, weights_all, frames.astype(jnp.float32), time_embed.astype(jnp.float32))
    grad_weights, grad_input, grad_time = pullback(cotangent.astype(jnp.float32))
    g_wq, g_bq, g_wo, g_bo, g_wu, g_bu, g_wd, g_bd, g_wm, g_bm = grad_weights
    return (block_out, grad_input, grad_time, g_wq, g_bq, g_wo, g_bo, g_wu, g_bu, g_wd, g_bd, g_wm, g_bm)
```

```python
import math

import jax
import jax.numpy as jnp
from jax import lax
from jax.sharding import PartitionSpec as P

HEADS = 16


norm_eps = 1e-06


def layer_norm(values):
    mean_val = jnp.mean(values, axis=-1, keepdims=True)
    centred = values - mean_val
    variance = jnp.mean(centred * centred, axis=-1, keepdims=True)
    return centred * lax.rsqrt(variance + norm_eps)


def modulate(values, shift_term, scale_term):
    return layer_norm(values) * (1.0 + scale_term) + shift_term


def rotate(values, cosine_tab, sine_tab):
    half_dim = values.shape[-1] // 2
    lower_half = values[..., :half_dim]
    upper_half = values[..., half_dim:]
    return jnp.concatenate(
        [
            lower_half * cosine_tab - upper_half * sine_tab,
            upper_half * cosine_tab + lower_half * sine_tab,
        ],
        axis=-1,
    )


def angles(positions, head_dim):
    half_dim = head_dim // 2
    inv_rate = jnp.exp(
        jnp.arange(half_dim, dtype=jnp.float32) * (-2.0 * math.log(10000.0) / head_dim)
    )
    phases = positions.astype(jnp.float32)[:, None] * inv_rate[None, :]
    return (jnp.cos(phases)[:, None, :], jnp.sin(phases)[:, None, :])


def across_rows(left_side, right_side):
    return lax.dot_general(
        left_side, right_side, (((0,), (0,)), ((), ())), preferred_element_type=jnp.float32
    )


def against(left_side, right_side):
    return lax.dot_general(
        left_side, right_side, (((1,), (1,)), ((), ())), preferred_element_type=jnp.float32
    )


def forward_dot(left_side, right_side):
    return jnp.dot(left_side, right_side, preferred_element_type=jnp.float32)


def column_sums(values):
    return jnp.sum(values.astype(jnp.float32), axis=0)


def seq_gather(value):
    return lax.all_gather(value, "seq", axis=0, tiled=True)


def dp_gather(value):
    return lax.all_gather(value, "dp", axis=0, tiled=True)


def seq_reduce(value):
    return lax.psum_scatter(
        value.astype(jnp.bfloat16), "seq", scatter_dimension=0, tiled=True
    ).astype(jnp.float32)


def dp_reduce(value):
    return lax.psum_scatter(value.astype(jnp.bfloat16), "dp", scatter_dimension=0, tiled=True)


def clip_layout(lengths, length):
    clips = lengths.shape[0]
    earlier = jnp.arange(clips)[None, :] <= jnp.arange(clips)[:, None]
    clip_end = jnp.sum(jnp.where(earlier, lengths[None, :], 0), axis=1)
    clip_start = clip_end - lengths
    item_frames = jnp.arange(length, dtype=jnp.int32)
    inside = (item_frames[:, None] >= clip_start[None, :]) & (
        item_frames[:, None] < clip_end[None, :]
    )
    clip_ids = jnp.sum(
        jnp.where(inside, jnp.arange(clips, dtype=jnp.int32)[None, :], 0), axis=1
    )
    positions = item_frames - jnp.sum(jnp.where(inside, clip_start[None, :], 0), axis=1)
    return (clip_ids, positions)


def per_device(
    frames,
    time_embed,
    clip_len,
    w_qkv,
    b_qkv,
    w_out,
    b_out,
    w_up,
    b_up,
    w_down,
    b_down,
    w_mod,
    b_mod,
    cotangent,
):
    seq_count = lax.axis_size("seq")
    seq_rank = lax.axis_index("seq")
    dp_count = lax.axis_size("dp")
    dp_rank = lax.axis_index("dp")
    frame_rows = frames.shape[0]
    model_width = frames.shape[1]
    length = frame_rows * seq_count
    heads_here = HEADS // seq_count
    head_dim = model_width // HEADS
    local_width = heads_here * head_dim
    factor = head_dim ** (-0.5)
    block_rows = min(512, length)
    block_count = length // block_rows
    own_rows = w_qkv.shape[0]
    ff_width = w_up.shape[1]
    units_each = w_down.shape[0] // seq_count
    units_here = ff_width // seq_count

    def own_part(value, axis):
        return lax.dynamic_index_in_dim(value, seq_rank, axis, keepdims=False)

    wq_part = own_part(w_qkv.reshape(own_rows, 3, seq_count, local_width), 2).reshape(
        own_rows, 3 * local_width
    )
    wu_part = own_part(w_up.reshape(own_rows, dp_count, seq_count, units_each), 2).reshape(
        own_rows, units_here
    )
    wd_part = own_part(w_down.reshape(seq_count, units_each, model_width), 0)
    wq_here = dp_gather(wq_part)
    wo_full = dp_gather(w_out)
    wu_here = dp_gather(wu_part)
    wd_here = dp_gather(wd_part)
    sizes = [b_qkv.shape[0], b_out.shape[0], b_up.shape[0], b_down.shape[0]]
    biases = lax.all_gather(jnp.concatenate([b_qkv, b_out, b_up, b_down]), "dp", axis=0)
    cuts = [sizes[0], sizes[0] + sizes[1], sizes[0] + sizes[1] + sizes[2]]
    bq_all, bo_all, bu_all, bd_all = (
        b.astype(jnp.float32) for b in jnp.split(biases, cuts, axis=1)
    )
    bq_here = own_part(bq_all.reshape(3, seq_count, local_width), 1).reshape(3 * local_width)
    bo_full = bo_all.reshape(model_width)
    bu_here = own_part(bu_all.reshape(dp_count, seq_count, units_each), 1).reshape(units_here)
    bd_full = bd_all.reshape(model_width)

    clip_ids, positions = clip_layout(clip_len[0], length)
    cosine_tab, sine_tab = angles(positions, head_dim)

    time_act = jax.nn.silu(time_embed).astype(jnp.bfloat16)
    time_all = dp_gather(time_act)
    time_cols = lax.dynamic_slice_in_dim(time_all, dp_rank * own_rows, own_rows, 1)
    bias_cols = lax.dynamic_update_slice(
        jnp.zeros((6 * model_width,), jnp.float32),
        b_mod.astype(jnp.float32),
        (dp_rank * b_mod.shape[0],),
    )
    modulation = lax.psum_scatter(
        forward_dot(time_cols, w_mod) + bias_cols, "dp", scatter_dimension=0, tiled=True
    )
    shift_a, scale_a, gate_a, shift_f, scale_f, gate_f = jnp.split(modulation, 6, axis=1)

    d_ffn = (gate_f * cotangent).astype(jnp.bfloat16)
    d_ffn_item = seq_gather(d_ffn)
    x_a = seq_gather(modulate(frames, shift_a, scale_a).astype(jnp.bfloat16))
    projected = forward_dot(x_a, wq_here) + bq_here
    pieces = projected.reshape(length, 3, heads_here, head_dim)
    query_heads = rotate(pieces[:, 0], cosine_tab, sine_tab).astype(jnp.bfloat16)
    keys_heads = rotate(pieces[:, 1], cosine_tab, sine_tab).astype(jnp.bfloat16)
    values_heads = pieces[:, 2].astype(jnp.bfloat16)

    def block_scores(block_index):
        first_row = block_index * block_rows
        query_blk = lax.dynamic_slice_in_dim(query_heads, first_row, block_rows, 0)
        clip_blk = lax.dynamic_slice_in_dim(clip_ids, first_row, block_rows, 0)
        same_clip = (clip_blk[:, None] == clip_ids[None, :])[None]
        raw_scores = (
            jnp.einsum("qhe,khe->hqk", query_blk, keys_heads, preferred_element_type=jnp.float32)
            * factor
        )
        return (query_blk, same_clip, jnp.where(same_clip, raw_scores, -1e30))

    def attend(block_index):
        query_blk, same_clip, masked = block_scores(block_index)
        row_max = jnp.max(masked, axis=-1, keepdims=True)
        exp_scores = jnp.exp(masked - row_max)
        row_sum = jnp.sum(exp_scores, axis=-1, keepdims=True)
        attn_prob = (exp_scores / row_sum).astype(jnp.bfloat16)
        mixed_rows = jnp.einsum(
            "hqk,khe->qhe", attn_prob, values_heads, preferred_element_type=jnp.float32
        )
        return (mixed_rows.astype(jnp.bfloat16), row_max + jnp.log(row_sum))

    attn_blocks, log_totals = lax.map(attend, jnp.arange(block_count))
    attn_heads = attn_blocks.reshape(length, local_width)
    attn_out = lax.all_to_all(attn_heads, "seq", split_axis=0, concat_axis=1, tiled=True)
    attn_branch = forward_dot(attn_out, wo_full) + bo_full
    x_mid = frames + gate_a * attn_branch
    x_f = seq_gather(modulate(x_mid, shift_f, scale_f).astype(jnp.bfloat16))
    hidden = forward_dot(x_f, wu_here) + bu_here
    gelu_act, gelu_pull = jax.vjp(lambda inner: jax.nn.gelu(inner, approximate=True), hidden)
    gelu_act = gelu_act.astype(jnp.bfloat16)
    ffn_branch = seq_reduce(forward_dot(gelu_act, wd_here)) + bd_full
    block_out = x_mid + gate_f * ffn_branch
    d_gate_f = jnp.sum(cotangent * ffn_branch, axis=0, keepdims=True)
    d_gelu = against(d_ffn_item, wd_here)
    d_hidden = gelu_pull(d_gelu)[0].astype(jnp.bfloat16)
    d_xf = seq_reduce(against(d_hidden, wu_here))
    g_wd = across_rows(gelu_act, d_ffn_item)
    g_bd = column_sums(d_ffn_item)
    g_wu = across_rows(x_f, d_hidden)
    g_bu = column_sums(d_hidden)
    mid_pull = jax.vjp(modulate, x_mid, shift_f, scale_f)[1]
    d_mid_part, d_shift_f, d_scale_f = mid_pull(d_xf)
    d_mid = cotangent + d_mid_part
    d_attn = (gate_a * d_mid).astype(jnp.bfloat16)
    d_gate_a = jnp.sum(d_mid * attn_branch, axis=0, keepdims=True)
    g_wo_run = across_rows(attn_out, d_attn)
    g_wo = lax.psum_scatter(
        g_wo_run.astype(jnp.bfloat16), "seq", scatter_dimension=1, tiled=True
    )
    g_bo = column_sums(d_attn)
    d_out = against(d_attn, wo_full).astype(jnp.bfloat16)
    grad_heads = lax.all_to_all(d_out, "seq", split_axis=1, concat_axis=0, tiled=True).reshape(
        length, heads_here, head_dim
    )

    def attend_back(running, inputs):
        grad_keys, grad_values = running
        block_index, log_blk = inputs
        query_blk, same_clip, masked = block_scores(block_index)
        attn_prob = jnp.exp(masked - log_blk)
        prob_low = attn_prob.astype(jnp.bfloat16)
        grad_blk = lax.dynamic_slice_in_dim(grad_heads, block_index * block_rows, block_rows, 0)
        d_prob = jnp.einsum(
            "qhe,khe->hqk", grad_blk, values_heads, preferred_element_type=jnp.float32
        )
        d_scores = attn_prob * (d_prob - jnp.sum(d_prob * attn_prob, axis=-1, keepdims=True))
        d_scores = jnp.where(same_clip, d_scores, 0.0).astype(jnp.bfloat16)
        d_query = (
            jnp.einsum("hqk,khe->qhe", d_scores, keys_heads, preferred_element_type=jnp.float32)
            * factor
        )
        grad_keys = (
            grad_keys
            + jnp.einsum("hqk,qhe->khe", d_scores, query_blk, preferred_element_type=jnp.float32)
            * factor
        )
        grad_values = grad_values + jnp.einsum(
            "hqk,qhe->khe", prob_low, grad_blk, preferred_element_type=jnp.float32
        )
        return ((grad_keys, grad_values), d_query.astype(jnp.bfloat16))

    zero_heads = jnp.zeros((length, heads_here, head_dim), jnp.float32)
    (grad_keys, grad_values), query_grads = lax.scan(
        attend_back, (zero_heads, zero_heads), (jnp.arange(block_count), log_totals)
    )
    def turned_back(value):
        return rotate(value.astype(jnp.bfloat16).astype(jnp.float32), cosine_tab, -sine_tab)

    d_projected = jnp.concatenate(
        [
            turned_back(query_grads.reshape(length, heads_here, head_dim)).reshape(length, -1),
            turned_back(grad_keys).reshape(length, -1),
            grad_values.reshape(length, -1),
        ],
        axis=1,
    ).astype(jnp.bfloat16)
    d_xa = seq_reduce(against(d_projected, wq_here))
    g_wq = across_rows(x_a, d_projected)
    g_bq = column_sums(d_projected)
    input_pull = jax.vjp(modulate, frames, shift_a, scale_a)[1]
    d_input_part, d_shift_a, d_scale_a = input_pull(d_xa)
    grad_input = d_mid + d_input_part
    mod_part = jnp.concatenate(
        [d_shift_a, d_scale_a, d_gate_a, d_shift_f, d_scale_f, d_gate_f, g_bo[None]], axis=1
    )
    mod_sum = lax.psum(mod_part, "seq")
    d_mod = dp_gather(mod_sum[:, : 6 * model_width].astype(jnp.bfloat16))
    g_wm = across_rows(time_cols, d_mod)
    g_bm = column_sums(
        lax.dynamic_slice_in_dim(d_mod, dp_rank * b_mod.shape[0], b_mod.shape[0], 1)
    )
    d_time_act = lax.all_to_all(
        against(d_mod, w_mod), "dp", split_axis=0, concat_axis=1, tiled=True
    )
    grad_time = jax.vjp(jax.nn.silu, time_embed)[1](d_time_act)[0]

    def spread(value):
        return lax.all_gather(dp_reduce(value), "seq", axis=0).astype(jnp.float32)

    s_wq = (
        spread(g_wq)
        .reshape(seq_count, own_rows, 3, local_width)
        .transpose(1, 2, 0, 3)
        .reshape(own_rows, 3 * model_width)
    )
    s_wo = spread(g_wo).transpose(1, 0, 2).reshape(own_rows, model_width)
    s_wu = (
        spread(g_wu)
        .reshape(seq_count, own_rows, dp_count, units_each)
        .transpose(1, 2, 0, 3)
        .reshape(own_rows, ff_width)
    )
    s_wd = spread(g_wd).reshape(seq_count * units_each, model_width)
    bq_item = lax.all_gather(g_bq, "seq", axis=0).reshape(seq_count, 3, local_width)
    bu_item = lax.all_gather(g_bu, "seq", axis=0).reshape(seq_count, dp_count, units_each)
    bias_terms = jnp.concatenate(
        [
            bq_item.transpose(1, 0, 2).reshape(dp_count, sizes[0]),
            mod_sum[:, 6 * model_width :].reshape(dp_count, sizes[1]),
            bu_item.transpose(1, 0, 2).reshape(dp_count, sizes[2]),
            g_bd.reshape(dp_count, sizes[3]),
        ],
        axis=1,
    )
    bias_sums = lax.psum_scatter(bias_terms, "dp", scatter_dimension=0, tiled=True)[0]
    s_bq, s_bo, s_bu, s_bd = jnp.split(bias_sums, cuts)
    return (
        block_out,
        grad_input,
        grad_time,
        s_wq,
        s_bq,
        s_wo,
        s_bo,
        s_wu,
        s_bu,
        s_wd,
        s_bd,
        g_wm,
        g_bm,
    )


def solution(mesh):
    placed = (
        P(("dp", "seq"), None),
        P("dp", None),
        P("dp", None),
        P("dp", None),
        P("dp"),
        P("dp", None),
        P("dp"),
        P("dp", None),
        P("dp"),
        P("dp", None),
        P("dp"),
        P("dp", None),
        P("dp"),
        P(("dp", "seq"), None),
    )
    return jax.shard_map(
        per_device,
        mesh=mesh,
        in_specs=placed,
        out_specs=(
            P(("dp", "seq"), None),
            P(("dp", "seq"), None),
            P("dp", None),
            P("dp", None),
            P("dp"),
            P("dp", None),
            P("dp"),
            P("dp", None),
            P("dp"),
            P("dp", None),
            P("dp"),
            P("dp", None),
            P("dp"),
        ),
        check_vma=False,
    )
```

```python
import functools
import math

import jax
import jax.numpy as jnp
from jax import lax
from jax.experimental import pallas as pl
from jax.experimental.pallas import tpu as pltpu
from jax.sharding import PartitionSpec as P

HEADS = 16
MESH = pl.DeviceIdType.MESH
f32 = jnp.float32
bf16 = jnp.bfloat16
norm_eps = 1e-06


def nn(left_side, right_side):
    return lax.dot_general(left_side, right_side, (((1,), (0,)), ((), ())), preferred_element_type=f32)


def nt(left_side, right_side):
    return lax.dot_general(left_side, right_side, (((1,), (1,)), ((), ())), preferred_element_type=f32)


def merged(ref):
    shape = ref.shape
    return ref[...].reshape(shape[0] * shape[1], shape[2])


def swap_halves(values, lane):
    up = pltpu.roll(values, 96, 1)
    down = pltpu.roll(values, 32, 1)
    return jnp.where(lane % 64 < 32, up, down)


def gelu_both(h):
    c = math.sqrt(2.0 / math.pi)
    h2 = h * h
    t = jnp.tanh(c * h * (1.0 + 0.044715 * h2))
    half = 0.5 * (1.0 + t)
    return h * half, half + 0.5 * h * (1.0 - t * t) * (c * (1.0 + 3.0 * 0.044715 * h2))


def normed(values):
    mean_val = jnp.mean(values, axis=-1, keepdims=True)
    centred = values - mean_val
    rstd = lax.rsqrt(jnp.mean(centred * centred, axis=-1, keepdims=True) + norm_eps)
    return centred * rstd, rstd


def norm_back(e, n, rstd):
    return (e - jnp.mean(e, axis=-1, keepdims=True) - n * jnp.mean(e * n, axis=-1, keepdims=True)) * rstd


class Links:
    def __init__(self, n, send, recv):
        self.n = n
        self.d = lax.axis_index("dp")
        self.s = lax.axis_index("seq")
        d, s = self.d, self.s
        self.px = d + 1 - 2 * (d % 2)
        self.s1 = s + 1 - 2 * (s % 2)
        self.s2 = (s + 2) % 4
        self.s3 = 3 - s
        self.send, self.recv = send, recv
        self.n_send = self.n_recv = 0

    def sems(self, sends, recvs):
        base = (self.n_send, self.n_recv)
        self.n_send += sends
        self.n_recv += recvs
        return base

    def block(self, i):
        s = self.s
        return (s % 2 + i % 2) % 2 + 2 * ((s // 2 + i // 2) % 2)

    def copy(self, src, dst, si, ri, dev):
        return pltpu.make_async_remote_copy(
            src_ref=src, dst_ref=dst, send_sem=self.send.at[si], recv_sem=self.recv.at[ri],
            device_id=dev, device_id_type=MESH,
        )

    def barrier(self):
        b = pltpu.get_barrier_semaphore()
        for k in range(1, self.n):
            pl.semaphore_signal(b, inc=1, device_id=((self.d + k) % self.n, self.s), device_id_type=MESH)
        for t in (self.s1, self.s2, self.s3):
            pl.semaphore_signal(b, inc=1, device_id=(self.d, t), device_id_type=MESH)
        pl.semaphore_wait(b, self.n + 2)


class ToAll:
    def __init__(self, links, src, buf):
        self.l, self.src, self.buf = links, src, buf
        self.si, self.ri = links.sems(links.n, links.n)

    def _to(self, k):
        l = self.l
        peer = (l.d + k) % l.n
        return l.copy(self.src(peer), self.buf.at[l.d], self.si + k, self.ri + l.d, (peer, l.s))

    def start(self):
        for k in range(1, self.l.n):
            self._to(k).start()

    def wait_recv(self):
        l = self.l
        for k in range(1, l.n):
            peer = (l.d + k) % l.n
            l.copy(self.buf.at[peer], self.buf.at[peer], self.si + k, self.ri + peer, (peer, l.s)).wait_recv()

    def wait_send(self):
        for k in range(1, self.l.n):
            self._to(k).wait_send()


class SeqAll:
    def __init__(self, links, buf):
        self.l, self.buf = links, buf
        self.si, self.ri = links.sems(4, 4)

    def _to(self, k):
        l = self.l
        t = l.block(k)
        return l.copy(self.buf.at[l.s], self.buf.at[l.s], self.si + k, self.ri + l.s, (l.d, t))

    def start(self):
        for k in (2, 3, 1):
            self._to(k).start()

    def wait_recv(self):
        l = self.l
        for k in (1, 2, 3):
            t = l.block(k)
            l.copy(self.buf.at[t], self.buf.at[t], self.si + k, self.ri + t, (l.d, t)).wait_recv()

    def wait_send(self):
        for k in (1, 2, 3):
            self._to(k).wait_send()


class DpGather:
    def __init__(self, links, buf):
        self.l, self.buf = links, buf
        self.si, self.ri = links.sems(links.n, links.n)
        self.half = links.n // 2

    def _z(self, k):
        l = self.l
        return l.copy(self.buf.at[l.d], self.buf.at[l.d], self.si + k, self.ri + l.d, ((l.d + 2 * k) % l.n, l.s))

    def _x(self, k):
        l = self.l
        r = (l.d + 2 * k) % l.n
        return l.copy(self.buf.at[r], self.buf.at[r], self.si + self.half + k, self.ri + r, (l.px, l.s))

    def start(self):
        for k in range(1, self.half):
            self._z(k).start()
        self._x(0).start()

    def hand_on(self):
        l = self.l
        for k in range(1, self.half):
            r = (l.d + 2 * k) % l.n
            l.copy(self.buf.at[r], self.buf.at[r], self.si, self.ri + r, (r, l.s)).wait_recv()
            self._x(k).start()

    def wait_rest(self):
        l = self.l
        for k in range(self.half):
            r = (l.px + 2 * k) % l.n
            l.copy(self.buf.at[r], self.buf.at[r], self.si, self.ri + r, (l.px, l.s)).wait_recv()

    def wait_send(self):
        for k in range(1, self.half):
            self._z(k).wait_send()
        for k in range(self.half):
            self._x(k).wait_send()


class SeqGather:
    def __init__(self, links, buf):
        self.l, self.buf = links, buf
        self.si, self.ri = links.sems(3, 4)

    def _c(self, slot, k, t):
        l = self.l
        return l.copy(self.buf.at[slot], self.buf.at[slot], self.si + k, self.ri + slot, (l.d, t))

    def start(self):
        l = self.l
        self._c(l.s, 0, l.s2).start()
        self._c(l.s, 1, l.s1).start()

    def hand_on(self):
        l = self.l
        self.wait(l.s2)
        self._c(l.s2, 2, l.s1).start()

    def wait(self, slot):
        l = self.l
        l.copy(self.buf.at[slot], self.buf.at[slot], self.si, self.ri + slot, (l.d, l.s1)).wait_recv()

    def wait_send(self):
        l = self.l
        self._c(l.s, 0, l.s2).wait_send()
        self._c(l.s, 1, l.s1).wait_send()
        self._c(l.s2, 2, l.s1).wait_send()


class SeqSwap:
    def __init__(self, links, out, into):
        self.l, self.out, self.into = links, out, into
        self.si, self.ri = links.sems(4, 4)

    def copy_to(self, i):
        l = self.l
        t = l.block(i)
        return l.copy(self.out.at[t], self.into.at[l.s], self.si + i, self.ri + l.s, (l.d, t))

    def wait_recv(self):
        l = self.l
        for i in (1, 2, 3):
            t = l.block(i)
            l.copy(self.into.at[t], self.into.at[t], self.si + i, self.ri + t, (l.d, t)).wait_recv()

    def wait_send(self):
        for i in (1, 2, 3):
            self.copy_to(i).wait_send()


class SeqSum:
    def __init__(self, links, held):
        self.l, self.held = links, held
        self.si, self.ri = links.sems(3, 3)

    def _c(self, k, t):
        l = self.l
        return l.copy(self.held.at[k], self.held.at[3 + k], self.si + k, self.ri + k, (l.d, t))

    def far(self, term):
        l, held = self.l, self.held
        held[0] = term(l.s3).astype(bf16)
        self._c(0, l.s1).start()
        mine = term(l.s2)
        self._c(0, l.s1).wait_recv()
        held[1] = (mine + held[3].astype(f32)).astype(bf16)
        self._c(1, l.s2).start()

    def near(self, term):
        l = self.l
        self.held[2] = term(l.s1).astype(bf16)
        self._c(2, l.s1).start()

    def total(self, mine):
        l, held = self.l, self.held
        self._c(2, l.s1).wait_recv()
        self._c(1, l.s2).wait_recv()
        return mine + held[5].astype(f32) + held[4].astype(f32)

    def wait_send(self):
        l = self.l
        self._c(0, l.s1).wait_send()
        self._c(1, l.s2).wait_send()
        self._c(2, l.s1).wait_send()


def kernel_a(
    n,
    frames, cot, tcols, bm, bias, wu_own, cos, sin, idr, idc, wm_hbm, wq_hbm, wo_hbm, wd_hbm,
    xa, q, k, v, kt, vt, lse, ao, gh, dffn, gelu, xf, dhid, wq, wd, dmid, xmid, dattn, mod, fsum, bd_full,
    wm, wu, wo, tbuf, psend, pbuf, bbuf, n_in, attn_branch, n_mid, ao_out, do_out, held,
    send, recv, local,
):
    l = Links(n, send, recv)
    d, s = l.d, l.s
    rows, width = frames.shape
    quarter = width // 4
    own_rows = tcols.shape[2]
    mq = bm.shape[1]
    units = wd.shape[1]
    ff_q = wu.shape[2]
    lane = lax.broadcasted_iota(jnp.int32, (rows, 128), 1)
    take = [
        pltpu.make_async_copy(wm_hbm.at[:, pl.ds(pl.multiple_of(s * mq, 128), mq)], wm, local.at[0]),
        pltpu.make_async_copy(wd_hbm.at[pl.ds(pl.multiple_of(s * units, 8), units), :], wd.at[d], local.at[1]),
        pltpu.make_async_copy(wo_hbm.at[:, pl.ds(pl.multiple_of(s * quarter, 128), quarter)], wo.at[s, d], local.at[2]),
    ] + [
        pltpu.make_async_copy(
            wq_hbm.at[:, pl.ds(pl.multiple_of(j * width + s * quarter, 128), quarter)],
            wq.at[d, :, pl.ds(j * quarter, quarter)], local.at[3 + j],
        )
        for j in range(3)
    ]
    for c in take:
        c.start()
    times = ToAll(l, lambda peer: tcols.at[peer], tbuf)
    parts = ToAll(l, lambda peer: psend.at[peer], pbuf)
    biases = ToAll(l, lambda peer: bias.at[0], bbuf)
    mods = SeqAll(l, mod)
    g_wq, g_wu, g_wd = DpGather(l, wq), DpGather(l, wu), DpGather(l, wd)
    g_wo = DpGather(l, wo.at[s])
    s_xa, s_df, s_xf, s_wo = SeqGather(l, xa), SeqGather(l, dffn), SeqGather(l, xf), SeqGather(l, wo)
    w_ao, w_do = SeqSwap(l, ao_out, ao), SeqSwap(l, do_out, gh)
    sums = SeqSum(l, held)
    l.barrier()
    times.start()
    for c in take[3:]:
        c.wait()
    g_wq.start()
    biases.start()
    tbuf[d] = tcols[d]
    wu[d] = wu_own[...]
    for c in take[:3]:
        c.wait()
    n_in[...] = normed(frames[...])[0]
    times.wait_recv()
    lhs = jnp.concatenate([tbuf[i] for i in range(n)], axis=0).astype(bf16)
    part = nn(lhs, wm[...]) + bm[...]
    for i in range(n):
        psend[i] = part[i : i + 1]
    parts.start()
    total = psend[d]
    parts.wait_recv()
    for j in range(1, n):
        total = total + pbuf[(d + j) % n]
    mod[s] = total
    mods.start()
    mods.wait_recv()
    flat = jnp.concatenate([mod[i] for i in range(4)], axis=1)
    shift_a, scale_a, gate_a, shift_f, scale_f, gate_f = (
        flat[:, i * width : (i + 1) * width] for i in range(6)
    )
    xa[s] = (n_in[...] * (1.0 + scale_a) + shift_a).astype(bf16)
    s_xa.start()
    dffn[s] = (gate_f * cot[...]).astype(bf16)
    g_wq.hand_on()
    g_wd.start()
    g_wu.start()
    g_wo.start()
    g_wq.wait_rest()
    biases.wait_recv()
    own_bias = bias[0]
    for j in range(1, n):
        own_bias = own_bias + bbuf[(d + j) % n]
    qw = 3 * quarter
    bq = own_bias[:, :qw]
    bo = own_bias[:, qw : qw + width]
    bu = own_bias[:, qw + width : qw + width + ff_q]
    bd_full[...] = own_bias[:, qw + width + ff_q :]

    def project(i, carry):
        @pl.when(i == 1)
        def _():
            s_xa.wait(l.s1)

        @pl.when(i == 2)
        def _():
            s_xa.hand_on()
            s_df.start()

        @pl.when(i == 3)
        def _():
            s_xa.wait(l.s3)

        b = l.block(i)
        at = pl.ds(pl.multiple_of(b * rows, rows), rows)
        pr = nn(xa[b], merged(wq)) + bq
        cb, sb = cos[at, :], sin[at, :]
        for p in range(quarter // 128):
            c0 = 128 * p
            qp = pr[:, c0 : c0 + 128]
            kp = pr[:, quarter + c0 : quarter + c0 + 128]
            vp = pr[:, 2 * quarter + c0 : 2 * quarter + c0 + 128].astype(bf16)
            qp = (qp * cb + swap_halves(qp, lane) * sb).astype(bf16)
            kp = (kp * cb + swap_halves(kp, lane) * sb).astype(bf16)
            q[at, c0 : c0 + 128] = qp * jnp.bfloat16(0.125)
            k[at, c0 : c0 + 128] = kp
            v[at, c0 : c0 + 128] = vp
            kt[p, :, at] = jnp.transpose(kp.astype(f32)).astype(bf16)
            vt[p, :, at] = jnp.transpose(vp.astype(f32)).astype(bf16)
        return carry

    lax.fori_loop(0, 4, project, 0)
    g_wd.hand_on()
    g_wu.hand_on()

    def attend(j, carry):
        i = (j + 2) % 4
        b = l.block(i)
        at = pl.ds(pl.multiple_of(b * rows, rows), rows)
        same = idc[...] == idr[:, at]
        for p in range(quarter // 128):
            qp, kp = q[at, 128 * p : 128 * p + 128], k[:, 128 * p : 128 * p + 128]
            outs = []
            for h in range(2):
                qm = jnp.where((lane < 64) == (h == 0), qp, jnp.zeros_like(qp))
                sc = jnp.where(same, nt(kp, qm), -1e30)
                top = jnp.max(sc, axis=0, keepdims=True)
                ex = jnp.exp(sc - top)
                su = jnp.sum(ex, axis=0, keepdims=True)
                lse[2 * p + h, :, at] = top + jnp.log(su)
                pt = (ex * (1.0 / su)).astype(bf16)
                outs.append(nn(vt[p, 64 * h : 64 * h + 64, :], pt))
            ao_out[b, :, 128 * p : 128 * p + 128] = jnp.transpose(jnp.concatenate(outs, axis=0)).astype(bf16)

        @pl.when(j != 2)
        def _():
            w_ao.copy_to(i).start()

        @pl.when(j == 2)
        def _():
            ao[s] = ao_out[s]

        @pl.when(j == 0)
        def _():
            g_wo.hand_on()
            s_df.hand_on()

        @pl.when(j == 1)
        def _():
            g_wo.wait_rest()
            s_wo.start()

        @pl.when(j == 3)
        def _():
            s_wo.hand_on()

        return carry

    lax.fori_loop(0, 4, attend, 0)
    s_wo.wait(l.s1)
    s_wo.wait(l.s3)
    w_ao.wait_recv()
    left = jnp.concatenate([ao[i] for i in range(4)], axis=1)
    for c in range(4):
        cs = slice(c * quarter, (c + 1) * quarter)
        attn_branch[:, cs] = nn(left, merged(wo.at[c])) + bo[:, cs]
    xm = frames[...] + gate_a * attn_branch[...]
    xmid[...] = xm
    nm, rstd = normed(xm)
    n_mid[...] = nm
    xf[s] = (nm * (1.0 + scale_f) + shift_f).astype(bf16)
    s_xf.start()
    s_df.wait(l.s1)
    s_df.wait(l.s3)
    g_wd.wait_rest()
    g_wu.wait_rest()

    def term(b):
        at = pl.ds(pl.multiple_of(b * rows, rows), rows)
        return nt(dhid[at, :], merged(wu))

    def feed(i, carry):
        @pl.when(i == 1)
        def _():
            s_xf.wait(l.s1)

        @pl.when(i == 2)
        def _():
            sums.near(term)
            s_xf.hand_on()

        @pl.when(i == 3)
        def _():
            s_xf.wait(l.s3)

        b = l.block(i)
        at = pl.ds(pl.multiple_of(b * rows, rows), rows)
        act, slope = gelu_both(nn(xf[b], merged(wu)) + bu)
        gelu[at, :] = act.astype(bf16)
        dhid[at, :] = (nt(dffn[b], merged(wd)) * slope).astype(bf16)
        return carry

    lax.fori_loop(0, 4, feed, 0)
    sums.far(term)
    g = sums.total(term(s))
    nm = n_mid[...]
    fsum[0:1, :] = jnp.sum(g, axis=0, keepdims=True)
    fsum[1:2, :] = jnp.sum(g * nm, axis=0, keepdims=True)
    dm = cot[...] + norm_back(g * (1.0 + scale_f), nm, rstd)
    dmid[...] = dm
    da = (gate_a * dm).astype(bf16)
    dattn[...] = da
    fsum[2:3, :] = jnp.sum(dm * attn_branch[...], axis=0, keepdims=True)
    fsum[3:4, :] = jnp.sum(da.astype(f32), axis=0, keepdims=True)
    per = n // 4

    def give(j, carry):
        i = (j + 2) % 4
        t = l.block(i)
        out = None
        for c in range(4):
            wt = wo[c, pl.ds(t * per, per)].reshape(quarter, quarter)
            o = nt(dattn[:, c * quarter : (c + 1) * quarter], wt)
            out = o if out is None else out + o
        do_out[t] = out.astype(bf16)

        @pl.when(j != 2)
        def _():
            w_do.copy_to(i).start()

        @pl.when(j == 2)
        def _():
            gh[s] = do_out[s]

        return carry

    lax.fori_loop(0, 4, give, 0)
    w_do.wait_recv()
    for c in (times, parts, biases, mods, g_wq, g_wu, g_wd, g_wo, s_xa, s_df, s_xf, s_wo, w_ao, w_do, sums):
        c.wait_send()


def run_a(n, frames, cot, tcols, bm, bias, wu_own, cos, sin, idr, idc, w_mod, w_qkv, w_out, w_down):
    rows, width = frames.shape
    item = 4 * rows
    quarter = width // 4
    ff = w_down.shape[0] * n
    ff_q = ff // 4
    own_rows = width // n
    units = ff_q // n
    heads = quarter // 64
    pairs = quarter // 128
    S = jax.ShapeDtypeStruct
    outs = [
        S((4, rows, width), bf16), S((item, quarter), bf16), S((item, quarter), bf16), S((item, quarter), bf16),
        S((pairs, 128, item), bf16), S((pairs, 128, item), bf16), S((heads, 1, item), f32),
        S((4, rows, quarter), bf16), S((4, rows, quarter), bf16), S((4, rows, width), bf16), S((item, ff_q), bf16),
        S((4, rows, width), bf16), S((item, ff_q), bf16), S((n, own_rows, 3 * quarter), bf16), S((n, units, width), bf16),
        S((rows, width), f32), S((rows, width), f32), S((rows, width), bf16), S((4, 1, 6 * quarter), f32),
        S((8, width), f32), S((1, width), f32),
    ]
    V = pltpu.VMEM
    scratch = [
        V((own_rows, 6 * quarter), bf16), V((n, own_rows, ff_q), bf16), V((4, n, own_rows, quarter), bf16),
        V((n, 1, own_rows), f32), V((n, 1, 6 * quarter), f32), V((n, 1, 6 * quarter), f32), V((n, 1, bias.shape[2]), f32),
        V((rows, width), f32), V((rows, width), f32), V((rows, width), f32), V((4, rows, quarter), bf16),
        V((4, rows, quarter), bf16), V((6, rows, width), bf16),
        pltpu.SemaphoreType.DMA((7 * n + 40,)), pltpu.SemaphoreType.DMA((7 * n + 40,)), pltpu.SemaphoreType.DMA((6,)),
    ]
    vm = pl.BlockSpec(memory_space=pltpu.VMEM)
    hb = pl.BlockSpec(memory_space=pl.ANY)
    return pl.pallas_call(
        functools.partial(kernel_a, n),
        out_shape=outs,
        in_specs=[vm] * 10 + [hb] * 4,
        out_specs=[vm] * len(outs),
        scratch_shapes=scratch,
        compiler_params=pltpu.CompilerParams(collective_id=0, has_side_effects=True, vmem_limit_bytes=60 << 20),
    )(frames, cot, tcols, bm, bias, wu_own, cos, sin, idr, idc, w_mod, w_qkv, w_out, w_down)


def clip_layout(lengths, length):
    clips = lengths.shape[0]
    earlier = jnp.arange(clips)[None, :] <= jnp.arange(clips)[:, None]
    clip_end = jnp.sum(jnp.where(earlier, lengths[None, :], 0), axis=1)
    clip_start = clip_end - lengths
    item_frames = jnp.arange(length, dtype=jnp.int32)
    inside = (item_frames[:, None] >= clip_start[None, :]) & (
        item_frames[:, None] < clip_end[None, :]
    )
    clip_ids = jnp.sum(
        jnp.where(inside, jnp.arange(clips, dtype=jnp.int32)[None, :], 0), axis=1
    )
    positions = item_frames - jnp.sum(jnp.where(inside, clip_start[None, :], 0), axis=1)
    return (clip_ids, positions)


def tables(positions):
    lanes = jnp.arange(128)
    inv_rate = jnp.exp((lanes % 32).astype(f32) * (-2.0 * math.log(10000.0) / 64))
    phases = positions.astype(f32)[:, None] * inv_rate[None, :]
    sign = jnp.where(lanes % 64 < 32, -1.0, 1.0)
    return jnp.cos(phases), jnp.sin(phases) * sign[None, :]


def prepare(seq_rank, dp_rank, n, frames, time_embed, clip_len, b_qkv, b_out, w_up, b_up, b_down, b_mod):
    rows, width = frames.shape
    quarter = width // 4
    own_rows, ff = w_up.shape
    units = ff // 4 // n
    clip_ids, positions = clip_layout(clip_len[0], 4 * rows)
    cos, sin = tables(positions)
    tcols = jax.nn.silu(time_embed).astype(bf16).astype(f32).reshape(n, 1, own_rows)

    def placed(b):
        return lax.dynamic_update_slice(
            jnp.zeros((b.shape[0] * n,), f32), b.astype(f32), (dp_rank * b.shape[0],)
        )

    def own(value, axis):
        return lax.dynamic_index_in_dim(value, seq_rank, axis, keepdims=False)

    bm = own(placed(b_mod).reshape(4, 6 * quarter), 0)[None]
    bias = jnp.concatenate(
        [
            own(placed(b_qkv).reshape(3, 4, quarter), 1).reshape(-1),
            placed(b_out),
            own(placed(b_up).reshape(n, 4, units), 1).reshape(-1),
            placed(b_down),
        ]
    ).reshape(1, 1, -1)
    wu_own = own(w_up.reshape(own_rows, n, 4, units), 2).reshape(own_rows, ff // 4)
    return tcols, bm, bias, wu_own, cos, sin, clip_ids[None, :], clip_ids[:, None]


def layer_norm(values):
    mean_val = jnp.mean(values, axis=-1, keepdims=True)
    centred = values - mean_val
    variance = jnp.mean(centred * centred, axis=-1, keepdims=True)
    return centred * lax.rsqrt(variance + norm_eps)


def modulate(values, shift_term, scale_term):
    return layer_norm(values) * (1.0 + scale_term) + shift_term


def rotate(values, cosine_tab, sine_tab):
    half_dim = values.shape[-1] // 2
    lower_half = values[..., :half_dim]
    upper_half = values[..., half_dim:]
    return jnp.concatenate(
        [
            lower_half * cosine_tab - upper_half * sine_tab,
            upper_half * cosine_tab + lower_half * sine_tab,
        ],
        axis=-1,
    )


def across_rows(left_side, right_side):
    return lax.dot_general(
        left_side, right_side, (((0,), (0,)), ((), ())), preferred_element_type=jnp.float32
    )


def against(left_side, right_side):
    return lax.dot_general(
        left_side, right_side, (((1,), (1,)), ((), ())), preferred_element_type=jnp.float32
    )


def forward_dot(left_side, right_side):
    return jnp.dot(left_side, right_side, preferred_element_type=jnp.float32)


def column_sums(values):
    return jnp.sum(values.astype(jnp.float32), axis=0)


def seq_gather(value):
    return lax.all_gather(value, "seq", axis=0, tiled=True)


def dp_gather(value):
    return lax.all_gather(value, "dp", axis=0, tiled=True)


def seq_reduce(value):
    return lax.psum_scatter(
        value.astype(jnp.bfloat16), "seq", scatter_dimension=0, tiled=True
    ).astype(jnp.float32)


def dp_reduce(value):
    return lax.psum_scatter(value.astype(jnp.bfloat16), "dp", scatter_dimension=0, tiled=True)


def per_device(
    frames,
    time_embed,
    clip_len,
    w_qkv,
    b_qkv,
    w_out,
    b_out,
    w_up,
    b_up,
    w_down,
    b_down,
    w_mod,
    b_mod,
    cotangent,
):
    seq_count = lax.axis_size("seq")
    seq_rank = lax.axis_index("seq")
    dp_count = lax.axis_size("dp")
    dp_rank = lax.axis_index("dp")
    frame_rows = frames.shape[0]
    model_width = frames.shape[1]
    length = frame_rows * seq_count
    heads_here = HEADS // seq_count
    head_dim = model_width // HEADS
    local_width = heads_here * head_dim
    factor = head_dim ** (-0.5)
    block_rows = min(512, length)
    block_count = length // block_rows
    own_rows = w_qkv.shape[0]
    ff_width = w_up.shape[1]
    units_each = w_down.shape[0] // seq_count
    units_here = ff_width // seq_count

    pre = prepare(
        seq_rank, dp_rank, dp_count, frames, time_embed, clip_len, b_qkv, b_out, w_up, b_up, b_down, b_mod
    )
    outs = run_a(dp_count, frames, cotangent, *pre, w_mod, w_qkv, w_out, w_down)
    x_a, q8, k, v, _, _, lse, attn_out, grad_heads, d_ffn_item, gelu_act, x_f, d_hidden, wq, wd = outs[:15]
    d_mid, x_mid, d_attn, mod, fsum, bd_full = outs[15:]
    tcols, _, _, _, cos, sin, clip_ids = pre[:7]
    clip_ids = clip_ids[0]
    cosine_tab, sine_tab = cos[:, None, :32], -sin[:, None, :32]
    sizes = [b_qkv.shape[0], b_out.shape[0], b_up.shape[0], b_down.shape[0]]
    cuts = [sizes[0], sizes[0] + sizes[1], sizes[0] + sizes[1] + sizes[2]]
    time_all = dp_gather(jax.nn.silu(time_embed).astype(jnp.bfloat16))
    time_cols = lax.dynamic_slice_in_dim(time_all, dp_rank * own_rows, own_rows, 1)
    x_a = x_a.reshape(length, model_width)
    x_f = x_f.reshape(length, model_width)
    d_ffn_item = d_ffn_item.reshape(length, model_width)
    wq_here = wq.reshape(model_width, -1)
    wd_here = wd.reshape(units_here, model_width)
    query_heads = (q8 * jnp.bfloat16(8)).reshape(length, heads_here, head_dim)
    keys_heads = k.reshape(length, heads_here, head_dim)
    values_heads = v.reshape(length, heads_here, head_dim)
    attn_out = attn_out.transpose(1, 0, 2).reshape(frame_rows, model_width)
    grad_heads = grad_heads.reshape(length, heads_here, head_dim)
    log_totals = (
        lse.reshape(heads_here, block_count, block_rows).transpose(1, 0, 2)[:, :, :, None]
    )
    shift_a, scale_a, gate_a, shift_f, scale_f, gate_f = jnp.split(
        mod.reshape(1, 6 * model_width), 6, axis=1
    )
    d_shift_f, d_scale_f, d_gate_a, g_bo = fsum[0:1], fsum[1:2], fsum[2:3], fsum[3]
    ffn_branch = seq_reduce(forward_dot(gelu_act, wd_here)) + bd_full
    block_out = x_mid + gate_f * ffn_branch
    d_gate_f = jnp.sum(cotangent * ffn_branch, axis=0, keepdims=True)
    g_wd = across_rows(gelu_act, d_ffn_item)
    g_bd = column_sums(d_ffn_item)
    g_wu = across_rows(x_f, d_hidden)
    g_bu = column_sums(d_hidden)
    g_wo_run = across_rows(attn_out, d_attn)
    g_wo = lax.psum_scatter(
        g_wo_run.astype(jnp.bfloat16), "seq", scatter_dimension=1, tiled=True
    )

    def block_scores(block_index):
        first_row = block_index * block_rows
        query_blk = lax.dynamic_slice_in_dim(query_heads, first_row, block_rows, 0)
        clip_blk = lax.dynamic_slice_in_dim(clip_ids, first_row, block_rows, 0)
        same_clip = (clip_blk[:, None] == clip_ids[None, :])[None]
        raw_scores = (
            jnp.einsum("qhe,khe->hqk", query_blk, keys_heads, preferred_element_type=jnp.float32)
            * factor
        )
        return (query_blk, same_clip, jnp.where(same_clip, raw_scores, -1e30))

    def attend_back(running, inputs):
        grad_keys, grad_values = running
        block_index, log_blk = inputs
        query_blk, same_clip, masked = block_scores(block_index)
        attn_prob = jnp.exp(masked - log_blk)
        prob_low = attn_prob.astype(jnp.bfloat16)
        grad_blk = lax.dynamic_slice_in_dim(grad_heads, block_index * block_rows, block_rows, 0)
        d_prob = jnp.einsum(
            "qhe,khe->hqk", grad_blk, values_heads, preferred_element_type=jnp.float32
        )
        d_scores = attn_prob * (d_prob - jnp.sum(d_prob * attn_prob, axis=-1, keepdims=True))
        d_scores = jnp.where(same_clip, d_scores, 0.0).astype(jnp.bfloat16)
        d_query = (
            jnp.einsum("hqk,khe->qhe", d_scores, keys_heads, preferred_element_type=jnp.float32)
            * factor
        )
        grad_keys = (
            grad_keys
            + jnp.einsum("hqk,qhe->khe", d_scores, query_blk, preferred_element_type=jnp.float32)
            * factor
        )
        grad_values = grad_values + jnp.einsum(
            "hqk,qhe->khe", prob_low, grad_blk, preferred_element_type=jnp.float32
        )
        return ((grad_keys, grad_values), d_query.astype(jnp.bfloat16))

    zero_heads = jnp.zeros((length, heads_here, head_dim), jnp.float32)
    (grad_keys, grad_values), query_grads = lax.scan(
        attend_back, (zero_heads, zero_heads), (jnp.arange(block_count), log_totals)
    )
    def turned_back(value):
        return rotate(value.astype(jnp.bfloat16).astype(jnp.float32), cosine_tab, -sine_tab)

    d_projected = jnp.concatenate(
        [
            turned_back(query_grads.reshape(length, heads_here, head_dim)).reshape(length, -1),
            turned_back(grad_keys).reshape(length, -1),
            grad_values.reshape(length, -1),
        ],
        axis=1,
    ).astype(jnp.bfloat16)
    d_xa = seq_reduce(against(d_projected, wq_here))
    g_wq = across_rows(x_a, d_projected)
    g_bq = column_sums(d_projected)
    input_pull = jax.vjp(modulate, frames, shift_a, scale_a)[1]
    d_input_part, d_shift_a, d_scale_a = input_pull(d_xa)
    grad_input = d_mid + d_input_part
    mod_part = jnp.concatenate(
        [d_shift_a, d_scale_a, d_gate_a, d_shift_f, d_scale_f, d_gate_f, g_bo[None]], axis=1
    )
    mod_sum = lax.psum(mod_part, "seq")
    d_mod = dp_gather(mod_sum[:, : 6 * model_width].astype(jnp.bfloat16))
    g_wm = across_rows(time_cols, d_mod)
    g_bm = column_sums(
        lax.dynamic_slice_in_dim(d_mod, dp_rank * b_mod.shape[0], b_mod.shape[0], 1)
    )
    d_time_act = lax.all_to_all(
        against(d_mod, w_mod), "dp", split_axis=0, concat_axis=1, tiled=True
    )
    grad_time = jax.vjp(jax.nn.silu, time_embed)[1](d_time_act)[0]

    def spread(value):
        return lax.all_gather(dp_reduce(value), "seq", axis=0).astype(jnp.float32)

    s_wq = (
        spread(g_wq)
        .reshape(seq_count, own_rows, 3, local_width)
        .transpose(1, 2, 0, 3)
        .reshape(own_rows, 3 * model_width)
    )
    s_wo = spread(g_wo).transpose(1, 0, 2).reshape(own_rows, model_width)
    s_wu = (
        spread(g_wu)
        .reshape(seq_count, own_rows, dp_count, units_each)
        .transpose(1, 2, 0, 3)
        .reshape(own_rows, ff_width)
    )
    s_wd = spread(g_wd).reshape(seq_count * units_each, model_width)
    bq_item = lax.all_gather(g_bq, "seq", axis=0).reshape(seq_count, 3, local_width)
    bu_item = lax.all_gather(g_bu, "seq", axis=0).reshape(seq_count, dp_count, units_each)
    bias_terms = jnp.concatenate(
        [
            bq_item.transpose(1, 0, 2).reshape(dp_count, sizes[0]),
            mod_sum[:, 6 * model_width :].reshape(dp_count, sizes[1]),
            bu_item.transpose(1, 0, 2).reshape(dp_count, sizes[2]),
            g_bd.reshape(dp_count, sizes[3]),
        ],
        axis=1,
    )
    bias_sums = lax.psum_scatter(bias_terms, "dp", scatter_dimension=0, tiled=True)[0]
    s_bq, s_bo, s_bu, s_bd = jnp.split(bias_sums, cuts)
    return (
        block_out,
        grad_input,
        grad_time,
        s_wq,
        s_bq,
        s_wo,
        s_bo,
        s_wu,
        s_bu,
        s_wd,
        s_bd,
        g_wm,
        g_bm,
    )


def solution(mesh):
    placed = (
        P(("dp", "seq"), None),
        P("dp", None),
        P("dp", None),
        P("dp", None),
        P("dp"),
        P("dp", None),
        P("dp"),
        P("dp", None),
        P("dp"),
        P("dp", None),
        P("dp"),
        P("dp", None),
        P("dp"),
        P(("dp", "seq"), None),
    )
    return jax.shard_map(
        per_device,
        mesh=mesh,
        in_specs=placed,
        out_specs=(
            P(("dp", "seq"), None),
            P(("dp", "seq"), None),
            P("dp", None),
            P("dp", None),
            P("dp"),
            P("dp", None),
            P("dp"),
            P("dp", None),
            P("dp"),
            P("dp", None),
            P("dp"),
            P("dp", None),
            P("dp"),
        ),
        check_vma=False,
    )
```

```python
import functools
import math

import jax
import jax.numpy as jnp
from jax import lax
from jax.experimental import pallas as pl
from jax.experimental.pallas import tpu as pltpu
from jax.sharding import PartitionSpec as P

HEADS = 16
MESH = pl.DeviceIdType.MESH
f32 = jnp.float32
bf16 = jnp.bfloat16
norm_eps = 1e-06


def nn(left_side, right_side):
    return lax.dot_general(left_side, right_side, (((1,), (0,)), ((), ())), preferred_element_type=f32)


def nt(left_side, right_side):
    return lax.dot_general(left_side, right_side, (((1,), (1,)), ((), ())), preferred_element_type=f32)


def merged(ref):
    shape = ref.shape
    return ref[...].reshape(shape[0] * shape[1], shape[2])


def swap_halves(values, lane):
    up = pltpu.roll(values, 96, 1)
    down = pltpu.roll(values, 32, 1)
    return jnp.where(lane % 64 < 32, up, down)


def gelu_both(h):
    c = math.sqrt(2.0 / math.pi)
    h2 = h * h
    t = jnp.tanh(c * h * (1.0 + 0.044715 * h2))
    half = 0.5 * (1.0 + t)
    return h * half, half + 0.5 * h * (1.0 - t * t) * (c * (1.0 + 3.0 * 0.044715 * h2))


def normed(values):
    mean_val = jnp.mean(values, axis=-1, keepdims=True)
    centred = values - mean_val
    rstd = lax.rsqrt(jnp.mean(centred * centred, axis=-1, keepdims=True) + norm_eps)
    return centred * rstd, rstd


def norm_back(e, n, rstd):
    return (e - jnp.mean(e, axis=-1, keepdims=True) - n * jnp.mean(e * n, axis=-1, keepdims=True)) * rstd


class Links:
    def __init__(self, n, send, recv):
        self.n = n
        self.d = lax.axis_index("dp")
        self.s = lax.axis_index("seq")
        d, s = self.d, self.s
        self.px = d + 1 - 2 * (d % 2)
        self.s1 = s + 1 - 2 * (s % 2)
        self.s2 = (s + 2) % 4
        self.s3 = 3 - s
        self.send, self.recv = send, recv
        self.n_send = self.n_recv = 0

    def sems(self, sends, recvs):
        base = (self.n_send, self.n_recv)
        self.n_send += sends
        self.n_recv += recvs
        return base

    def block(self, i):
        s = self.s
        return (s % 2 + i % 2) % 2 + 2 * ((s // 2 + i // 2) % 2)

    def copy(self, src, dst, si, ri, dev):
        return pltpu.make_async_remote_copy(
            src_ref=src, dst_ref=dst, send_sem=self.send.at[si], recv_sem=self.recv.at[ri],
            device_id=dev, device_id_type=MESH,
        )

    def barrier(self):
        b = pltpu.get_barrier_semaphore()
        for k in range(1, self.n):
            pl.semaphore_signal(b, inc=1, device_id=((self.d + k) % self.n, self.s), device_id_type=MESH)
        for t in (self.s1, self.s2, self.s3):
            pl.semaphore_signal(b, inc=1, device_id=(self.d, t), device_id_type=MESH)
        pl.semaphore_wait(b, self.n + 2)


class ToAll:
    def __init__(self, links, src, buf):
        self.l, self.src, self.buf = links, src, buf
        self.si, self.ri = links.sems(links.n, links.n)

    def _to(self, k):
        l = self.l
        peer = (l.d + k) % l.n
        return l.copy(self.src(peer), self.buf.at[l.d], self.si + k, self.ri + l.d, (peer, l.s))

    def start(self):
        for k in range(1, self.l.n):
            self._to(k).start()

    def wait_recv(self):
        l = self.l
        for k in range(1, l.n):
            peer = (l.d + k) % l.n
            l.copy(self.buf.at[peer], self.buf.at[peer], self.si + k, self.ri + peer, (peer, l.s)).wait_recv()

    def wait_send(self):
        for k in range(1, self.l.n):
            self._to(k).wait_send()


class SeqAll:
    def __init__(self, links, buf):
        self.l, self.buf = links, buf
        self.si, self.ri = links.sems(4, 4)

    def _to(self, k):
        l = self.l
        t = l.block(k)
        return l.copy(self.buf.at[l.s], self.buf.at[l.s], self.si + k, self.ri + l.s, (l.d, t))

    def start(self):
        for k in (2, 3, 1):
            self._to(k).start()

    def wait_recv(self):
        l = self.l
        for k in (1, 2, 3):
            t = l.block(k)
            l.copy(self.buf.at[t], self.buf.at[t], self.si + k, self.ri + t, (l.d, t)).wait_recv()

    def wait_send(self):
        for k in (1, 2, 3):
            self._to(k).wait_send()


class DpGather:
    def __init__(self, links, buf):
        self.l, self.buf = links, buf
        self.si, self.ri = links.sems(links.n, links.n)
        self.half = links.n // 2

    def _z(self, k):
        l = self.l
        return l.copy(self.buf.at[l.d], self.buf.at[l.d], self.si + k, self.ri + l.d, ((l.d + 2 * k) % l.n, l.s))

    def _x(self, k):
        l = self.l
        r = (l.d + 2 * k) % l.n
        return l.copy(self.buf.at[r], self.buf.at[r], self.si + self.half + k, self.ri + r, (l.px, l.s))

    def start(self):
        for k in range(1, self.half):
            self._z(k).start()
        self._x(0).start()

    def hand_on(self):
        l = self.l
        for k in range(1, self.half):
            r = (l.d + 2 * k) % l.n
            l.copy(self.buf.at[r], self.buf.at[r], self.si, self.ri + r, (r, l.s)).wait_recv()
            self._x(k).start()

    def wait_rest(self):
        l = self.l
        for k in range(self.half):
            r = (l.px + 2 * k) % l.n
            l.copy(self.buf.at[r], self.buf.at[r], self.si, self.ri + r, (l.px, l.s)).wait_recv()

    def wait_send(self):
        for k in range(1, self.half):
            self._z(k).wait_send()
        for k in range(self.half):
            self._x(k).wait_send()


class SeqGather:
    def __init__(self, links, buf):
        self.l, self.buf = links, buf
        self.si, self.ri = links.sems(3, 4)

    def _c(self, slot, k, t):
        l = self.l
        return l.copy(self.buf.at[slot], self.buf.at[slot], self.si + k, self.ri + slot, (l.d, t))

    def start(self):
        l = self.l
        self._c(l.s, 0, l.s2).start()
        self._c(l.s, 1, l.s1).start()

    def hand_on(self):
        l = self.l
        self.wait(l.s2)
        self._c(l.s2, 2, l.s1).start()

    def wait(self, slot):
        l = self.l
        l.copy(self.buf.at[slot], self.buf.at[slot], self.si, self.ri + slot, (l.d, l.s1)).wait_recv()

    def wait_send(self):
        l = self.l
        self._c(l.s, 0, l.s2).wait_send()
        self._c(l.s, 1, l.s1).wait_send()
        self._c(l.s2, 2, l.s1).wait_send()


class SeqSwap:
    def __init__(self, links, out, into):
        self.l, self.out, self.into = links, out, into
        self.si, self.ri = links.sems(4, 4)

    def copy_to(self, i):
        l = self.l
        t = l.block(i)
        return l.copy(self.out.at[t], self.into.at[l.s], self.si + i, self.ri + l.s, (l.d, t))

    def wait_recv(self):
        l = self.l
        for i in (1, 2, 3):
            t = l.block(i)
            l.copy(self.into.at[t], self.into.at[t], self.si + i, self.ri + t, (l.d, t)).wait_recv()

    def wait_send(self):
        for i in (1, 2, 3):
            self.copy_to(i).wait_send()


class SeqSum:
    def __init__(self, links, held):
        self.l, self.held = links, held
        self.si, self.ri = links.sems(3, 3)

    def _c(self, k, t):
        l = self.l
        return l.copy(self.held.at[k], self.held.at[3 + k], self.si + k, self.ri + k, (l.d, t))

    def far(self, term):
        l, held = self.l, self.held
        held[0] = term(l.s3).astype(bf16)
        self._c(0, l.s1).start()
        mine = term(l.s2)
        self._c(0, l.s1).wait_recv()
        held[1] = (mine + held[3].astype(f32)).astype(bf16)
        self._c(1, l.s2).start()

    def near(self, term):
        l = self.l
        self.held[2] = term(l.s1).astype(bf16)
        self._c(2, l.s1).start()

    def total(self, mine):
        l, held = self.l, self.held
        self._c(2, l.s1).wait_recv()
        self._c(1, l.s2).wait_recv()
        return mine + held[5].astype(f32) + held[4].astype(f32)

    def wait_send(self):
        l = self.l
        self._c(0, l.s1).wait_send()
        self._c(1, l.s2).wait_send()
        self._c(2, l.s1).wait_send()


def kernel_a(
    n,
    frames, cot, tcols, bm, bias, wu_own, cos, sin, idr, idc, wm_hbm, wq_hbm, wo_hbm, wd_hbm,
    xa, q, k, v, kt, vt, lse, ao, gh, dffn, gelu, xf, dhid, wq, wd, dmid, xmid, dattn, mod, fsum, bd_full, tbuf,
    wm, wu, wo, psend, pbuf, bbuf, n_in, attn_branch, n_mid, ao_out, do_out, held,
    send, recv, local,
):
    l = Links(n, send, recv)
    d, s = l.d, l.s
    rows, width = frames.shape
    quarter = width // 4
    own_rows = tcols.shape[2]
    mq = bm.shape[1]
    units = wd.shape[1]
    ff_q = wu.shape[2]
    lane = lax.broadcasted_iota(jnp.int32, (rows, 128), 1)
    take = [
        pltpu.make_async_copy(wm_hbm.at[:, pl.ds(pl.multiple_of(s * mq, 128), mq)], wm, local.at[0]),
        pltpu.make_async_copy(wd_hbm.at[pl.ds(pl.multiple_of(s * units, 8), units), :], wd.at[d], local.at[1]),
        pltpu.make_async_copy(wo_hbm.at[:, pl.ds(pl.multiple_of(s * quarter, 128), quarter)], wo.at[s, d], local.at[2]),
    ] + [
        pltpu.make_async_copy(
            wq_hbm.at[:, pl.ds(pl.multiple_of(j * width + s * quarter, 128), quarter)],
            wq.at[d, :, pl.ds(j * quarter, quarter)], local.at[3 + j],
        )
        for j in range(3)
    ]
    for c in take:
        c.start()
    times = ToAll(l, lambda peer: tcols.at[peer], tbuf)
    parts = ToAll(l, lambda peer: psend.at[peer], pbuf)
    biases = ToAll(l, lambda peer: bias.at[0], bbuf)
    mods = SeqAll(l, mod)
    g_wq, g_wu, g_wd = DpGather(l, wq), DpGather(l, wu), DpGather(l, wd)
    g_wo = DpGather(l, wo.at[s])
    s_xa, s_df, s_xf, s_wo = SeqGather(l, xa), SeqGather(l, dffn), SeqGather(l, xf), SeqGather(l, wo)
    w_ao, w_do = SeqSwap(l, ao_out, ao), SeqSwap(l, do_out, gh)
    sums = SeqSum(l, held)
    l.barrier()
    times.start()
    for c in take[3:]:
        c.wait()
    g_wq.start()
    biases.start()
    tbuf[d] = tcols[d]
    wu[d] = wu_own[...]
    for c in take[:3]:
        c.wait()
    n_in[...] = normed(frames[...])[0]
    times.wait_recv()
    lhs = jnp.concatenate([tbuf[i] for i in range(n)], axis=0).astype(bf16)
    part = nn(lhs, wm[...]) + bm[...]
    for i in range(n):
        psend[i] = part[i : i + 1]
    parts.start()
    total = psend[d]
    parts.wait_recv()
    for j in range(1, n):
        total = total + pbuf[(d + j) % n]
    mod[s] = total
    mods.start()
    mods.wait_recv()
    flat = jnp.concatenate([mod[i] for i in range(4)], axis=1)
    shift_a, scale_a, gate_a, shift_f, scale_f, gate_f = (
        flat[:, i * width : (i + 1) * width] for i in range(6)
    )
    xa[s] = (n_in[...] * (1.0 + scale_a) + shift_a).astype(bf16)
    s_xa.start()
    dffn[s] = (gate_f * cot[...]).astype(bf16)
    g_wq.hand_on()
    g_wd.start()
    g_wu.start()
    g_wo.start()
    g_wq.wait_rest()
    biases.wait_recv()
    own_bias = bias[0]
    for j in range(1, n):
        own_bias = own_bias + bbuf[(d + j) % n]
    qw = 3 * quarter
    bq = own_bias[:, :qw]
    bo = own_bias[:, qw : qw + width]
    bu = own_bias[:, qw + width : qw + width + ff_q]
    bd_full[...] = own_bias[:, qw + width + ff_q :]

    def project(i, carry):
        @pl.when(i == 1)
        def _():
            s_xa.wait(l.s1)

        @pl.when(i == 2)
        def _():
            s_xa.hand_on()
            s_df.start()

        @pl.when(i == 3)
        def _():
            s_xa.wait(l.s3)

        b = l.block(i)
        at = pl.ds(pl.multiple_of(b * rows, rows), rows)
        pr = nn(xa[b], merged(wq)) + bq
        cb, sb = cos[at, :], sin[at, :]
        for p in range(quarter // 128):
            c0 = 128 * p
            qp = pr[:, c0 : c0 + 128]
            kp = pr[:, quarter + c0 : quarter + c0 + 128]
            vp = pr[:, 2 * quarter + c0 : 2 * quarter + c0 + 128].astype(bf16)
            qp = (qp * cb + swap_halves(qp, lane) * sb).astype(bf16)
            kp = (kp * cb + swap_halves(kp, lane) * sb).astype(bf16)
            q[at, c0 : c0 + 128] = qp * jnp.bfloat16(0.125)
            k[at, c0 : c0 + 128] = kp
            v[at, c0 : c0 + 128] = vp
            kt[p, :, at] = jnp.transpose(kp.astype(f32)).astype(bf16)
            vt[p, :, at] = jnp.transpose(vp.astype(f32)).astype(bf16)
        return carry

    lax.fori_loop(0, 4, project, 0)
    g_wd.hand_on()
    g_wu.hand_on()

    def attend(j, carry):
        i = (j + 2) % 4
        b = l.block(i)
        at = pl.ds(pl.multiple_of(b * rows, rows), rows)
        same = idc[...] == idr[:, at]
        for p in range(quarter // 128):
            qp, kp = q[at, 128 * p : 128 * p + 128], k[:, 128 * p : 128 * p + 128]
            outs = []
            for h in range(2):
                qm = jnp.where((lane < 64) == (h == 0), qp, jnp.zeros_like(qp))
                sc = jnp.where(same, nt(kp, qm), -1e30)
                top = jnp.max(sc, axis=0, keepdims=True)
                ex = jnp.exp(sc - top)
                su = jnp.sum(ex, axis=0, keepdims=True)
                lse[2 * p + h, :, at] = top + jnp.log(su)
                pt = (ex * (1.0 / su)).astype(bf16)
                outs.append(nn(vt[p, 64 * h : 64 * h + 64, :], pt))
            ao_out[b, :, 128 * p : 128 * p + 128] = jnp.transpose(jnp.concatenate(outs, axis=0)).astype(bf16)

        @pl.when(j != 2)
        def _():
            w_ao.copy_to(i).start()

        @pl.when(j == 2)
        def _():
            ao[s] = ao_out[s]

        @pl.when(j == 0)
        def _():
            g_wo.hand_on()
            s_df.hand_on()

        @pl.when(j == 1)
        def _():
            g_wo.wait_rest()
            s_wo.start()

        @pl.when(j == 3)
        def _():
            s_wo.hand_on()

        return carry

    lax.fori_loop(0, 4, attend, 0)
    s_wo.wait(l.s1)
    s_wo.wait(l.s3)
    w_ao.wait_recv()
    left = jnp.concatenate([ao[i] for i in range(4)], axis=1)
    for c in range(4):
        cs = slice(c * quarter, (c + 1) * quarter)
        attn_branch[:, cs] = nn(left, merged(wo.at[c])) + bo[:, cs]
    xm = frames[...] + gate_a * attn_branch[...]
    xmid[...] = xm
    nm, rstd = normed(xm)
    n_mid[...] = nm
    xf[s] = (nm * (1.0 + scale_f) + shift_f).astype(bf16)
    s_xf.start()
    s_df.wait(l.s1)
    s_df.wait(l.s3)
    g_wd.wait_rest()
    g_wu.wait_rest()

    def term(b):
        at = pl.ds(pl.multiple_of(b * rows, rows), rows)
        return nt(dhid[at, :], merged(wu))

    def feed(i, carry):
        @pl.when(i == 1)
        def _():
            s_xf.wait(l.s1)

        @pl.when(i == 2)
        def _():
            sums.near(term)
            s_xf.hand_on()

        @pl.when(i == 3)
        def _():
            s_xf.wait(l.s3)

        b = l.block(i)
        at = pl.ds(pl.multiple_of(b * rows, rows), rows)
        act, slope = gelu_both(nn(xf[b], merged(wu)) + bu)
        gelu[at, :] = act.astype(bf16)
        dhid[at, :] = (nt(dffn[b], merged(wd)) * slope).astype(bf16)
        return carry

    lax.fori_loop(0, 4, feed, 0)
    sums.far(term)
    g = sums.total(term(s))
    nm = n_mid[...]
    fsum[0:1, :] = jnp.sum(g, axis=0, keepdims=True)
    fsum[1:2, :] = jnp.sum(g * nm, axis=0, keepdims=True)
    dm = cot[...] + norm_back(g * (1.0 + scale_f), nm, rstd)
    dmid[...] = dm
    da = (gate_a * dm).astype(bf16)
    dattn[...] = da
    fsum[2:3, :] = jnp.sum(dm * attn_branch[...], axis=0, keepdims=True)
    fsum[3:4, :] = jnp.sum(da.astype(f32), axis=0, keepdims=True)
    per = n // 4

    def give(j, carry):
        i = (j + 2) % 4
        t = l.block(i)
        out = None
        for c in range(4):
            wt = wo[c, pl.ds(t * per, per)].reshape(quarter, quarter)
            o = nt(dattn[:, c * quarter : (c + 1) * quarter], wt)
            out = o if out is None else out + o
        do_out[t] = out.astype(bf16)

        @pl.when(j != 2)
        def _():
            w_do.copy_to(i).start()

        @pl.when(j == 2)
        def _():
            gh[s] = do_out[s]

        return carry

    lax.fori_loop(0, 4, give, 0)
    w_do.wait_recv()
    for c in (times, parts, biases, mods, g_wq, g_wu, g_wd, g_wo, s_xa, s_df, s_xf, s_wo, w_ao, w_do, sums):
        c.wait_send()


def run_a(n, frames, cot, tcols, bm, bias, wu_own, cos, sin, idr, idc, w_mod, w_qkv, w_out, w_down):
    rows, width = frames.shape
    item = 4 * rows
    quarter = width // 4
    ff = w_down.shape[0] * n
    ff_q = ff // 4
    own_rows = width // n
    units = ff_q // n
    heads = quarter // 64
    pairs = quarter // 128
    S = jax.ShapeDtypeStruct
    outs = [
        S((4, rows, width), bf16), S((item, quarter), bf16), S((item, quarter), bf16), S((item, quarter), bf16),
        S((pairs, 128, item), bf16), S((pairs, 128, item), bf16), S((heads, 1, item), f32),
        S((4, rows, quarter), bf16), S((4, rows, quarter), bf16), S((4, rows, width), bf16), S((item, ff_q), bf16),
        S((4, rows, width), bf16), S((item, ff_q), bf16), S((n, own_rows, 3 * quarter), bf16), S((n, units, width), bf16),
        S((rows, width), f32), S((rows, width), f32), S((rows, width), bf16), S((4, 1, 6 * quarter), f32),
        S((8, width), f32), S((1, width), f32), S((n, 1, own_rows), f32),
    ]
    V = pltpu.VMEM
    scratch = [
        V((own_rows, 6 * quarter), bf16), V((n, own_rows, ff_q), bf16), V((4, n, own_rows, quarter), bf16),
        V((n, 1, 6 * quarter), f32), V((n, 1, 6 * quarter), f32), V((n, 1, bias.shape[2]), f32),
        V((rows, width), f32), V((rows, width), f32), V((rows, width), f32), V((4, rows, quarter), bf16),
        V((4, rows, quarter), bf16), V((6, rows, width), bf16),
        pltpu.SemaphoreType.DMA((7 * n + 40,)), pltpu.SemaphoreType.DMA((7 * n + 40,)), pltpu.SemaphoreType.DMA((6,)),
    ]
    vm = pl.BlockSpec(memory_space=pltpu.VMEM)
    hb = pl.BlockSpec(memory_space=pl.ANY)
    return pl.pallas_call(
        functools.partial(kernel_a, n),
        out_shape=outs,
        in_specs=[vm] * 10 + [hb] * 4,
        out_specs=[vm] * len(outs),
        scratch_shapes=scratch,
        compiler_params=pltpu.CompilerParams(collective_id=0, has_side_effects=True, vmem_limit_bytes=60 << 20),
    )(frames, cot, tcols, bm, bias, wu_own, cos, sin, idr, idc, w_mod, w_qkv, w_out, w_down)


def tn(left_side, right_side):
    return lax.dot_general(left_side, right_side, (((0,), (0,)), ((), ())), preferred_element_type=f32)


class DpSum:
    def __init__(self, links, g, xin, zin):
        self.l, self.g, self.xin, self.zin = links, g, xin, zin
        self.half = links.n // 2
        self.si, self.ri = links.sems(links.n, links.n)

    def _x(self, t):
        l = self.l
        h = t // 2
        return l.copy(self.g.at[t], self.xin.at[h], self.si + h, self.ri + h, (l.px, l.s))

    def _z(self, k):
        l = self.l
        t = (l.d + 2 * k) % l.n
        at = self.half + k
        return l.copy(self.g.at[t], self.zin.at[k], self.si + at, self.ri + at, (t, l.s))

    def send_x(self, first, count):
        for i in range(count // 2):
            self._x(first + 2 * i + self.l.px % 2).start()

    def fold(self):
        l = self.l

        def one(k, carry):
            t = (l.d + 2 * k) % l.n
            h = t // 2
            l.copy(self.xin.at[h], self.xin.at[h], self.si, self.ri + h, (l.px, l.s)).wait_recv()
            self.g[t] = (self.g[t].astype(f32) + self.xin[h].astype(f32)).astype(bf16)
            self._z(k).start()
            return carry

        lax.fori_loop(1, self.half, one, 0)

    def total(self):
        l = self.l
        h = l.d // 2
        l.copy(self.xin.at[h], self.xin.at[h], self.si, self.ri + h, (l.px, l.s)).wait_recv()
        out = self.g[l.d].astype(f32) + self.xin[h].astype(f32)
        for k in range(1, self.half):
            self._z(k).wait_recv()
            out = out + self.zin[k].astype(f32)
        return out

    def wait_send(self):
        l = self.l
        for k in range(self.half):
            self._x((l.px + 2 * k) % l.n).wait_send()
        for k in range(1, self.half):
            self._z(k).wait_send()


def kernel_b(
    n,
    frames, cot, time3, tbuf, cos, sin, idr, idc, xa, q, k, v, kt, lse, ao, gh, dffn, gelu, xf, dhid, wq, wd,
    dmid, xmid, dattn, mod, fsum, bd_full, wm,
    block_out, grad_input, grad_time, gwm, gbm, f_wq, f_wo, f_wu, f_wd, f_b,
    g_wq, x_wq, z_wq, g_wo, x_wo, z_wo, g_wu, x_wu, z_wu, g_wd, x_wd, z_wd,
    held_f, held_o, held_a, dk, dv, dproj, n_in, em, lm, ebuf, lbuf, eb, ebb, lb, lbb, dts, dtb,
    send, recv,
):
    l = Links(n, send, recv)
    d, s = l.d, l.s
    rows, width = frames.shape
    item = 4 * rows
    quarter = width // 4
    own_rows = wm.shape[0]
    units = wd.shape[1]
    ff_q = gelu.shape[1]
    pairs = quarter // 128
    lane = lax.broadcasted_iota(jnp.int32, (rows, 128), 1)
    sum_f, sum_o, sum_a = SeqSum(l, held_f), SeqSum(l, held_o), SeqSum(l, held_a)
    d_wq, d_wo, d_wu, d_wd = (
        DpSum(l, g_wq, x_wq, z_wq), DpSum(l, g_wo, x_wo, z_wo), DpSum(l, g_wu, x_wu, z_wu), DpSum(l, g_wd, x_wd, z_wd),
    )
    o_wq, o_wo, o_wu, o_wd = SeqGather(l, f_wq), SeqGather(l, f_wo), SeqGather(l, f_wu), SeqGather(l, f_wd)
    e_mod, l_mod, o_b = SeqAll(l, em), SeqAll(l, lm), SeqAll(l, f_b)
    e_all, l_all = ToAll(l, lambda peer: ebuf.at[d], ebuf), ToAll(l, lambda peer: lbuf.at[d], lbuf)
    eb_all, lb_all = ToAll(l, lambda peer: eb, ebb), ToAll(l, lambda peer: lb, lbb)
    t_all = ToAll(l, lambda peer: dts.at[peer], dtb)
    flat = jnp.concatenate([mod[i] for i in range(4)], axis=1)
    scale_a = flat[:, width : 2 * width]
    gate_f = flat[:, 5 * width :]
    l.barrier()

    def at_rows(b):
        return pl.ds(pl.multiple_of(b * rows, rows), rows)

    def ffn_term(b):
        return nn(gelu[at_rows(b), :], merged(wd))

    def out_term(t):
        part = dattn[:, pl.ds(pl.multiple_of(t * quarter, 128), quarter)]
        return jnp.concatenate([tn(ao[i], part) for i in range(4)], axis=0)

    def xa_term(b):
        return nt(dproj[at_rows(b), :], merged(wq))

    sum_f.far(ffn_term)

    def make(left_of, right, g, chain, each):
        per = 256 // each

        def one(m, carry):
            val = tn(left_of(m), right()).astype(bf16)
            g[pl.ds(m * per, per)] = val.reshape(per, each, val.shape[1])
            chain.send_x(m * per, per)
            return carry

        lax.fori_loop(0, n // per, one, 0)

    make(lambda m: gelu[:, pl.ds(pl.multiple_of(m * 256, 256), 256)], lambda: merged(dffn), g_wd, d_wd, units)

    def cols_of(ref, m):
        return ref[:, :, pl.ds(pl.multiple_of(m * 256, 256), 256)].reshape(item, 256)

    make(lambda m: cols_of(xf, m), lambda: dhid[...], g_wu, d_wu, own_rows)
    sum_f.near(ffn_term)
    eb[:, :ff_q] = jnp.sum(dhid[...].astype(f32), axis=0, keepdims=True)
    eb[:, ff_q : ff_q + width] = fsum[3:4, :]
    eb[:, ff_q + width :] = jnp.sum(dffn[s].astype(f32), axis=0, keepdims=True)
    eb_all.start()
    n_val, rstd = normed(frames[...])
    n_in[...] = n_val
    dk[...] = jnp.zeros_like(dk)
    dv[...] = jnp.zeros_like(dv)

    def turned(values, at):
        val = values.astype(bf16).astype(f32)
        return (val * cos[at, :] - swap_halves(val, lane) * sin[at, :]).astype(bf16)

    def attend_back(j, carry):
        b = j
        at = at_rows(b)
        same = idc[...] == idr[:, at]
        for p in range(pairs):
            c0 = 128 * p
            kp, vp = k[:, c0 : c0 + 128], v[:, c0 : c0 + 128]
            qp, dop = q[at, c0 : c0 + 128], gh[b, :, c0 : c0 + 128]
            dqs = []
            for h in range(2):
                mine = (lane < 64) == (h == 0)
                qm = jnp.where(mine, qp, jnp.zeros_like(qp))
                dom = jnp.where(mine, dop, jnp.zeros_like(dop))
                pt = jnp.exp(jnp.where(same, nt(kp, qm), -1e30) - lse[2 * p + h, :, at])
                dpt = nt(vp, dom)
                mean = jnp.sum(dpt * pt, axis=0, keepdims=True)
                dst = (pt * (dpt - mean)).astype(bf16)
                dv[p] += nn(pt.astype(bf16), dom)
                dk[p] += nn(dst, qm)
                dqs.append(nn(kt[p, 64 * h : 64 * h + 64, :], dst))
            dq = jnp.transpose(jnp.concatenate(dqs, axis=0)) * 0.125
            dproj[at, c0 : c0 + 128] = turned(dq, at)

        @pl.when(j == 0)
        def _():
            d_wd.fold()
            sum_o.far(out_term)

        @pl.when(j == 1)
        def _():
            sum_o.near(out_term)
            ffn = sum_f.total(ffn_term(s)) + bd_full[...]
            block_out[...] = xmid[...] + gate_f * ffn
            em[s, :, 3 * width :] = jnp.sum(cot[...] * ffn, axis=0, keepdims=True)
            em[s, :, :width] = fsum[2:3, :]
            em[s, :, width : 2 * width] = fsum[0:1, :]
            em[s, :, 2 * width : 3 * width] = fsum[1:2, :]
            e_mod.start()

        @pl.when(j == 2)
        def _():
            d_wu.fold()
            g_wo[...] = sum_o.total(out_term(s)).astype(bf16).reshape(n, own_rows, quarter)
            d_wo.send_x(0, n)

        @pl.when(j == 3)
        def _():
            e_mod.wait_recv()
            tot = em[0] + em[1] + em[2] + em[3]
            ebuf[d] = tot.astype(bf16).astype(f32)
            e_all.start()
            f_wd[s] = d_wd.total().astype(bf16)
            o_wd.start()

        return carry

    lax.fori_loop(0, 4, attend_back, 0)

    def finish(b, carry):
        at = at_rows(b)
        for p in range(pairs):
            c0 = 128 * p
            dproj[at, quarter + c0 : quarter + c0 + 128] = turned(dk[p, at, :], at)
            dproj[at, 2 * quarter + c0 : 2 * quarter + c0 + 128] = dv[p, at, :].astype(bf16)
        return carry

    lax.fori_loop(0, 4, finish, 0)
    sum_a.far(xa_term)
    make(lambda m: cols_of(xa, m), lambda: dproj[...], g_wq, d_wq, own_rows)
    sum_a.near(xa_term)
    d_wo.fold()
    lb[...] = jnp.sum(dproj[...].astype(f32), axis=0, keepdims=True)
    lb_all.start()
    o_wd.hand_on()
    f_wu[s] = d_wu.total().astype(bf16)
    o_wu.start()
    times = jnp.concatenate([tbuf[i] for i in range(n)], axis=0).astype(bf16)
    e_all.wait_recv()
    dm_e = jnp.concatenate([ebuf[i] for i in range(n)], axis=0)
    gbm[:, 2 * width :] = jnp.sum(dm_e, axis=0, keepdims=True)
    dm_e = dm_e.astype(bf16)
    for c in range(2, 6):
        gwm[:, c * width : (c + 1) * width] = tn(times, dm_e[:, (c - 2) * width : (c - 1) * width])
    dt = nt(dm_e, wm[:, 2 * width :])
    g = sum_a.total(xa_term(s))
    n_val = n_in[...]
    lm[s, :, :width] = jnp.sum(g, axis=0, keepdims=True)
    lm[s, :, width:] = jnp.sum(g * n_val, axis=0, keepdims=True)
    l_mod.start()
    grad_input[...] = dmid[...] + norm_back(g * (1.0 + scale_a), n_val, rstd)
    d_wq.fold()
    l_mod.wait_recv()
    lbuf[d] = (lm[0] + lm[1] + lm[2] + lm[3]).astype(bf16).astype(f32)
    l_all.start()
    o_wu.hand_on()
    f_wo[s] = d_wo.total().astype(bf16)
    o_wo.start()
    eb_all.wait_recv()
    lb_all.wait_recv()
    esum, lsum = eb[...], lb[...]
    for j in range(1, n):
        esum = esum + ebb[(d + j) % n]
        lsum = lsum + lbb[(d + j) % n]
    f_b[s, :, : 3 * quarter] = lsum
    f_b[s, :, 3 * quarter :] = esum
    o_b.start()
    l_all.wait_recv()
    dm_l = jnp.concatenate([lbuf[i] for i in range(n)], axis=0)
    gbm[:, : 2 * width] = jnp.sum(dm_l, axis=0, keepdims=True)
    dm_l = dm_l.astype(bf16)
    dt = dt + nt(dm_l, wm[:, : 2 * width])
    for i in range(n):
        dts[i] = dt[i : i + 1]
    t_all.start()
    for c in range(2):
        gwm[:, c * width : (c + 1) * width] = tn(times, dm_l[:, c * width : (c + 1) * width])
    f_wq[s] = d_wq.total().astype(bf16)
    o_wq.start()
    o_wo.hand_on()
    t_all.wait_recv()
    dtb[d] = dts[d]
    tv = time3[...]
    sig = 1.0 / (1.0 + jnp.exp(-tv))
    grad_time[...] = dtb[...] * (sig + tv * sig * (1.0 - sig))
    o_wq.hand_on()
    for o in (o_wq, o_wo, o_wu, o_wd):
        o.wait(l.s1)
        o.wait(l.s3)
    o_b.wait_recv()
    for c in (
        sum_f, sum_o, sum_a, d_wq, d_wo, d_wu, d_wd, o_wq, o_wo, o_wu, o_wd, e_mod, l_mod, o_b,
        e_all, l_all, eb_all, lb_all, t_all,
    ):
        c.wait_send()


def run_b(n, *ops):
    frames, w_mod, wd, gelu = ops[0], ops[-1], ops[21], ops[17]
    rows, width = frames.shape
    item, quarter, own_rows, units, ff_q = 4 * rows, width // 4, w_mod.shape[0], wd.shape[1], gelu.shape[1]
    S, V = jax.ShapeDtypeStruct, pltpu.VMEM
    bw = 3 * quarter + ff_q + 2 * width
    outs = [
        S((rows, width), f32), S((rows, width), f32), S((n, 1, own_rows), f32), S((own_rows, 6 * width), f32),
        S((1, 6 * width), f32), S((4, own_rows, 3 * quarter), bf16), S((4, own_rows, quarter), bf16),
        S((4, own_rows, ff_q), bf16), S((4, units, width), bf16), S((4, 1, bw), f32),
    ]

    def chain(a, b):
        return [V((n, a, b), bf16), V((n // 2, a, b), bf16), V((n // 2, a, b), bf16)]

    scratch = (
        chain(own_rows, 3 * quarter) + chain(own_rows, quarter) + chain(own_rows, ff_q) + chain(units, width)
        + [V((6, rows, width), bf16), V((6, width, quarter), bf16), V((6, rows, width), bf16)]
        + [V((quarter // 128, item, 128), f32)] * 2
        + [
            V((item, 3 * quarter), bf16), V((rows, width), f32), V((4, 1, 4 * width), f32), V((4, 1, 2 * width), f32),
            V((n, 1, 4 * width), f32), V((n, 1, 2 * width), f32), V((1, ff_q + 2 * width), f32),
            V((n, 1, ff_q + 2 * width), f32), V((1, 3 * quarter), f32), V((n, 1, 3 * quarter), f32),
            V((n, 1, own_rows), f32), V((n, 1, own_rows), f32),
        ]
        + [pltpu.SemaphoreType.DMA((9 * n + 40,)), pltpu.SemaphoreType.DMA((9 * n + 40,))]
    )
    vm = pl.BlockSpec(memory_space=pltpu.VMEM)
    return pl.pallas_call(
        functools.partial(kernel_b, n),
        out_shape=outs,
        in_specs=[vm] * len(ops),
        out_specs=[vm] * len(outs),
        scratch_shapes=scratch,
        compiler_params=pltpu.CompilerParams(collective_id=1, has_side_effects=True, vmem_limit_bytes=62 << 20),
    )(*ops)


def clip_layout(lengths, length):
    clips = lengths.shape[0]
    earlier = jnp.arange(clips)[None, :] <= jnp.arange(clips)[:, None]
    clip_end = jnp.sum(jnp.where(earlier, lengths[None, :], 0), axis=1)
    clip_start = clip_end - lengths
    item_frames = jnp.arange(length, dtype=jnp.int32)
    inside = (item_frames[:, None] >= clip_start[None, :]) & (
        item_frames[:, None] < clip_end[None, :]
    )
    clip_ids = jnp.sum(
        jnp.where(inside, jnp.arange(clips, dtype=jnp.int32)[None, :], 0), axis=1
    )
    positions = item_frames - jnp.sum(jnp.where(inside, clip_start[None, :], 0), axis=1)
    return (clip_ids, positions)


def tables(positions):
    lanes = jnp.arange(128)
    inv_rate = jnp.exp((lanes % 32).astype(f32) * (-2.0 * math.log(10000.0) / 64))
    phases = positions.astype(f32)[:, None] * inv_rate[None, :]
    sign = jnp.where(lanes % 64 < 32, -1.0, 1.0)
    return jnp.cos(phases), jnp.sin(phases) * sign[None, :]


def prepare(seq_rank, dp_rank, n, frames, time_embed, clip_len, b_qkv, b_out, w_up, b_up, b_down, b_mod):
    rows, width = frames.shape
    quarter = width // 4
    own_rows, ff = w_up.shape
    units = ff // 4 // n
    clip_ids, positions = clip_layout(clip_len[0], 4 * rows)
    cos, sin = tables(positions)
    tcols = jax.nn.silu(time_embed).astype(bf16).astype(f32).reshape(n, 1, own_rows)

    def placed(b):
        return lax.dynamic_update_slice(
            jnp.zeros((b.shape[0] * n,), f32), b.astype(f32), (dp_rank * b.shape[0],)
        )

    def own(value, axis):
        return lax.dynamic_index_in_dim(value, seq_rank, axis, keepdims=False)

    bm = own(placed(b_mod).reshape(4, 6 * quarter), 0)[None]
    bias = jnp.concatenate(
        [
            own(placed(b_qkv).reshape(3, 4, quarter), 1).reshape(-1),
            placed(b_out),
            own(placed(b_up).reshape(n, 4, units), 1).reshape(-1),
            placed(b_down),
        ]
    ).reshape(1, 1, -1)
    wu_own = own(w_up.reshape(own_rows, n, 4, units), 2).reshape(own_rows, ff // 4)
    return tcols, bm, bias, wu_own, cos, sin, clip_ids[None, :], clip_ids[:, None]


def per_device(
    frames, time_embed, clip_len, w_qkv, b_qkv, w_out, b_out, w_up, b_up, w_down, b_down, w_mod, b_mod, cotangent
):
    n = lax.axis_size("dp")
    seq_rank, dp_rank = lax.axis_index("seq"), lax.axis_index("dp")
    rows, width = frames.shape
    quarter = width // 4
    own_rows, ff = w_up.shape
    units = w_down.shape[0] // 4
    pre = prepare(seq_rank, dp_rank, n, frames, time_embed, clip_len, b_qkv, b_out, w_up, b_up, b_down, b_mod)
    cos, sin, idr, idc = pre[4:]
    outs = run_a(n, frames, cotangent, *pre, w_mod, w_qkv, w_out, w_down)
    xa, q, k, v, kt, _, lse, ao, gh, dffn, gelu, xf, dhid, wq, wd, dmid, xmid, dattn, mod, fsum, bd, tbuf = outs
    time3 = time_embed.reshape(n, 1, own_rows)
    block_out, grad_input, grad_time, gwm, gbm, f_wq, f_wo, f_wu, f_wd, f_b = run_b(
        n, frames, cotangent, time3, tbuf, cos, sin, idr, idc, xa, q, k, v, kt, lse, ao, gh, dffn, gelu, xf, dhid,
        wq, wd, dmid, xmid, dattn, mod, fsum, bd, w_mod,
    )
    s_wq = f_wq.astype(f32).reshape(4, own_rows, 3, quarter).transpose(1, 2, 0, 3).reshape(own_rows, 3 * width)
    s_wo = f_wo.astype(f32).transpose(1, 0, 2).reshape(own_rows, width)
    s_wu = f_wu.astype(f32).reshape(4, own_rows, n, units).transpose(1, 2, 0, 3).reshape(own_rows, ff)
    s_wd = f_wd.astype(f32).reshape(4 * units, width)
    qw, fq = 3 * quarter, ff // 4
    bq = f_b[:, 0, :qw].reshape(4, 3, quarter).transpose(1, 0, 2).reshape(-1)
    bu = f_b[:, 0, qw : qw + fq].reshape(4, n, units).transpose(1, 0, 2).reshape(-1)
    bo = jnp.sum(f_b[:, 0, qw + fq : qw + fq + width], axis=0)
    bd = jnp.sum(f_b[:, 0, qw + fq + width :], axis=0)

    def own(value, like):
        size = like.shape[0]
        return lax.dynamic_slice_in_dim(value, dp_rank * size, size, 0)

    return (
        block_out, grad_input, grad_time.reshape(1, width), s_wq, own(bq, b_qkv), s_wo, own(bo, b_out), s_wu,
        own(bu, b_up), s_wd, own(bd, b_down), gwm, own(gbm[0], b_mod),
    )


def solution(mesh):
    placed = (
        P(("dp", "seq"), None),
        P("dp", None),
        P("dp", None),
        P("dp", None),
        P("dp"),
        P("dp", None),
        P("dp"),
        P("dp", None),
        P("dp"),
        P("dp", None),
        P("dp"),
        P("dp", None),
        P("dp"),
        P(("dp", "seq"), None),
    )
    return jax.shard_map(
        per_device,
        mesh=mesh,
        in_specs=placed,
        out_specs=(
            P(("dp", "seq"), None),
            P(("dp", "seq"), None),
            P("dp", None),
            P("dp", None),
            P("dp"),
            P("dp", None),
            P("dp"),
            P("dp", None),
            P("dp"),
            P("dp", None),
            P("dp"),
            P("dp", None),
            P("dp"),
        ),
        check_vma=False,
    )
```

```python
import functools
import math

import jax
import jax.numpy as jnp
from jax import lax
from jax.experimental import pallas as pl
from jax.experimental.pallas import tpu as pltpu
from jax.sharding import PartitionSpec as P

HEADS = 16
MESH = pl.DeviceIdType.MESH
f32 = jnp.float32
bf16 = jnp.bfloat16
norm_eps = 1e-06


def nn(left_side, right_side):
    return lax.dot_general(left_side, right_side, (((1,), (0,)), ((), ())), preferred_element_type=f32)


def nt(left_side, right_side):
    return lax.dot_general(left_side, right_side, (((1,), (1,)), ((), ())), preferred_element_type=f32)


def merged(ref):
    shape = ref.shape
    return ref[...].reshape(shape[0] * shape[1], shape[2])


def swap_halves(values, lane):
    up = pltpu.roll(values, 96, 1)
    down = pltpu.roll(values, 32, 1)
    return jnp.where(lane % 64 < 32, up, down)


def gelu_both(h):
    c = math.sqrt(2.0 / math.pi)
    h2 = h * h
    t = jnp.tanh(c * h * (1.0 + 0.044715 * h2))
    half = 0.5 * (1.0 + t)
    return h * half, half + 0.5 * h * (1.0 - t * t) * (c * (1.0 + 3.0 * 0.044715 * h2))


def normed(values):
    mean_val = jnp.mean(values, axis=-1, keepdims=True)
    centred = values - mean_val
    rstd = lax.rsqrt(jnp.mean(centred * centred, axis=-1, keepdims=True) + norm_eps)
    return centred * rstd, rstd


def norm_back(e, n, rstd):
    return (e - jnp.mean(e, axis=-1, keepdims=True) - n * jnp.mean(e * n, axis=-1, keepdims=True)) * rstd


class Links:
    def __init__(self, n, send, recv):
        self.n = n
        self.d = lax.axis_index("dp")
        self.s = lax.axis_index("seq")
        d, s = self.d, self.s
        self.px = d + 1 - 2 * (d % 2)
        self.s1 = s + 1 - 2 * (s % 2)
        self.s2 = (s + 2) % 4
        self.s3 = 3 - s
        self.send, self.recv = send, recv
        self.n_send = self.n_recv = 0

    def sems(self, sends, recvs):
        base = (self.n_send, self.n_recv)
        self.n_send += sends
        self.n_recv += recvs
        return base

    def block(self, i):
        s = self.s
        return (s % 2 + i % 2) % 2 + 2 * ((s // 2 + i // 2) % 2)

    def copy(self, src, dst, si, ri, dev):
        return pltpu.make_async_remote_copy(
            src_ref=src, dst_ref=dst, send_sem=self.send.at[si], recv_sem=self.recv.at[ri],
            device_id=dev, device_id_type=MESH,
        )

    def barrier(self):
        b = pltpu.get_barrier_semaphore()
        for k in range(1, self.n):
            pl.semaphore_signal(b, inc=1, device_id=((self.d + k) % self.n, self.s), device_id_type=MESH)
        for t in (self.s1, self.s2, self.s3):
            pl.semaphore_signal(b, inc=1, device_id=(self.d, t), device_id_type=MESH)
        pl.semaphore_wait(b, self.n + 2)


class ToAll:
    def __init__(self, links, src, buf):
        self.l, self.src, self.buf = links, src, buf
        self.si, self.ri = links.sems(links.n, links.n)

    def _to(self, k):
        l = self.l
        peer = (l.d + k) % l.n
        return l.copy(self.src(peer), self.buf.at[l.d], self.si + k, self.ri + l.d, (peer, l.s))

    def start(self):
        for k in range(1, self.l.n):
            self._to(k).start()

    def wait_recv(self):
        l = self.l
        for k in range(1, l.n):
            peer = (l.d + k) % l.n
            l.copy(self.buf.at[peer], self.buf.at[peer], self.si + k, self.ri + peer, (peer, l.s)).wait_recv()

    def wait_send(self):
        for k in range(1, self.l.n):
            self._to(k).wait_send()


class SeqAll:
    def __init__(self, links, buf):
        self.l, self.buf = links, buf
        self.si, self.ri = links.sems(4, 4)

    def _to(self, k):
        l = self.l
        t = l.block(k)
        return l.copy(self.buf.at[l.s], self.buf.at[l.s], self.si + k, self.ri + l.s, (l.d, t))

    def start(self):
        for k in (2, 3, 1):
            self._to(k).start()

    def wait_recv(self):
        l = self.l
        for k in (1, 2, 3):
            t = l.block(k)
            l.copy(self.buf.at[t], self.buf.at[t], self.si + k, self.ri + t, (l.d, t)).wait_recv()

    def wait_send(self):
        for k in (1, 2, 3):
            self._to(k).wait_send()


class DpGather:
    def __init__(self, links, buf):
        self.l, self.buf = links, buf
        self.si, self.ri = links.sems(links.n, links.n)
        self.half = links.n // 2

    def _z(self, k):
        l = self.l
        return l.copy(self.buf.at[l.d], self.buf.at[l.d], self.si + k, self.ri + l.d, ((l.d + 2 * k) % l.n, l.s))

    def _x(self, k):
        l = self.l
        r = (l.d + 2 * k) % l.n
        return l.copy(self.buf.at[r], self.buf.at[r], self.si + self.half + k, self.ri + r, (l.px, l.s))

    def start(self):
        for k in range(1, self.half):
            self._z(k).start()
        self._x(0).start()

    def hand_on(self):
        l = self.l
        for k in range(1, self.half):
            r = (l.d + 2 * k) % l.n
            l.copy(self.buf.at[r], self.buf.at[r], self.si, self.ri + r, (r, l.s)).wait_recv()
            self._x(k).start()

    def wait_rest(self):
        l = self.l
        for k in range(self.half):
            r = (l.px + 2 * k) % l.n
            l.copy(self.buf.at[r], self.buf.at[r], self.si, self.ri + r, (l.px, l.s)).wait_recv()

    def wait_send(self):
        for k in range(1, self.half):
            self._z(k).wait_send()
        for k in range(self.half):
            self._x(k).wait_send()


class SeqGather:
    def __init__(self, links, buf):
        self.l, self.buf = links, buf
        self.si, self.ri = links.sems(3, 4)

    def _c(self, slot, k, t):
        l = self.l
        return l.copy(self.buf.at[slot], self.buf.at[slot], self.si + k, self.ri + slot, (l.d, t))

    def start(self):
        l = self.l
        self._c(l.s, 0, l.s2).start()
        self._c(l.s, 1, l.s1).start()

    def hand_on(self):
        l = self.l
        self.wait(l.s2)
        self._c(l.s2, 2, l.s1).start()

    def wait(self, slot):
        l = self.l
        l.copy(self.buf.at[slot], self.buf.at[slot], self.si, self.ri + slot, (l.d, l.s1)).wait_recv()

    def wait_send(self):
        l = self.l
        self._c(l.s, 0, l.s2).wait_send()
        self._c(l.s, 1, l.s1).wait_send()
        self._c(l.s2, 2, l.s1).wait_send()


class SeqSwap:
    def __init__(self, links, out, into):
        self.l, self.out, self.into = links, out, into
        self.si, self.ri = links.sems(4, 4)

    def copy_to(self, i):
        l = self.l
        t = l.block(i)
        return l.copy(self.out.at[t], self.into.at[l.s], self.si + i, self.ri + l.s, (l.d, t))

    def wait_one(self, i):
        l = self.l
        t = l.block(i)
        l.copy(self.into.at[t], self.into.at[t], self.si + i, self.ri + t, (l.d, t)).wait_recv()

    def wait_recv(self):
        l = self.l
        for i in (1, 2, 3):
            t = l.block(i)
            l.copy(self.into.at[t], self.into.at[t], self.si + i, self.ri + t, (l.d, t)).wait_recv()

    def wait_send(self):
        for i in (1, 2, 3):
            self.copy_to(i).wait_send()


class SeqSum:
    def __init__(self, links, held):
        self.l, self.held = links, held
        self.si, self.ri = links.sems(3, 3)

    def _c(self, k, t):
        l = self.l
        return l.copy(self.held.at[k], self.held.at[3 + k], self.si + k, self.ri + k, (l.d, t))

    def far(self, term):
        l, held = self.l, self.held
        held[0] = term(l.s3).astype(bf16)
        self._c(0, l.s1).start()
        mine = term(l.s2)
        self._c(0, l.s1).wait_recv()
        held[1] = (mine + held[3].astype(f32)).astype(bf16)
        self._c(1, l.s2).start()

    def near(self, term):
        l = self.l
        self.held[2] = term(l.s1).astype(bf16)
        self._c(2, l.s1).start()

    def total(self, mine):
        l, held = self.l, self.held
        self._c(2, l.s1).wait_recv()
        self._c(1, l.s2).wait_recv()
        return mine + held[5].astype(f32) + held[4].astype(f32)

    def wait_send(self):
        l = self.l
        self._c(0, l.s1).wait_send()
        self._c(1, l.s2).wait_send()
        self._c(2, l.s1).wait_send()


def tn(left_side, right_side):
    return lax.dot_general(left_side, right_side, (((0,), (0,)), ((), ())), preferred_element_type=f32)


class SlotGather:
    def __init__(self, links, buf):
        self.l, self.buf = links, buf
        self.half = links.n // 2
        self.si, self.ri = links.sems(3 * links.n, 3 * links.n)

    def _c(self, block, r, kind, t):
        l = self.l
        at = kind * l.n + r
        return l.copy(self.buf.at[block, r], self.buf.at[block, r], self.si + at, self.ri + at, (l.d, t))

    def _each(self, base, body):
        def one(k, carry):
            body((base + 2 * k) % self.l.n)
            return carry

        lax.fori_loop(0, self.half, one, 0)

    def send(self, base):
        l = self.l

        def body(r):
            self._c(l.s, r, 0, l.s2).start()
            self._c(l.s, r, 1, l.s1).start()

        self._each(base, body)

    def hand_on(self, base):
        l = self.l

        def body(r):
            self._c(l.s2, r, 0, l.s2).wait_recv()
            self._c(l.s2, r, 2, l.s1).start()

        self._each(base, body)

    def wait_rest(self):
        l = self.l

        def one(r, carry):
            self._c(l.s1, r, 1, l.s1).wait_recv()
            self._c(l.s3, r, 2, l.s1).wait_recv()
            return carry

        lax.fori_loop(0, l.n, one, 0)

    def wait_send(self):
        l = self.l

        def one(r, carry):
            self._c(l.s, r, 0, l.s2).wait_send()
            self._c(l.s, r, 1, l.s1).wait_send()
            self._c(l.s2, r, 2, l.s1).wait_send()
            return carry

        lax.fori_loop(0, l.n, one, 0)


class DpSum:
    def __init__(self, links, g, xin, zin):
        self.l, self.g, self.xin, self.zin = links, g, xin, zin
        self.half = links.n // 2
        self.si, self.ri = links.sems(links.n, links.n)

    def _x(self, t):
        l = self.l
        h = t // 2
        return l.copy(self.g.at[t], self.xin.at[h], self.si + h, self.ri + h, (l.px, l.s))

    def _z(self, k):
        l = self.l
        t = (l.d + 2 * k) % l.n
        at = self.half + k
        return l.copy(self.g.at[t], self.zin.at[k], self.si + at, self.ri + at, (t, l.s))

    def send_x(self, first, count):
        for i in range(count // 2):
            self._x(first + 2 * i + self.l.px % 2).start()

    def fold(self):
        l = self.l

        def one(k, carry):
            t = (l.d + 2 * k) % l.n
            h = t // 2
            l.copy(self.xin.at[h], self.xin.at[h], self.si, self.ri + h, (l.px, l.s)).wait_recv()
            self.g[t] = (self.g[t].astype(f32) + self.xin[h].astype(f32)).astype(bf16)
            self._z(k).start()
            return carry

        lax.fori_loop(1, self.half, one, 0)

    def total(self):
        l = self.l
        h = l.d // 2
        l.copy(self.xin.at[h], self.xin.at[h], self.si, self.ri + h, (l.px, l.s)).wait_recv()
        out = self.g[l.d].astype(f32) + self.xin[h].astype(f32)
        for k in range(1, self.half):
            self._z(k).wait_recv()
            out = out + self.zin[k].astype(f32)
        return out

    def wait_send(self):
        l = self.l
        for k in range(self.half):
            self._x((l.px + 2 * k) % l.n).wait_send()
        for k in range(1, self.half):
            self._z(k).wait_send()


def whole_kernel(
    n,
    lengths, frames, cot, time_row, bm, bias, wu_own, wm_hbm, wq_hbm, wo_hbm, wd_hbm,
    block_out, grad_input, grad_time, tbuf, ebuf, lbuf, f_q0, f_q1, f_wo, f_wu, f_wd, f_b,
    wm, wq, wu, wd, wo, tsrc, psend, pbuf, bbuf, mod, n_in, attn_branch, n_mid, cos, sin, idc, idr,
    xa, dffn, xf, q, k, v, kt, vt, lse, ao_out, ao, do_out, gh, gelu, dhid, dattn, fsum, dk, dv, dproj,
    held, held_f, held_o, g_q0, x_q0, z_q0, g_q1, x_q1, z_q1, g_wo, x_wo, z_wo, g_wu, x_wu, z_wu, g_wd, x_wd, z_wd,
    em, lm, eb, ebb, lb, lbb, dts, dtb,
    send, recv, local,
):
    l = Links(n, send, recv)
    d, s = l.d, l.s
    rows, width = frames.shape
    item = 4 * rows
    quarter = width // 4
    own_rows = wm.shape[0]
    mq = bm.shape[1]
    units = wd.shape[1]
    ff_q = wu.shape[2]
    pairs = quarter // 128
    qw = 3 * quarter
    pw = qw // pairs
    lane = lax.broadcasted_iota(jnp.int32, (rows, 128), 1)
    take = [
        pltpu.make_async_copy(wm_hbm, wm, local.at[0]),
        pltpu.make_async_copy(wd_hbm.at[pl.ds(pl.multiple_of(s * units, 8), units), :], wd.at[d], local.at[1]),
        pltpu.make_async_copy(wo_hbm.at[:, pl.ds(pl.multiple_of(s * quarter, 128), quarter)], wo.at[s, d], local.at[2]),
    ] + [
        pltpu.make_async_copy(
            wq_hbm.at[:, pl.ds(pl.multiple_of(j * width + s * quarter + 128 * p, 128), 128)],
            wq.at[d, :, pl.ds(p * pw + 128 * j, 128)], local.at[3 + 3 * p + j],
        )
        for p in range(pairs) for j in range(3)
    ]
    for c in take:
        c.start()
    times = ToAll(l, lambda peer: tsrc.at[peer], tbuf)
    parts = ToAll(l, lambda peer: psend.at[peer], pbuf)
    biases = ToAll(l, lambda peer: bias.at[0], bbuf)
    mods = SeqAll(l, mod)
    a_wq, a_wu, a_wd, a_wo = DpGather(l, wq), DpGather(l, wu), DpGather(l, wd), DpGather(l, wo.at[s])
    s_xa, s_df, s_xf, s_wo = SeqGather(l, xa), SeqGather(l, dffn), SeqGather(l, xf), SlotGather(l, wo)
    w_ao, w_do = SeqSwap(l, ao_out, ao), SeqSwap(l, do_out, gh)
    sum_x, sum_f, sum_o, sum_a = SeqSum(l, held), SeqSum(l, held_f), SeqSum(l, held_o), SeqSum(l, held)
    d_q0, d_q1, d_wo, d_wu, d_wd = (
        DpSum(l, g_q0, x_q0, z_q0), DpSum(l, g_q1, x_q1, z_q1), DpSum(l, g_wo, x_wo, z_wo),
        DpSum(l, g_wu, x_wu, z_wu), DpSum(l, g_wd, x_wd, z_wd),
    )
    o_q0, o_q1, o_wo, o_wu, o_wd = (
        SeqGather(l, f_q0), SeqGather(l, f_q1), SeqGather(l, f_wo), SeqGather(l, f_wu), SeqGather(l, f_wd)
    )
    e_mod, l_mod, o_b = SeqAll(l, em), SeqAll(l, lm), SeqAll(l, f_b)
    e_all, l_all = ToAll(l, lambda peer: ebuf.at[d], ebuf), ToAll(l, lambda peer: lbuf.at[d], lbuf)
    eb_all, lb_all = ToAll(l, lambda peer: eb, ebb), ToAll(l, lambda peer: lb, lbb)
    t_all = ToAll(l, lambda peer: dts.at[peer], dtb)

    def at_rows(b):
        return pl.ds(pl.multiple_of(b * rows, rows), rows)

    tv = time_row[...]
    act = (tv / (1.0 + jnp.exp(-tv))).astype(bf16).astype(f32)
    for i in range(n):
        tsrc[i] = act[:, i * own_rows : (i + 1) * own_rows]
    dffn[s] = cot[...].astype(bf16)
    for c in take[3:]:
        c.wait()
    l.barrier()
    times.start()
    a_wq.start()
    s_df.start()
    biases.start()
    tbuf[d] = tsrc[d]
    wu[d] = wu_own[...]
    for c in take[:3]:
        c.wait()
    n_in[...] = normed(frames[...])[0]
    times.wait_recv()
    lhs = jnp.concatenate([tbuf[i] for i in range(n)], axis=0).astype(bf16)
    part = nn(lhs, wm[:, pl.ds(pl.multiple_of(s * mq, 128), mq)]) + bm[...]
    for i in range(n):
        psend[i] = part[i : i + 1]
    parts.start()
    total = psend[d]
    parts.wait_recv()
    for j in range(1, n):
        total = total + pbuf[(d + j) % n]
    mod[s] = total
    mods.start()
    mods.wait_recv()
    flat = jnp.concatenate([mod[i] for i in range(4)], axis=1)
    shift_a, scale_a, gate_a, shift_f, scale_f, gate_f = (
        flat[:, i * width : (i + 1) * width] for i in range(6)
    )
    xa[s] = (n_in[...] * (1.0 + scale_a) + shift_a).astype(bf16)
    s_xa.start()

    def places(shape, dim):
        at = lax.broadcasted_iota(jnp.int32, shape, dim)
        number, first, end = jnp.zeros(shape, jnp.int32), jnp.zeros(shape, jnp.int32), 0
        for c in range(lengths.shape[1] - 1):
            end = end + lengths[0, c]
            past = at >= end
            number = number + jnp.where(past, 1, 0)
            first = jnp.where(past, end, first)
        return number, at - first

    idr[...] = places((1, item), 1)[0]
    number, position = places((item, 1), 0)
    idc[...] = number
    lanes = lax.broadcasted_iota(jnp.int32, (1, 128), 1)
    rate = jnp.exp((lanes % 32).astype(f32) * (-2.0 * math.log(10000.0) / 64))
    phase = position.astype(f32) * rate
    cos[...] = jnp.cos(phase)
    sin[...] = jnp.where(lanes % 64 < 32, -1.0, 1.0) * jnp.sin(phase)

    a_wq.hand_on()
    a_wo.start()
    s_df.hand_on()
    a_wq.wait_rest()
    biases.wait_recv()
    own_bias = bias[0]
    for j in range(1, n):
        own_bias = own_bias + bbuf[(d + j) % n]
    bq = own_bias[:, :qw]
    bo = own_bias[:, qw : qw + width]
    bu = own_bias[:, qw + width : qw + width + ff_q]
    bd = own_bias[:, qw + width + ff_q :]

    def project(i, carry):
        @pl.when(i == 1)
        def _():
            s_xa.wait(l.s1)
            a_wu.start()

        @pl.when(i == 2)
        def _():
            s_xa.hand_on()
            a_wd.start()

        @pl.when(i == 3)
        def _():
            s_xa.wait(l.s3)

        b = l.block(i)
        at = at_rows(b)
        pr = nn(xa[b], merged(wq)) + bq
        cb, sb = cos[at, :], sin[at, :]
        for p in range(pairs):
            c0 = 128 * p
            qp, kp, vp = (pr[:, p * pw + 128 * j : p * pw + 128 * j + 128] for j in range(3))
            vp = vp.astype(bf16)
            qp = (qp * cb + swap_halves(qp, lane) * sb).astype(bf16)
            kp = (kp * cb + swap_halves(kp, lane) * sb).astype(bf16)
            q[at, c0 : c0 + 128] = qp * jnp.bfloat16(0.125)
            k[at, c0 : c0 + 128] = kp
            v[at, c0 : c0 + 128] = vp
            kt[p, :, at] = jnp.transpose(kp.astype(f32)).astype(bf16)
            vt[p, :, at] = jnp.transpose(vp.astype(f32)).astype(bf16)
        return carry

    lax.fori_loop(0, 4, project, 0)
    a_wo.hand_on()
    s_wo.send(d)

    def attend(j, carry):
        i = (j + 2) % 4
        b = l.block(i)
        at = at_rows(b)
        same = idc[...] == idr[:, at]
        for p in range(pairs):
            qp, kp = q[at, 128 * p : 128 * p + 128], k[:, 128 * p : 128 * p + 128]
            outs = []
            for h in range(2):
                qm = jnp.where((lane < 64) == (h == 0), qp, jnp.zeros_like(qp))
                sc = jnp.where(same, nt(kp, qm), -1e30)
                top = jnp.max(sc, axis=0, keepdims=True)
                ex = jnp.exp(sc - top)
                su = jnp.sum(ex, axis=0, keepdims=True)
                lse[2 * p + h, :, at] = top + jnp.log(su)
                pt = (ex * (1.0 / su)).astype(bf16)
                outs.append(nn(vt[p, 64 * h : 64 * h + 64, :], pt))
            ao_out[b, :, 128 * p : 128 * p + 128] = jnp.transpose(jnp.concatenate(outs, axis=0)).astype(bf16)

        @pl.when(j != 2)
        def _():
            w_ao.copy_to(i).start()

        @pl.when(j == 0)
        def _():
            a_wo.wait_rest()
            s_wo.send(l.px)

        @pl.when(j == 1)
        def _():
            s_wo.hand_on(d)

        @pl.when(j == 2)
        def _():
            ao[s] = ao_out[s]
            a_wu.hand_on()

        @pl.when(j == 3)
        def _():
            s_wo.hand_on(l.px)

        return carry

    lax.fori_loop(0, 4, attend, 0)
    s_wo.wait_rest()
    w_ao.wait_recv()
    left = jnp.concatenate([ao[i] for i in range(4)], axis=1)
    for c in range(4):
        cs = slice(c * quarter, (c + 1) * quarter)
        attn_branch[:, cs] = nn(left, merged(wo.at[c])) + bo[:, cs]
    xm = frames[...] + gate_a * attn_branch[...]
    block_out[...] = xm
    nm, rstd = normed(xm)
    n_mid[...] = nm
    xf[s] = (nm * (1.0 + scale_f) + shift_f).astype(bf16)
    s_xf.start()
    a_wd.hand_on()
    s_df.wait(l.s1)
    s_df.wait(l.s3)
    s_df.wait_send()
    for b in range(4):
        dffn[b] = (gate_f * dffn[b].astype(f32)).astype(bf16)
    a_wu.wait_rest()
    a_wd.wait_rest()

    def hidden_term(b):
        return nt(dhid[at_rows(b), :], merged(wu))

    def ffn_term(b):
        return nn(gelu[at_rows(b), :], merged(wd))

    def out_term(t):
        part = dattn[:, pl.ds(pl.multiple_of(t * quarter, 128), quarter)]
        return jnp.concatenate([tn(ao[i], part) for i in range(4)], axis=0)

    def xa_term(b):
        return nt(dproj[at_rows(b), :], merged(wq))

    def feed(i, carry):
        @pl.when(i == 1)
        def _():
            s_xf.wait(l.s1)

        @pl.when(i == 2)
        def _():
            sum_x.near(hidden_term)
            s_xf.hand_on()

        @pl.when(i == 3)
        def _():
            s_xf.wait(l.s3)

        b = l.block(i)
        at = at_rows(b)
        act, slope = gelu_both(nn(xf[b], merged(wu)) + bu)
        gelu[at, :] = act.astype(bf16)
        dhid[at, :] = (nt(dffn[b], merged(wd)) * slope).astype(bf16)
        return carry

    lax.fori_loop(0, 4, feed, 0)
    sum_x.far(hidden_term)

    def make(left_of, right, g, chain, each):
        per = 256 // each

        def one(m, carry):
            val = tn(left_of(m), right()).astype(bf16)
            g[pl.ds(m * per, per)] = val.reshape(per, each, val.shape[1])
            chain.send_x(m * per, per)
            return carry

        lax.fori_loop(0, n // per, one, 0)

    def cols_of(ref, m):
        return ref[:, :, pl.ds(pl.multiple_of(m * 256, 256), 256)].reshape(item, 256)

    make(lambda m: gelu[:, pl.ds(pl.multiple_of(m * 256, 256), 256)], lambda: merged(dffn), g_wd, d_wd, units)
    make(lambda m: cols_of(xf, m), lambda: dhid[...], g_wu, d_wu, own_rows)
    eb[:, :ff_q] = jnp.sum(dhid[...].astype(f32), axis=0, keepdims=True)
    eb[:, ff_q + width :] = jnp.sum(dffn[s].astype(f32), axis=0, keepdims=True)
    dk[...] = jnp.zeros_like(dk)
    dv[...] = jnp.zeros_like(dv)
    g = sum_x.total(hidden_term(s))
    nm = n_mid[...]
    fsum[0:1, :] = jnp.sum(g, axis=0, keepdims=True)
    fsum[1:2, :] = jnp.sum(g * nm, axis=0, keepdims=True)
    dm = cot[...] + norm_back(g * (1.0 + scale_f), nm, normed(block_out[...])[1])
    grad_input[...] = dm
    dattn[...] = (gate_a * dm).astype(bf16)
    per4 = n // 4

    def give(j, carry):
        i = (j + 2) % 4
        t = l.block(i)
        out = None
        for c in range(4):
            wt = wo[c, pl.ds(t * per4, per4)].reshape(quarter, quarter)
            o = nt(dattn[:, c * quarter : (c + 1) * quarter], wt)
            out = o if out is None else out + o
        do_out[t] = out.astype(bf16)

        @pl.when(j != 2)
        def _():
            w_do.copy_to(i).start()

        @pl.when(j == 2)
        def _():
            gh[s] = do_out[s]

        return carry

    lax.fori_loop(0, 4, give, 0)
    fsum[2:3, :] = jnp.sum(dm * attn_branch[...], axis=0, keepdims=True)
    eb[:, ff_q : ff_q + width] = jnp.sum(dattn[...].astype(f32), axis=0, keepdims=True)
    eb_all.start()

    def turned(values, at):
        val = values.astype(bf16).astype(f32)
        return (val * cos[at, :] - swap_halves(val, lane) * sin[at, :]).astype(bf16)

    def back_pair(p, before, after):
        c0, base = 128 * p, p * pw

        def one(i, carry):
            before(i)
            b = l.block(i)
            at = at_rows(b)
            same = idc[...] == idr[:, at]
            kp, vp = k[:, c0 : c0 + 128], v[:, c0 : c0 + 128]
            qp, dop = q[at, c0 : c0 + 128], gh[b, :, c0 : c0 + 128]
            dqs = []
            for h in range(2):
                mine = (lane < 64) == (h == 0)
                qm = jnp.where(mine, qp, jnp.zeros_like(qp))
                dom = jnp.where(mine, dop, jnp.zeros_like(dop))
                pt = jnp.exp(jnp.where(same, nt(kp, qm), -1e30) - lse[2 * p + h, :, at])
                dpt = nt(vp, dom)
                mean = jnp.sum(dpt * pt, axis=0, keepdims=True)
                dst = (pt * (dpt - mean)).astype(bf16)
                dv[p] += nn(pt.astype(bf16), dom)
                dk[p] += nn(dst, qm)
                dqs.append(nn(kt[p, 64 * h : 64 * h + 64, :], dst))
            dq = jnp.transpose(jnp.concatenate(dqs, axis=0)) * 0.125
            dproj[at, base : base + 128] = turned(dq, at)
            after(i)
            return carry

        lax.fori_loop(0, 4, one, 0)

        def finish(b, carry):
            at = at_rows(b)
            dproj[at, base + 128 : base + 256] = turned(dk[p, at, :], at)
            dproj[at, base + 256 : base + 384] = dv[p, at, :].astype(bf16)
            return carry

        lax.fori_loop(0, 4, finish, 0)

    def before0(i):
        @pl.when(i == 1)
        def _():
            w_do.wait_one(1)

        @pl.when(i == 2)
        def _():
            w_do.wait_one(2)

        @pl.when(i == 3)
        def _():
            w_do.wait_one(3)

    def after0(i):
        @pl.when(i == 0)
        def _():
            d_wd.fold()

        @pl.when(i == 2)
        def _():
            sum_f.far(ffn_term)
            sum_f.near(ffn_term)

        @pl.when(i == 3)
        def _():
            d_wu.fold()

    def after1(i):
        @pl.when(i == 0)
        def _():
            sum_o.far(out_term)
            sum_o.near(out_term)

        @pl.when(i == 2)
        def _():
            ffn = sum_f.total(ffn_term(s)) + bd
            block_out[...] = block_out[...] + gate_f * ffn
            em[s, :, 3 * width :] = jnp.sum(cot[...] * ffn, axis=0, keepdims=True)
            em[s, :, :width] = fsum[2:3, :]
            em[s, :, width : 2 * width] = fsum[0:1, :]
            em[s, :, 2 * width : 3 * width] = fsum[1:2, :]
            e_mod.start()

        @pl.when(i == 3)
        def _():
            e_mod.wait_recv()
            ebuf[d] = (em[0] + em[1] + em[2] + em[3]).astype(bf16).astype(f32)
            e_all.start()

    back_pair(0, before0, after0)
    make(lambda m: cols_of(xa, m), lambda: dproj[:, :pw], g_q0, d_q0, own_rows)
    back_pair(1, lambda i: None, after1)
    sum_x.wait_send()
    sum_a.far(xa_term)
    make(lambda m: cols_of(xa, m), lambda: dproj[:, pw:], g_q1, d_q1, own_rows)
    sum_a.near(xa_term)
    d_q0.fold()
    g_wo[...] = sum_o.total(out_term(s)).astype(bf16).reshape(n, own_rows, quarter)
    d_wo.send_x(0, n)
    lb[...] = jnp.sum(dproj[...].astype(f32), axis=0, keepdims=True)
    lb_all.start()
    e_all.wait_recv()
    dm_e = jnp.concatenate([ebuf[i] for i in range(n)], axis=0).astype(bf16)
    dt = nt(dm_e, wm[:, 2 * width :])
    d_q1.fold()
    d_wo.fold()
    g = sum_a.total(xa_term(s))
    n_val = n_in[...]
    lm[s, :, :width] = jnp.sum(g, axis=0, keepdims=True)
    lm[s, :, width:] = jnp.sum(g * n_val, axis=0, keepdims=True)
    l_mod.start()
    f_wd[s] = d_wd.total().astype(bf16)
    o_wd.start()
    f_wu[s] = d_wu.total().astype(bf16)
    o_wu.start()
    grad_input[...] = grad_input[...] + norm_back(g * (1.0 + scale_a), n_val, normed(frames[...])[1])
    l_mod.wait_recv()
    lbuf[d] = (lm[0] + lm[1] + lm[2] + lm[3]).astype(bf16).astype(f32)
    l_all.start()
    eb_all.wait_recv()
    lb_all.wait_recv()
    esum, lsum = eb[...], lb[...]
    for j in range(1, n):
        esum = esum + ebb[(d + j) % n]
        lsum = lsum + lbb[(d + j) % n]
    f_b[s, :, :qw] = lsum
    f_b[s, :, qw:] = esum
    o_b.start()
    f_q0[s] = d_q0.total().astype(bf16)
    o_q0.start()
    l_all.wait_recv()
    dm_l = jnp.concatenate([lbuf[i] for i in range(n)], axis=0).astype(bf16)
    dt = dt + nt(dm_l, wm[:, : 2 * width])
    for i in range(n):
        dts[i] = dt[i : i + 1]
    t_all.start()
    f_wo[s] = d_wo.total().astype(bf16)
    o_wo.start()
    o_wd.hand_on()
    o_wu.hand_on()
    f_q1[s] = d_q1.total().astype(bf16)
    o_q1.start()
    o_q0.hand_on()
    o_wo.hand_on()
    t_all.wait_recv()
    dtb[d] = dts[d]
    sig = 1.0 / (1.0 + jnp.exp(-tv))
    slope = sig + tv * sig * (1.0 - sig)
    for i in range(n):
        at = slice(i * own_rows, (i + 1) * own_rows)
        grad_time[:, at] = dtb[i] * slope[:, at]
    o_q1.hand_on()
    for o in (o_q0, o_q1, o_wo, o_wu, o_wd):
        o.wait(l.s1)
        o.wait(l.s3)
    o_b.wait_recv()
    for c in (
        times, parts, biases, mods, a_wq, a_wu, a_wd, a_wo, s_xa, s_xf, s_wo, w_ao, w_do,
        sum_f, sum_o, sum_a, d_q0, d_q1, d_wo, d_wu, d_wd, o_q0, o_q1, o_wo, o_wu, o_wd, e_mod, l_mod, o_b,
        e_all, l_all, eb_all, lb_all, t_all,
    ):
        c.wait_send()


def run_whole(n, clip_len, frames, cot, time_embed, bm, bias, wu_own, w_mod, w_qkv, w_out, w_down):
    rows, width = frames.shape
    item, quarter, own_rows = 4 * rows, width // 4, width // n
    ff_q = w_down.shape[0] * n // 4
    units, heads, pairs = ff_q // n, quarter // 64, quarter // 128
    qw = 3 * quarter
    pw = qw // pairs
    S, V = jax.ShapeDtypeStruct, pltpu.VMEM
    bw = qw + ff_q + 2 * width
    outs = [
        S((rows, width), f32), S((rows, width), f32), S((1, width), f32), S((n, 1, own_rows), f32),
        S((n, 1, 4 * width), f32), S((n, 1, 2 * width), f32), S((4, own_rows, pw), bf16), S((4, own_rows, pw), bf16),
        S((4, own_rows, quarter), bf16), S((4, own_rows, ff_q), bf16), S((4, units, width), bf16), S((4, 1, bw), f32),
    ]

    def chain(a, b):
        return [V((n, a, b), bf16), V((n // 2, a, b), bf16), V((n // 2, a, b), bf16)]

    held = V((6, rows, width), bf16)
    scratch = (
        [
            V((own_rows, 6 * width), bf16), V((n, own_rows, qw), bf16), V((n, own_rows, ff_q), bf16), V((n, units, width), bf16),
            V((4, n, own_rows, quarter), bf16), V((n, 1, own_rows), f32), V((n, 1, 6 * quarter), f32),
            V((n, 1, 6 * quarter), f32), V((n, 1, bw), f32), V((4, 1, 6 * quarter), f32),
            V((rows, width), f32), V((rows, width), f32), V((rows, width), f32), V((item, 128), f32), V((item, 128), f32),
            V((item, 1), jnp.int32), V((1, item), jnp.int32),
            V((4, rows, width), bf16), V((4, rows, width), bf16), V((4, rows, width), bf16),
            V((item, quarter), bf16), V((item, quarter), bf16), V((item, quarter), bf16),
            V((pairs, 128, item), bf16), V((pairs, 128, item), bf16), V((heads, 1, item), f32),
        ]
        + [V((4, rows, quarter), bf16)] * 4
        + [
            V((item, ff_q), bf16), V((item, ff_q), bf16), V((rows, width), bf16), V((8, width), f32),
            V((pairs, item, 128), f32), V((pairs, item, 128), f32), V((item, qw), bf16),
            held, held, V((6, width, quarter), bf16),
        ]
        + chain(own_rows, pw) + chain(own_rows, pw) + chain(own_rows, quarter) + chain(own_rows, ff_q) + chain(units, width)
        + [
            V((4, 1, 4 * width), f32), V((4, 1, 2 * width), f32), V((1, ff_q + 2 * width), f32),
            V((n, 1, ff_q + 2 * width), f32), V((1, qw), f32), V((n, 1, qw), f32),
            V((n, 1, own_rows), f32), V((n, 1, own_rows), f32),
            pltpu.SemaphoreType.DMA((20 * n + 80,)), pltpu.SemaphoreType.DMA((20 * n + 90,)), pltpu.SemaphoreType.DMA((9,)),
        ]
    )
    vm = pl.BlockSpec(memory_space=pltpu.VMEM)
    hb = pl.BlockSpec(memory_space=pl.ANY)
    return pl.pallas_call(
        functools.partial(whole_kernel, n),
        out_shape=outs,
        in_specs=[pl.BlockSpec(memory_space=pltpu.SMEM)] + [vm] * 6 + [hb] * 4,
        out_specs=[vm] * len(outs),
        scratch_shapes=scratch,
        compiler_params=pltpu.CompilerParams(collective_id=0, has_side_effects=True, vmem_limit_bytes=63 << 20),
    )(clip_len, frames, cot, time_embed, bm, bias, wu_own, w_mod, w_qkv, w_out, w_down)


def per_device(
    frames, time_embed, clip_len, w_qkv, b_qkv, w_out, b_out, w_up, b_up, w_down, b_down, w_mod, b_mod, cotangent
):
    n = lax.axis_size("dp")
    seq_rank, dp_rank = lax.axis_index("seq"), lax.axis_index("dp")
    rows, width = frames.shape
    quarter = width // 4
    own_rows, ff = w_up.shape
    units = w_down.shape[0] // 4
    pairs = quarter // 128
    ff_q = ff // 4
    qw = 3 * quarter

    def placed(b):
        return lax.dynamic_update_slice(
            jnp.zeros((b.shape[0] * n,), f32), b.astype(f32), (dp_rank * b.shape[0],)
        )

    def mine(value, axis):
        return lax.dynamic_index_in_dim(value, seq_rank, axis, keepdims=False)

    bm = mine(placed(b_mod).reshape(4, 6 * quarter), 0)[None]
    bias = jnp.concatenate(
        [
            mine(placed(b_qkv).reshape(3, 4, pairs, 128), 1).transpose(1, 0, 2).reshape(-1),
            placed(b_out),
            mine(placed(b_up).reshape(n, 4, units), 1).reshape(-1),
            placed(b_down),
        ]
    ).reshape(1, 1, -1)
    wu_own = mine(w_up.reshape(own_rows, n, 4, units), 2).reshape(own_rows, ff_q)
    block_out, grad_input, grad_time, tbuf, ebuf, lbuf, f_q0, f_q1, f_wo, f_wu, f_wd, f_b = run_whole(
        n, clip_len, frames, cotangent, time_embed, bm, bias, wu_own, w_mod, w_qkv, w_out, w_down
    )
    f_wq = jnp.stack([f_q0, f_q1], axis=2).astype(f32).reshape(4, own_rows, pairs, 3, 128)
    s_wq = f_wq.transpose(1, 3, 0, 2, 4).reshape(own_rows, 3 * width)
    s_wo = f_wo.astype(f32).transpose(1, 0, 2).reshape(own_rows, width)
    s_wu = f_wu.astype(f32).reshape(4, own_rows, n, units).transpose(1, 2, 0, 3).reshape(own_rows, ff)
    s_wd = f_wd.astype(f32).reshape(4 * units, width)
    d_mod = jnp.concatenate([lbuf[:, 0], ebuf[:, 0]], axis=1)
    gwm = tn(tbuf[:, 0].astype(bf16), d_mod.astype(bf16))
    gbm = jnp.sum(d_mod, axis=0)
    bq = f_b[:, 0, :qw].reshape(4, pairs, 3, 128).transpose(2, 0, 1, 3).reshape(-1)
    bu = f_b[:, 0, qw : qw + ff_q].reshape(4, n, units).transpose(1, 0, 2).reshape(-1)
    bo = jnp.sum(f_b[:, 0, qw + ff_q : qw + ff_q + width], axis=0)
    bd = jnp.sum(f_b[:, 0, qw + ff_q + width :], axis=0)

    def own(value, like):
        size = like.shape[0]
        return lax.dynamic_slice_in_dim(value, dp_rank * size, size, 0)

    return (
        block_out, grad_input, grad_time, s_wq, own(bq, b_qkv), s_wo, own(bo, b_out), s_wu,
        own(bu, b_up), s_wd, own(bd, b_down), gwm, own(gbm, b_mod),
    )


def solution(mesh):
    placed = (
        P(("dp", "seq"), None),
        P("dp", None),
        P("dp", None),
        P("dp", None),
        P("dp"),
        P("dp", None),
        P("dp"),
        P("dp", None),
        P("dp"),
        P("dp", None),
        P("dp"),
        P("dp", None),
        P("dp"),
        P(("dp", "seq"), None),
    )
    return jax.shard_map(
        per_device,
        mesh=mesh,
        in_specs=placed,
        out_specs=(
            P(("dp", "seq"), None),
            P(("dp", "seq"), None),
            P("dp", None),
            P("dp", None),
            P("dp"),
            P("dp", None),
            P("dp"),
            P("dp", None),
            P("dp"),
            P("dp", None),
            P("dp"),
            P("dp", None),
            P("dp"),
        ),
        check_vma=False,
    )
```

```python
import functools
import math

import jax
import jax.numpy as jnp
from jax import lax
from jax.experimental import pallas as pl
from jax.experimental.pallas import tpu as pltpu
from jax.sharding import PartitionSpec as P

HEADS = 16
MESH = pl.DeviceIdType.MESH
f32 = jnp.float32
bf16 = jnp.bfloat16
norm_eps = 1e-06


def nn(left_side, right_side):
    return lax.dot_general(left_side, right_side, (((1,), (0,)), ((), ())), preferred_element_type=f32)


def nt(left_side, right_side):
    return lax.dot_general(left_side, right_side, (((1,), (1,)), ((), ())), preferred_element_type=f32)


def merged(ref):
    shape = ref.shape
    return ref[...].reshape(shape[0] * shape[1], shape[2])


def swap_halves(values, lane):
    up = pltpu.roll(values, 96, 1)
    down = pltpu.roll(values, 32, 1)
    return jnp.where(lane % 64 < 32, up, down)


def gelu_both(h):
    c = math.sqrt(2.0 / math.pi)
    h2 = h * h
    t = jnp.tanh(c * h * (1.0 + 0.044715 * h2))
    half = 0.5 * (1.0 + t)
    return h * half, half + 0.5 * h * (1.0 - t * t) * (c * (1.0 + 3.0 * 0.044715 * h2))


def normed(values):
    mean_val = jnp.mean(values, axis=-1, keepdims=True)
    centred = values - mean_val
    rstd = lax.rsqrt(jnp.mean(centred * centred, axis=-1, keepdims=True) + norm_eps)
    return centred * rstd, rstd


def norm_back(e, n, rstd):
    return (e - jnp.mean(e, axis=-1, keepdims=True) - n * jnp.mean(e * n, axis=-1, keepdims=True)) * rstd


class Links:
    def __init__(self, n, send, recv):
        self.n = n
        self.d = lax.axis_index("dp")
        self.s = lax.axis_index("seq")
        d, s = self.d, self.s
        self.px = d + 1 - 2 * (d % 2)
        self.s1 = s + 1 - 2 * (s % 2)
        self.s2 = (s + 2) % 4
        self.s3 = 3 - s
        self.send, self.recv = send, recv
        self.n_send = self.n_recv = 0

    def sems(self, sends, recvs):
        base = (self.n_send, self.n_recv)
        self.n_send += sends
        self.n_recv += recvs
        return base

    def block(self, i):
        s = self.s
        return (s % 2 + i % 2) % 2 + 2 * ((s // 2 + i // 2) % 2)

    def copy(self, src, dst, si, ri, dev):
        return pltpu.make_async_remote_copy(
            src_ref=src, dst_ref=dst, send_sem=self.send.at[si], recv_sem=self.recv.at[ri],
            device_id=dev, device_id_type=MESH,
        )

    def barrier(self):
        b = pltpu.get_barrier_semaphore()
        for k in range(1, self.n):
            pl.semaphore_signal(b, inc=1, device_id=((self.d + k) % self.n, self.s), device_id_type=MESH)
        for t in (self.s1, self.s2, self.s3):
            pl.semaphore_signal(b, inc=1, device_id=(self.d, t), device_id_type=MESH)
        pl.semaphore_wait(b, self.n + 2)


class ToAll:
    def __init__(self, links, src, buf, cols=None):
        self.l, self.src, self.buf, self.cols = links, src, buf, cols
        self.si, self.ri = links.sems(links.n, links.n)

    def _at(self, slot):
        return self.buf.at[slot] if self.cols is None else self.buf.at[slot, :, self.cols]

    def _to(self, k):
        l = self.l
        peer = (l.d + k) % l.n
        src = self._at(l.d) if self.src is None else self.src(peer)
        return l.copy(src, self._at(l.d), self.si + k, self.ri + l.d, (peer, l.s))

    def start(self):
        for k in range(1, self.l.n):
            self._to(k).start()

    def wait_recv(self):
        l = self.l
        for k in range(1, l.n):
            peer = (l.d + k) % l.n
            l.copy(self._at(peer), self._at(peer), self.si + k, self.ri + peer, (peer, l.s)).wait_recv()

    def wait_send(self):
        for k in range(1, self.l.n):
            self._to(k).wait_send()


class SeqAll:
    def __init__(self, links, buf):
        self.l, self.buf = links, buf
        self.si, self.ri = links.sems(4, 4)

    def _to(self, k):
        l = self.l
        t = l.block(k)
        return l.copy(self.buf.at[l.s], self.buf.at[l.s], self.si + k, self.ri + l.s, (l.d, t))

    def start(self):
        for k in (2, 3, 1):
            self._to(k).start()

    def wait_recv(self):
        l = self.l
        for k in (1, 2, 3):
            t = l.block(k)
            l.copy(self.buf.at[t], self.buf.at[t], self.si + k, self.ri + t, (l.d, t)).wait_recv()

    def wait_send(self):
        for k in (1, 2, 3):
            self._to(k).wait_send()


class DpGather:
    def __init__(self, links, buf):
        self.l, self.buf = links, buf
        self.si, self.ri = links.sems(links.n, links.n)
        self.half = links.n // 2

    def _z(self, k):
        l = self.l
        return l.copy(self.buf.at[l.d], self.buf.at[l.d], self.si + k, self.ri + l.d, ((l.d + 2 * k) % l.n, l.s))

    def _x(self, k):
        l = self.l
        r = (l.d + 2 * k) % l.n
        return l.copy(self.buf.at[r], self.buf.at[r], self.si + self.half + k, self.ri + r, (l.px, l.s))

    def start(self):
        for k in range(1, self.half):
            self._z(k).start()
        self._x(0).start()

    def hand_on(self):
        l = self.l
        for k in range(1, self.half):
            r = (l.d + 2 * k) % l.n
            l.copy(self.buf.at[r], self.buf.at[r], self.si, self.ri + r, (r, l.s)).wait_recv()
            self._x(k).start()

    def wait_rest(self):
        l = self.l
        for k in range(self.half):
            r = (l.px + 2 * k) % l.n
            l.copy(self.buf.at[r], self.buf.at[r], self.si, self.ri + r, (l.px, l.s)).wait_recv()

    def wait_send(self):
        for k in range(1, self.half):
            self._z(k).wait_send()
        for k in range(self.half):
            self._x(k).wait_send()


class SeqGather:
    def __init__(self, links, buf, rows=None):
        self.l, self.buf, self.rows = links, buf, rows
        self.si, self.ri = links.sems(3, 4)

    def _at(self, slot):
        return self.buf.at[slot] if self.rows is None else self.buf.at[slot, self.rows]

    def _c(self, slot, k, t):
        l = self.l
        return l.copy(self._at(slot), self._at(slot), self.si + k, self.ri + slot, (l.d, t))

    def start(self):
        l = self.l
        self._c(l.s, 0, l.s2).start()
        self._c(l.s, 1, l.s1).start()

    def hand_on(self):
        l = self.l
        self.wait(l.s2)
        self._c(l.s2, 2, l.s1).start()

    def wait(self, slot):
        self._c(slot, 0, self.l.s1).wait_recv()

    def wait_send(self):
        l = self.l
        self._c(l.s, 0, l.s2).wait_send()
        self._c(l.s, 1, l.s1).wait_send()
        self._c(l.s2, 2, l.s1).wait_send()


class SeqSwap:
    def __init__(self, links, out, into):
        self.l, self.out, self.into = links, out, into
        self.si, self.ri = links.sems(4, 4)

    def copy_to(self, i):
        l = self.l
        t = l.block(i)
        return l.copy(self.out.at[t], self.into.at[l.s], self.si + i, self.ri + l.s, (l.d, t))

    def wait_one(self, i):
        l = self.l
        t = l.block(i)
        l.copy(self.into.at[t], self.into.at[t], self.si + i, self.ri + t, (l.d, t)).wait_recv()

    def wait_recv(self):
        l = self.l
        for i in (1, 2, 3):
            t = l.block(i)
            l.copy(self.into.at[t], self.into.at[t], self.si + i, self.ri + t, (l.d, t)).wait_recv()

    def wait_send(self):
        for i in (1, 2, 3):
            self.copy_to(i).wait_send()


class SeqSum:
    def __init__(self, links, held):
        self.l, self.held = links, held
        self.rows = held.shape[1]
        self.si, self.ri = links.sems(5, 5)

    def _c(self, k, h, t):
        l = self.l
        half = self.rows // 2
        at = slice(None) if k == 2 else slice(h * half, (h + 1) * half)
        sem = 4 if k == 2 else 2 * k + h
        return l.copy(self.held.at[k, at], self.held.at[3 + k, at], self.si + sem, self.ri + sem, (l.d, t))

    def _part(self, b, h):
        half = self.rows // 2
        return pl.ds(pl.multiple_of(b * self.rows + h * half, half), half)

    def far(self, term, cross=True):
        l, held, half = self.l, self.held, self.rows // 2
        for h in range(2):
            held[0, h * half : (h + 1) * half] = term(self._part(l.s3, h)).astype(bf16)
            self._c(0, h, l.s1).start()
        for h in range(2):
            at = slice(h * half, (h + 1) * half)
            mine = term(self._part(l.s2, h))
            self._c(0, h, l.s1).wait_recv()
            held[1, at] = (mine + held[3, at].astype(f32)).astype(bf16)
            if cross:
                self._c(1, h, l.s2).start()

    def cross(self):
        for h in range(2):
            self._c(1, h, self.l.s2).start()

    def near(self, term):
        l = self.l
        self.held[2] = term(pl.ds(pl.multiple_of(l.s1 * self.rows, self.rows), self.rows)).astype(bf16)
        self._c(2, 0, l.s1).start()

    def total(self, term):
        l, held = self.l, self.held
        mine = term(pl.ds(pl.multiple_of(l.s * self.rows, self.rows), self.rows))
        self._c(2, 0, l.s1).wait_recv()
        for h in range(2):
            self._c(1, h, l.s2).wait_recv()
        return mine + held[5].astype(f32) + held[4].astype(f32)

    def wait_send(self):
        l = self.l
        for h in range(2):
            self._c(0, h, l.s1).wait_send()
            self._c(1, h, l.s2).wait_send()
        self._c(2, 0, l.s1).wait_send()


def half_of_each(one, two, odd):
    lane = lax.broadcasted_iota(jnp.int32, one.shape, 1)
    low = jnp.where(odd, pltpu.roll(one, 64, 1), one)
    high = jnp.where(odd, two, pltpu.roll(two, 64, 1))
    return jnp.where(lane < 64, low, high)


def tn(left_side, right_side):
    return lax.dot_general(left_side, right_side, (((0,), (0,)), ((), ())), preferred_element_type=f32)


class SlotGather:
    def __init__(self, links, buf):
        self.l, self.buf = links, buf
        self.half = links.n // 2
        self.si, self.ri = links.sems(3 * links.n, 3 * links.n)

    def _c(self, block, r, kind, t):
        l = self.l
        at = kind * l.n + r
        return l.copy(self.buf.at[block, r], self.buf.at[block, r], self.si + at, self.ri + at, (l.d, t))

    def _each(self, base, body):
        def one(k, carry):
            body((base + 2 * k) % self.l.n)
            return carry

        lax.fori_loop(0, self.half, one, 0)

    def send(self, base):
        l = self.l

        def body(r):
            self._c(l.s, r, 0, l.s2).start()
            self._c(l.s, r, 1, l.s1).start()

        self._each(base, body)

    def hand_on(self, base):
        l = self.l

        def body(r):
            self._c(l.s2, r, 0, l.s2).wait_recv()
            self._c(l.s2, r, 2, l.s1).start()

        self._each(base, body)

    def wait_rest(self):
        l = self.l

        def one(r, carry):
            self._c(l.s1, r, 1, l.s1).wait_recv()
            self._c(l.s3, r, 2, l.s1).wait_recv()
            return carry

        lax.fori_loop(0, l.n, one, 0)

    def wait_send(self):
        l = self.l

        def one(r, carry):
            self._c(l.s, r, 0, l.s2).wait_send()
            self._c(l.s, r, 1, l.s1).wait_send()
            self._c(l.s2, r, 2, l.s1).wait_send()
            return carry

        lax.fori_loop(0, l.n, one, 0)


class One:
    def __init__(self, links, src, dst, to):
        self.l, self.src, self.dst, self.to = links, src, dst, to
        self.si, self.ri = links.sems(1, 1)

    def _c(self):
        return self.l.copy(self.src, self.dst, self.si, self.ri, (self.l.d, self.to))

    def start(self):
        self._c().start()

    def wait_recv(self):
        self._c().wait_recv()

    def wait_send(self):
        self._c().wait_send()


class DpSum:
    def __init__(self, links, g, xin, zin):
        self.l, self.g, self.xin, self.zin = links, g, xin, zin
        self.half = links.n // 2
        self.si, self.ri = links.sems(links.n, links.n)

    def _x(self, t):
        l = self.l
        h = t // 2
        return l.copy(self.g.at[t], self.xin.at[h], self.si + h, self.ri + h, (l.px, l.s))

    def _z(self, k):
        l = self.l
        t = (l.d + 2 * k) % l.n
        at = self.half + k
        return l.copy(self.g.at[t], self.zin.at[k - 1], self.si + at, self.ri + at, (t, l.s))

    def send_x(self, first, count):
        for i in range(count // 2):
            self._x(first + 2 * i + self.l.px % 2).start()

    def fold(self):
        l = self.l

        def one(k, carry):
            t = (l.d + 2 * k) % l.n
            h = t // 2
            l.copy(self.xin.at[h], self.xin.at[h], self.si, self.ri + h, (l.px, l.s)).wait_recv()
            self.g[t] = (self.g[t].astype(f32) + self.xin[h].astype(f32)).astype(bf16)
            self._z(k).start()
            return carry

        lax.fori_loop(1, self.half, one, 0)

    def total(self):
        l = self.l
        h = l.d // 2
        l.copy(self.xin.at[h], self.xin.at[h], self.si, self.ri + h, (l.px, l.s)).wait_recv()
        out = self.g[l.d].astype(f32) + self.xin[h].astype(f32)
        for k in range(1, self.half):
            self._z(k).wait_recv()
            out = out + self.zin[k - 1].astype(f32)
        return out

    def wait_send(self):
        l = self.l
        for k in range(self.half):
            self._x((l.px + 2 * k) % l.n).wait_send()
        for k in range(1, self.half):
            self._z(k).wait_send()


def whole_kernel(
    n, plain,
    lengths, time_row, bias, b1, b2, b3, b4, b5, wu_own, frames_hbm, cot_hbm, wm_hbm, wq_hbm, wo_hbm, wd_hbm,
    grad_time, tmat, dmat, f_wu, bias_out, o_bq, o_bo, o_bd, o_bu, o_bm, out_hbm, grad_hbm, gwq_hbm, gwo_hbm, gwu_hbm, gwd_hbm,
    tbuf, dmb, frames, cot, block_out, grad_input, bmv, wu_raw, f_b, wm, wq0, wq1, wu, wd, wo, tsrc, psend, pbuf, psend2, pbuf2, bbuf, mod, n_in, attn_branch, n_mid, cos, sin, idc, idr,
    xa, dffn, xf, q, k, v, kt, vt, lse, ao_out, ao, gh, gelu, dhid, dattn, fsum, dk, dv, dproj,
    f_q0, f_q1, f_wo, f_wd, held, held_f, ho, fo, g_q0, x_q0, z_q0, g_q1, x_q1, z_q1, g_wo, x_wo, z_wo, g_wu, x_wu, z_wu, g_wd, x_wd, z_wd,
    em, lm, eb, ebb, lb, lbb, dts, dtb,
    send, recv, local, gone,
):
    l = Links(n, send, recv)
    d, s = l.d, l.s
    rows, width = frames.shape
    item = 4 * rows
    quarter = width // 4
    own_rows = wm.shape[0]
    units = wd.shape[1]
    ff_q = wu.shape[2]
    pairs = quarter // 128
    qw = 3 * quarter
    pw = qw // pairs
    lane = lax.broadcasted_iota(jnp.int32, (rows, 128), 1)
    take = [
        pltpu.make_async_copy(wm_hbm, wm, local.at[0]),
        pltpu.make_async_copy(wd_hbm.at[pl.ds(pl.multiple_of(s * units, 8), units), :], wd.at[d], local.at[1]),
        pltpu.make_async_copy(wo_hbm.at[:, pl.ds(pl.multiple_of(s * quarter, 128), quarter)], wo.at[s, d], local.at[2]),
    ] + [
        pltpu.make_async_copy(
            wq_hbm.at[:, pl.ds(pl.multiple_of(j * width + s * quarter + 128 * p, 128), 128)],
            (wq0, wq1)[p].at[d, :, pl.ds(128 * j, 128)], local.at[3 + 3 * p + j],
        )
        for p in range(pairs) for j in range(3)
    ]
    first = [
        pltpu.make_async_copy(frames_hbm, frames, local.at[9]),
        pltpu.make_async_copy(cot_hbm, cot, local.at[10]),
    ]
    if not plain:
        wide = pl.multiple_of(s // 2 * 128, 128)
        take_wu = [
            pltpu.make_async_copy(wu_own.at[:, pl.ds(i * 4 * units + wide, 128)], wu_raw.at[i], local.at[11 + i])
            for i in range(n)
        ]
    for c in first + take:
        c.start()
    times = ToAll(l, lambda peer: tsrc.at[peer], tbuf)
    parts, parts2 = ToAll(l, lambda peer: psend.at[peer], pbuf), ToAll(l, lambda peer: psend2.at[peer], pbuf2)
    wide_b = bbuf.shape[2]
    biases = ToAll(l, None, bbuf)
    mods = SeqAll(l, mod)
    a_q0, a_q1, a_wu, a_wd, a_wo = DpGather(l, wq0), DpGather(l, wq1), DpGather(l, wu), DpGather(l, wd), DpGather(l, wo.at[s])
    s_wo = SlotGather(l, wo)
    s_a0, s_a1 = (SeqGather(l, xa, pl.ds(h * (rows // 2), rows // 2)) for h in range(2))
    s_x0, s_x1 = (SeqGather(l, xf, pl.ds(h * (rows // 2), rows // 2)) for h in range(2))
    s_d0, s_d1 = (SeqGather(l, dffn, pl.ds(h * (rows // 2), rows // 2)) for h in range(2))
    w_ao, w_do = SeqSwap(l, ao_out, ao), SeqSwap(l, ao_out, gh)
    sum_x, sum_f, sum_a = SeqSum(l, held), SeqSum(l, held_f), SeqSum(l, held)
    d_q0, d_q1, d_wo, d_wu, d_wd = (
        DpSum(l, g_q0, x_q0, z_q0), DpSum(l, g_q1, x_q1, z_q1), DpSum(l, g_wo, x_wo, z_wo),
        DpSum(l, g_wu, x_wu, z_wu), DpSum(l, g_wd, x_wd, z_wd),
    )
    o_q0, o_q1, o_wu, o_wd = (
        SeqGather(l, f_q0), SeqGather(l, f_q1), SeqGather(l, f_wu), SeqGather(l, f_wd)
    )
    core = s % 2
    c_wo, y_wo = One(l, ho.at[0], ho.at[1], l.s1), One(l, fo.at[0], fo.at[1], l.s2)
    o_wo = One(l, f_wo.at[core], f_wo.at[core], l.s1)
    e_mod, l_mod, o_b = SeqAll(l, em), SeqAll(l, lm), SeqAll(l, f_b)
    e_all, l_all = ToAll(l, None, dmb, slice(2 * width, 6 * width)), ToAll(l, None, dmb, slice(0, 2 * width))
    eb_all, lb_all = ToAll(l, lambda peer: eb, ebb), ToAll(l, lambda peer: lb, lbb)
    t_all = ToAll(l, lambda peer: dts.at[peer], dtb)

    def at_rows(b):
        return pl.ds(pl.multiple_of(b * rows, rows), rows)

    if plain:
        bbuf[d] = bias[0, :, :wide_b]
        own_mod = bias[0, :, wide_b:]
    else:
        bbuf[d] = jnp.concatenate([b[...].astype(f32) for b in (b1, b2, b3, b4)], axis=1)
        own_mod = b5[...].astype(f32)
    if plain:
        bmv[...] = own_mod
    else:
        bmv[...] = jnp.concatenate([jnp.where(d == i, own_mod, jnp.zeros_like(own_mod)) for i in range(n)], axis=1)
    tv = time_row[...]
    act = (tv / (1.0 + jnp.exp(-tv))).astype(bf16).astype(f32)
    for i in range(n):
        tsrc[i] = act[:, i * own_rows : (i + 1) * own_rows]
    for c in first:
        c.wait()
    n_in[...] = normed(frames[...])[0]
    dffn[s] = cot[...].astype(bf16)
    for c in take[3:]:
        c.wait()
    l.barrier()
    times.start()
    a_q0.start()
    s_d0.start()
    biases.start()
    tbuf[d] = tsrc[d]
    if plain:
        wu_copy = pltpu.make_async_copy(wu_own, wu.at[d], local.at[11])
        wu_copy.start()
        wu_copy.wait()
    else:
        for c in take_wu:
            c.start()
    for c in take[:3]:
        c.wait()
    times.wait_recv()
    lhs = jnp.concatenate([tbuf[i] for i in range(n)], axis=0).astype(bf16)
    tmat[...] = lhs
    part = nn(lhs, wm[:, : 2 * width]) + bmv[:, : 2 * width]
    for i in range(n):
        psend[i] = part[i : i + 1]
    parts.start()
    part = nn(lhs, wm[:, pl.ds(pl.multiple_of((2 + s) * width, 128), width)]) + bmv[:, pl.ds(pl.multiple_of((2 + s) * width, 128), width)]
    for i in range(n):
        psend2[i] = part[i : i + 1]
    total = psend[d]
    parts.wait_recv()
    for j in range(1, n):
        total = total + pbuf[(d + j) % n]
    shift_a, scale_a = total[:, :width], total[:, width:]
    xa[s] = (n_in[...] * (1.0 + scale_a) + shift_a).astype(bf16)
    s_a0.start()
    s_a1.start()
    parts2.start()
    a_q1.start()
    a_wo.start()

    def places(shape, dim):
        at = lax.broadcasted_iota(jnp.int32, shape, dim)
        number, first, end = jnp.zeros(shape, jnp.int32), jnp.zeros(shape, jnp.int32), 0
        for c in range(lengths.shape[1] - 1):
            end = end + lengths[0, c]
            past = at >= end
            number = number + jnp.where(past, 1, 0)
            first = jnp.where(past, end, first)
        return number, at - first

    idr[...] = places((1, item), 1)[0]
    number, position = places((item, 1), 0)
    idc[...] = number
    lanes = lax.broadcasted_iota(jnp.int32, (1, 128), 1)
    rate = jnp.exp((lanes % 32).astype(f32) * (-2.0 * math.log(10000.0) / 64))
    phase = position.astype(f32) * rate
    cos[...] = jnp.cos(phase)
    sin[...] = jnp.where(lanes % 64 < 32, -1.0, 1.0) * jnp.sin(phase)

    a_q0.hand_on()
    total = psend2[d]
    parts2.wait_recv()
    for j in range(1, n):
        total = total + pbuf2[(d + j) % n]
    mod[s] = total
    mods.start()
    biases.wait_recv()
    if plain:
        own_bias = bbuf[0]
        for j in range(1, n):
            own_bias = own_bias + bbuf[j]
        bq = own_bias[:, :qw]
        bo = own_bias[:, qw : qw + width]
        bu = own_bias[:, qw + width : qw + width + ff_q]
        bd = own_bias[:, qw + width + ff_q :]
    else:
        each = 3 * own_rows // 128
        bqs = []
        for p in range(pairs):
            for j in range(3):
                u = j * (width // 128) + s * pairs + p
                bqs.append(bbuf[u // each, :, pl.ds(pl.multiple_of(u % each * 128, 128), 128)])
        bq = jnp.concatenate(bqs, axis=1)
        c0 = 3 * own_rows
        bo = jnp.concatenate([bbuf[i, :, c0 : c0 + own_rows] for i in range(n)], axis=1)
        c0 = c0 + own_rows
        c1 = c0 + 4 * units
        bd = jnp.concatenate([bbuf[i, :, c1 : c1 + own_rows] for i in range(n)], axis=1)
        odd = s % 2 == 1
        at = pl.ds(c0 + wide, 128)
        bu = jnp.concatenate([half_of_each(bbuf[2 * i, :, at], bbuf[2 * i + 1, :, at], odd) for i in range(n // 2)], axis=1)
        for c in take_wu:
            c.wait()
        for i in range(n // 2):
            pair = half_of_each(wu_raw[2 * i].astype(f32), wu_raw[2 * i + 1].astype(f32), odd)
            wu[d, :, 128 * i : 128 * i + 128] = pair.astype(bf16)
    mods.wait_recv()
    gate_a, shift_f, scale_f, gate_f = (mod[i] for i in range(4))
    a_q0.wait_rest()

    def project_pair(p, wq, before):
        c0 = 128 * p

        def one(i, carry):
            before(i)
            b = l.block(i)
            at = at_rows(b)
            pr = nn(xa[b], merged(wq)) + bq[:, p * pw : (p + 1) * pw]
            cb, sb = cos[at, :], sin[at, :]
            qp, kp, vp = (pr[:, 128 * j : 128 * j + 128] for j in range(3))
            vp = vp.astype(bf16)
            qp = (qp * cb + swap_halves(qp, lane) * sb).astype(bf16)
            kp = (kp * cb + swap_halves(kp, lane) * sb).astype(bf16)
            q[at, c0 : c0 + 128] = qp * jnp.bfloat16(0.125)
            k[at, c0 : c0 + 128] = kp
            v[at, c0 : c0 + 128] = vp
            kt[p, :, at] = jnp.transpose(kp.astype(f32)).astype(bf16)
            vt[p, :, at] = jnp.transpose(vp.astype(f32)).astype(bf16)
            return carry

        lax.fori_loop(0, 4, one, 0)

    def attend_pair(p, after):
        def one(j, carry):
            i = (j + 2) % 4
            b = l.block(i)
            at = at_rows(b)
            same = idc[...] == idr[:, at]
            qp, kp = q[at, 128 * p : 128 * p + 128], k[:, 128 * p : 128 * p + 128]
            outs = []
            for h in range(2):
                qm = jnp.where((lane < 64) == (h == 0), qp, jnp.zeros_like(qp))
                sc = jnp.where(same, nt(kp, qm), -1e30)
                top = jnp.max(sc, axis=0, keepdims=True)
                ex = jnp.exp(sc - top)
                su = jnp.sum(ex, axis=0, keepdims=True)
                lse[2 * p + h, :, at] = top + jnp.log(su)
                pt = (ex * (1.0 / su)).astype(bf16)
                outs.append(nn(vt[p, 64 * h : 64 * h + 64, :], pt))
            ao_out[b, :, 128 * p : 128 * p + 128] = jnp.transpose(jnp.concatenate(outs, axis=0)).astype(bf16)
            after(j, i)
            return carry

        lax.fori_loop(0, 4, one, 0)

    def after_first(j, i):
        @pl.when(j == 0)
        def _():
            a_wo.hand_on()
            s_wo.send(d)

        @pl.when(j == 1)
        def _():
            a_wd.start()

        @pl.when(j == 2)
        def _():
            s_d1.hand_on()

    def after_second(j, i):
        @pl.when(j != 2)
        def _():
            w_ao.copy_to(i).start()

        @pl.when(j == 0)
        def _():
            s_wo.hand_on(d)

        @pl.when(j == 1)
        def _():
            a_wu.hand_on()

        @pl.when(j == 2)
        def _():
            ao[s] = ao_out[s]

        @pl.when(j == 3)
        def _():
            s_wo.hand_on(l.px)

    def before_first(i):
        @pl.when(i == 1)
        def _():
            s_a0.wait(l.s1)
            s_a1.wait(l.s1)

        @pl.when(i == 2)
        def _():
            s_a0.hand_on()
            s_a1.hand_on()
            s_d1.start()

        @pl.when(i == 3)
        def _():
            s_a0.wait(l.s3)
            s_a1.wait(l.s3)
            s_d0.hand_on()
            a_wu.start()

    project_pair(0, wq0, before_first)
    a_q1.hand_on()
    attend_pair(0, after_first)
    a_q1.wait_rest()
    a_wo.wait_rest()
    s_wo.send(l.px)
    project_pair(1, wq1, lambda i: None)
    attend_pair(1, after_second)
    s_wo.wait_rest()
    w_ao.wait_recv()
    left = jnp.concatenate([ao[i] for i in range(4)], axis=1)
    for c in range(4):
        cs = slice(c * quarter, (c + 1) * quarter)
        attn_branch[:, cs] = nn(left, merged(wo.at[c])) + bo[:, cs]
    xm = frames[...] + gate_a * attn_branch[...]
    block_out[...] = xm
    nm, rstd = normed(xm)
    n_mid[...] = nm
    xf[s] = (nm * (1.0 + scale_f) + shift_f).astype(bf16)
    s_x0.start()
    s_x1.start()
    a_wd.hand_on()
    for g in (s_d0, s_d1):
        g.wait(l.s1)
        g.wait(l.s3)
        g.wait_send()
    for b in range(4):
        dffn[b] = (gate_f * dffn[b].astype(f32)).astype(bf16)
    a_wu.wait_rest()
    a_wd.wait_rest()

    def hidden_term(at):
        return nt(dhid[at, :], merged(wu))

    def ffn_term(at):
        return nn(gelu[at, :], merged(wd))

    def out_half(c):
        part = dattn[:, pl.ds(pl.multiple_of(c * 2 * quarter, 128), 2 * quarter)]
        return jnp.concatenate([tn(ao[i], part) for i in range(4)], axis=0)

    def xa_term(at):
        return nt(dproj[at, :pw], merged(wq0)) + nt(dproj[at, pw:], merged(wq1))

    half = rows // 2

    def feed(j, carry):
        late = j // 4
        i = late * (2 + j % 2) + (1 - late) * (j // 2)
        h = late * (j // 2 % 2) + (1 - late) * (j % 2)

        @pl.when(j == 2)
        def _():
            s_x0.wait(l.s1)
            s_x1.wait(l.s1)

        @pl.when(j == 4)
        def _():
            sum_x.near(hidden_term)
            s_x0.hand_on()

        @pl.when(j == 5)
        def _():
            s_x0.wait(l.s3)

        @pl.when(j == 6)
        def _():
            s_x1.hand_on()

        @pl.when(j == 7)
        def _():
            s_x1.wait(l.s3)

        b = l.block(i)
        inner = pl.ds(pl.multiple_of(h * half, half), half)
        at = pl.ds(pl.multiple_of(b * rows + h * half, half), half)
        act, slope = gelu_both(nn(xf[b, inner], merged(wu)) + bu)
        gelu[at, :] = act.astype(bf16)
        dhid[at, :] = (nt(dffn[b, inner], merged(wd)) * slope).astype(bf16)
        return carry

    lax.fori_loop(0, 8, feed, 0)
    sum_x.far(hidden_term)

    def make(left_of, right, g, chain, each):
        per = 256 // each

        def one(m, carry):
            val = tn(left_of(m), right()).astype(bf16)
            g[pl.ds(m * per, per)] = val.reshape(per, each, val.shape[1])
            chain.send_x(m * per, per)
            return carry

        lax.fori_loop(0, n // per, one, 0)

    def cols_of(ref, m):
        return ref[:, :, pl.ds(pl.multiple_of(m * 256, 256), 256)].reshape(item, 256)

    make(lambda m: gelu[:, pl.ds(pl.multiple_of(m * 256, 256), 256)], lambda: merged(dffn), g_wd, d_wd, units)
    make(lambda m: cols_of(xf, m), lambda: dhid[...], g_wu, d_wu, own_rows)
    eb[:, :ff_q] = jnp.sum(dhid[...].astype(f32), axis=0, keepdims=True)
    eb[:, ff_q + width :] = jnp.sum(dffn[s].astype(f32), axis=0, keepdims=True)
    dk[...] = jnp.zeros_like(dk)
    dv[...] = jnp.zeros_like(dv)
    sum_f.far(ffn_term, False)
    sum_f.near(ffn_term)
    g = sum_x.total(hidden_term)
    nm = n_mid[...]
    fsum[0:1, :] = jnp.sum(g, axis=0, keepdims=True)
    fsum[1:2, :] = jnp.sum(g * nm, axis=0, keepdims=True)
    dm = cot[...] + norm_back(g * (1.0 + scale_f), nm, normed(block_out[...])[1])
    grad_input[...] = dm
    dattn[...] = (gate_a * dm).astype(bf16)
    per4 = n // 4
    w_ao.wait_send()

    def give(j, carry):
        i = (j + 2) % 4
        t = l.block(i)
        out = None
        for c in range(4):
            wt = wo[c, pl.ds(t * per4, per4)].reshape(quarter, quarter)
            o = nt(dattn[:, c * quarter : (c + 1) * quarter], wt)
            out = o if out is None else out + o
        ao_out[t] = out.astype(bf16)

        @pl.when(j != 2)
        def _():
            w_do.copy_to(i).start()

        @pl.when(j == 2)
        def _():
            gh[s] = ao_out[s]

        return carry

    lax.fori_loop(0, 4, give, 0)
    fsum[2:3, :] = jnp.sum(dm * attn_branch[...], axis=0, keepdims=True)
    eb[:, ff_q : ff_q + width] = jnp.sum(dattn[...].astype(f32), axis=0, keepdims=True)
    eb_all.start()

    def leave(src, dst, k):
        return pltpu.make_async_copy(src, dst, gone.at[k])

    def turned(values, at):
        val = values.astype(bf16).astype(f32)
        return (val * cos[at, :] - swap_halves(val, lane) * sin[at, :]).astype(bf16)

    def back_pair(p, before, after):
        c0, base = 128 * p, p * pw

        def one(i, carry):
            before(i)
            b = l.block(i)
            at = at_rows(b)
            same = idc[...] == idr[:, at]
            kp, vp = k[:, c0 : c0 + 128], v[:, c0 : c0 + 128]
            qp, dop = q[at, c0 : c0 + 128], gh[b, :, c0 : c0 + 128]
            dqs, pts, dsts, qms, doms = [], [], [], [], []
            for h in range(2):
                mine = (lane < 64) == (h == 0)
                qm = jnp.where(mine, qp, jnp.zeros_like(qp))
                dom = jnp.where(mine, dop, jnp.zeros_like(dop))
                pt = jnp.exp(jnp.where(same, nt(kp, qm), -1e30) - lse[2 * p + h, :, at])
                dpt = nt(vp, dom)
                mean = jnp.sum(dpt * pt, axis=0, keepdims=True)
                dst = (pt * (dpt - mean)).astype(bf16)
                pts.append(pt.astype(bf16))
                dsts.append(dst)
                qms.append(qm)
                doms.append(dom)
                dqs.append(nn(kt[p, 64 * h : 64 * h + 64, :], dst))
            dv[p] += nn(jnp.concatenate(pts, axis=1), jnp.concatenate(doms, axis=0))
            dk[p] += nn(jnp.concatenate(dsts, axis=1), jnp.concatenate(qms, axis=0))
            dq = jnp.transpose(jnp.concatenate(dqs, axis=0)) * 0.125
            dproj[at, base : base + 128] = turned(dq, at)
            after(i)
            return carry

        lax.fori_loop(0, 4, one, 0)

        def finish(b, carry):
            at = at_rows(b)
            dproj[at, base + 128 : base + 256] = turned(dk[p, at, :], at)
            dproj[at, base + 256 : base + 384] = dv[p, at, :].astype(bf16)
            return carry

        lax.fori_loop(0, 4, finish, 0)

    def before0(i):
        @pl.when(i == 1)
        def _():
            w_do.wait_one(1)

        @pl.when(i == 2)
        def _():
            w_do.wait_one(2)

        @pl.when(i == 3)
        def _():
            w_do.wait_one(3)

    def after0(i):
        @pl.when(i == 0)
        def _():
            ho[0] = out_half(1 - core).astype(bf16)
            c_wo.start()

        @pl.when(i == 1)
        def _():
            mine = out_half(core)
            c_wo.wait_recv()
            g_wo[...] = (mine + ho[1].astype(f32)).astype(bf16).reshape(n, own_rows, 2 * quarter)
            d_wo.send_x(0, n)

        @pl.when(i == 2)
        def _():
            sum_f.cross()
            d_wu.fold()

    def after1(i):
        @pl.when(i == 2)
        def _():
            ffn = sum_f.total(ffn_term) + bd
            block_out[...] = block_out[...] + gate_f * ffn
            leave(block_out, out_hbm, 0).start()
            d_wo.fold()
            em[s, :, 3 * width :] = jnp.sum(cot[...] * ffn, axis=0, keepdims=True)
            em[s, :, :width] = fsum[2:3, :]
            em[s, :, width : 2 * width] = fsum[0:1, :]
            em[s, :, 2 * width : 3 * width] = fsum[1:2, :]
            e_mod.start()

        @pl.when(i == 3)
        def _():
            e_mod.wait_recv()
            dmb[d, :, 2 * width :] = (em[0] + em[1] + em[2] + em[3]).astype(bf16).astype(f32)
            e_all.start()

    d_wd.fold()
    back_pair(0, before0, after0)
    make(lambda m: cols_of(xa, m), lambda: dproj[:, :pw], g_q0, d_q0, own_rows)
    back_pair(1, lambda i: None, after1)
    sum_x.wait_send()
    sum_a.far(xa_term)
    d_q0.fold()
    make(lambda m: cols_of(xa, m), lambda: dproj[:, pw:], g_q1, d_q1, own_rows)
    sum_a.near(xa_term)
    lb[...] = jnp.sum(dproj[...].astype(f32), axis=0, keepdims=True)
    lb_all.start()
    f_wd[s] = d_wd.total().astype(bf16)
    f_wu[s] = d_wu.total().astype(bf16)
    e_all.wait_recv()
    dm_e = jnp.concatenate([dmb[i, :, 2 * width :] for i in range(n)], axis=0).astype(bf16)
    dmat[:, 2 * width :] = dm_e
    dt = nt(dm_e, wm[:, 2 * width :])
    d_q1.fold()
    g = sum_a.total(xa_term)
    n_val = n_in[...]
    lm[s, :, :width] = jnp.sum(g, axis=0, keepdims=True)
    lm[s, :, width:] = jnp.sum(g * n_val, axis=0, keepdims=True)
    l_mod.start()
    o_wd.start()
    o_wu.start()
    grad_input[...] = grad_input[...] + norm_back(g * (1.0 + scale_a), n_val, normed(frames[...])[1])
    leave(grad_input, grad_hbm, 1).start()
    l_mod.wait_recv()
    dmb[d, :, : 2 * width] = (lm[0] + lm[1] + lm[2] + lm[3]).astype(bf16).astype(f32)
    l_all.start()
    fo[0] = d_wo.total().astype(bf16)
    y_wo.start()
    f_q0[s] = d_q0.total().astype(bf16)
    o_q0.start()
    eb_all.wait_recv()
    lb_all.wait_recv()
    esum, lsum = eb[...], lb[...]
    for j in range(1, n):
        esum = esum + ebb[(d + j) % n]
        lsum = lsum + lbb[(d + j) % n]
    f_b[s, :, :qw] = lsum
    f_b[s, :, qw:] = esum
    o_b.start()
    l_all.wait_recv()
    dm_l = jnp.concatenate([dmb[i, :, : 2 * width] for i in range(n)], axis=0).astype(bf16)
    dmat[:, : 2 * width] = dm_l
    dt = dt + nt(dm_l, wm[:, : 2 * width])
    for i in range(n):
        dts[i] = dt[i : i + 1]
    t_all.start()
    f_q1[s] = d_q1.total().astype(bf16)
    o_q1.start()
    o_wd.hand_on()
    o_wu.hand_on()
    y_wo.wait_recv()
    f_wo[core] = (fo[0].astype(f32) + fo[1].astype(f32)).astype(bf16)
    o_wo.start()
    o_q0.hand_on()
    t_all.wait_recv()
    dtb[d] = dts[d]
    sig = 1.0 / (1.0 + jnp.exp(-tv))
    slope = sig + tv * sig * (1.0 - sig)
    for i in range(n):
        at = slice(i * own_rows, (i + 1) * own_rows)
        grad_time[:, at] = dtb[i] * slope[:, at]
    for o in (o_wu, o_wd, o_q0):
        o.wait(l.s1)
        o.wait(l.s3)
    for t in range(4):
        n_mid[t * units : (t + 1) * units, :] = f_wd[t].astype(f32)
    ends = [leave(n_mid.at[: 4 * units], gwd_hbm, 2)]
    ends[0].start()
    if not plain:
        for i in range(n):
            for h in range(2):
                c0 = i // 2 * 128
                pair = half_of_each(
                    f_wu[2 * h, :, c0 : c0 + 128].astype(f32), f_wu[2 * h + 1, :, c0 : c0 + 128].astype(f32), i % 2 == 1
                )
                col = i * 4 * units + 128 * h
                r0 = col // width * own_rows
                n_in[r0 : r0 + own_rows, col % width : col % width + 128] = pair
        for c in range(2):
            ends.append(leave(n_in.at[c * own_rows : (c + 1) * own_rows], gwu_hbm.at[:, c * width : (c + 1) * width], 3 + c))
            ends[-1].start()
    o_wo.wait_recv()
    for c in range(2):
        attn_branch[:own_rows, c * 2 * quarter : (c + 1) * 2 * quarter] = f_wo[c].astype(f32)
    ends.append(leave(attn_branch.at[:own_rows], gwo_hbm, 5))
    ends[-1].start()
    thirds = (cot.at[:own_rows], cot.at[own_rows : 2 * own_rows], attn_branch.at[own_rows : 2 * own_rows])

    def place(p, held_p):
        for t in range(4):
            for j in range(3):
                at = t * quarter + 128 * p
                thirds[j][:, at : at + 128] = held_p[t, :, 128 * j : 128 * j + 128].astype(f32)

    place(0, f_q0)
    o_b.wait_recv()
    if plain:
        bias_out[...] = f_b[...]
    else:
        outs = []
        for i in range(each):
            u = d * each + i
            j, v = u // (width // 128), u % (width // 128)
            outs.append(f_b[v // pairs, :, pl.ds(pl.multiple_of(v % pairs * pw + j * 128, 128), 128)])
        for base in (qw + ff_q, qw + ff_q + width):
            at = pl.ds(pl.multiple_of(base + d * own_rows, 128), own_rows)
            outs.append(f_b[0, :, at] + f_b[1, :, at] + f_b[2, :, at] + f_b[3, :, at])
        at = pl.ds(pl.multiple_of(qw + d // 2 * 128, 128), 128)
        for h in range(2):
            outs.append(half_of_each(f_b[2 * h, :, at], f_b[2 * h + 1, :, at], d % 2 == 1))
        mod_each = 6 * width // n
        at = pl.ds(pl.multiple_of(d * mod_each, 128), mod_each)
        row = dmb[0, :, at]
        for i in range(1, n):
            row = row + dmb[i, :, at]
        outs.append(row)
        o_bq[...] = jnp.concatenate(outs[:each], axis=1)
        o_bo[...] = outs[each]
        o_bd[...] = outs[each + 1]
        o_bu[...] = jnp.concatenate(outs[each + 2 : each + 4], axis=1)
        o_bm[...] = outs[each + 4]
    o_q1.hand_on()
    o_q1.wait(l.s1)
    o_q1.wait(l.s3)
    place(1, f_q1)
    for j in range(3):
        ends.append(leave(thirds[j], gwq_hbm.at[:, j * width : (j + 1) * width], 6 + j))
        ends[-1].start()
    leave(block_out, out_hbm, 0).wait()
    leave(grad_input, grad_hbm, 1).wait()
    for c in ends:
        c.wait()
    for c in (
        times, parts, parts2, biases, mods, s_a0, s_a1, a_q0, a_q1, a_wu, a_wd, a_wo, s_x0, s_x1, s_wo, w_do,
        sum_f, sum_a, c_wo, y_wo, d_q0, d_q1, d_wo, d_wu, d_wd, o_q0, o_q1, o_wo, o_wu, o_wd, e_mod, l_mod, o_b,
        e_all, l_all, eb_all, lb_all, t_all,
    ):
        c.wait_send()


def run_whole(n, plain, clip_len, time_embed, bias, raw, wu_own, frames, cot, w_mod, w_qkv, w_out, w_down):
    rows, width = frames.shape
    item, quarter, own_rows = 4 * rows, width // 4, width // n
    ff_q = w_down.shape[0] * n // 4
    units, heads, pairs = ff_q // n, quarter // 64, quarter // 128
    qw = 3 * quarter
    pw = qw // pairs
    S, V = jax.ShapeDtypeStruct, pltpu.VMEM
    bw = qw + ff_q + 2 * width
    mod_own = 6 * width if plain else 6 * width // n
    bias_wide = bw if plain else 7 * width // n
    wide = V((rows, width), f32)
    outs = [
        S((1, width), f32), S((n, own_rows), bf16), S((n, 6 * width), bf16), S((4, own_rows, ff_q), bf16),
        S((4, 1, bw) if plain else (1, 1, 128), f32), S((1, 3 * own_rows), f32), S((1, own_rows), f32), S((1, own_rows), f32),
        S((1, 4 * units), f32), S((1, 6 * own_rows), f32), S((rows, width), f32), S((rows, width), f32),
        S((own_rows, 3 * width), f32), S((own_rows, width), f32), S((own_rows, 4 * ff_q), f32), S((4 * units, width), f32),
    ]

    def chain(a, b):
        return [V((n, a, b), bf16), V((n // 2, a, b), bf16), V((n // 2 - 1, a, b), bf16)]

    held = V((6, rows, width), bf16)
    scratch = (
        [V((n, 1, own_rows), f32), V((n, 1, 6 * width), f32)]
        + [wide] * 4
        + [
            V((1, 6 * width), f32), V((8, 128) if plain else (n, own_rows, 128), bf16), V((4, 1, bw), f32),
            V((own_rows, 6 * width), bf16), V((n, own_rows, pw), bf16), V((n, own_rows, pw), bf16),
            V((n, own_rows, ff_q), bf16), V((n, units, width), bf16), V((4, n, own_rows, quarter), bf16),
            V((n, 1, own_rows), f32), V((n, 1, 2 * width), f32), V((n, 1, 2 * width), f32), V((n, 1, width), f32),
            V((n, 1, width), f32), V((n, 1, bias_wide), f32), V((4, 1, width), f32), wide, wide, wide,
            V((item, 128), f32), V((item, 128), f32), V((item, 1), jnp.int32), V((1, item), jnp.int32),
            V((4, rows, width), bf16), V((4, rows, width), bf16), V((4, rows, width), bf16),
            V((item, quarter), bf16), V((item, quarter), bf16), V((item, quarter), bf16),
            V((pairs, 128, item), bf16), V((pairs, 128, item), bf16), V((heads, 1, item), f32),
        ]
        + [V((4, rows, quarter), bf16)] * 3
        + [
            V((item, ff_q), bf16), V((item, ff_q), bf16), V((rows, width), bf16), V((8, width), f32),
            V((pairs, item, 128), f32), V((pairs, item, 128), f32), V((item, qw), bf16),
            V((4, own_rows, pw), bf16), V((4, own_rows, pw), bf16), V((2, own_rows, 2 * quarter), bf16),
            V((4, units, width), bf16), held, held, V((2, width, 2 * quarter), bf16), V((2, own_rows, 2 * quarter), bf16),
        ]
        + chain(own_rows, pw) + chain(own_rows, pw) + chain(own_rows, 2 * quarter) + chain(own_rows, ff_q) + chain(units, width)
        + [
            V((4, 1, 4 * width), f32), V((4, 1, 2 * width), f32), V((1, ff_q + 2 * width), f32),
            V((n, 1, ff_q + 2 * width), f32), V((1, qw), f32), V((n, 1, qw), f32),
            V((n, 1, own_rows), f32), V((n, 1, own_rows), f32),
            pltpu.SemaphoreType.DMA((22 * n + 90,)), pltpu.SemaphoreType.DMA((22 * n + 100,)),
            pltpu.SemaphoreType.DMA((11 + n,)), pltpu.SemaphoreType.DMA((9,)),
        ]
    )
    vm = pl.BlockSpec(memory_space=pltpu.VMEM)
    hb = pl.BlockSpec(memory_space=pl.ANY)
    return pl.pallas_call(
        functools.partial(whole_kernel, n, plain),
        out_shape=outs,
        in_specs=[pl.BlockSpec(memory_space=pltpu.SMEM)] + [vm] * 7 + [hb] * 7,
        out_specs=[vm] * 10 + [hb] * 6,
        scratch_shapes=scratch,
        compiler_params=pltpu.CompilerParams(collective_id=0, has_side_effects=True, vmem_limit_bytes=63 << 20),
    )(clip_len, time_embed, bias, *raw, wu_own, frames, cot, w_mod, w_qkv, w_out, w_down)


def per_device(
    frames, time_embed, clip_len, w_qkv, b_qkv, w_out, b_out, w_up, b_up, w_down, b_down, w_mod, b_mod, cotangent
):
    n = lax.axis_size("dp")
    seq_rank, dp_rank = lax.axis_index("seq"), lax.axis_index("dp")
    rows, width = frames.shape
    quarter = width // 4
    own_rows, ff = w_up.shape
    units = w_down.shape[0] // 4
    pairs = quarter // 128
    ff_q = ff // 4
    qw = 3 * quarter

    plain = own_rows % 128 != 0 or units != 64
    raw = [b.reshape(1, -1) for b in (b_qkv, b_out, b_up, b_down, b_mod)]
    bias = jnp.zeros((1, 1, 128), f32)
    if plain:

        def placed(b):
            return lax.dynamic_update_slice(
                jnp.zeros((b.shape[0] * n,), f32), b.astype(f32), (dp_rank * b.shape[0],)
            )

        def mine(value, axis):
            return lax.dynamic_index_in_dim(value, seq_rank, axis, keepdims=False)

        laid = [
            mine(placed(b_qkv).reshape(3, 4, pairs, 128), 1).transpose(1, 0, 2).reshape(-1),
            placed(b_out),
            mine(placed(b_up).reshape(n, 4, units), 1).reshape(-1),
            placed(b_down),
            placed(b_mod),
        ]
        bias = jnp.concatenate(laid).reshape(1, 1, -1)
        wu_own = mine(w_up.reshape(own_rows, n, 4, units), 2).reshape(own_rows, ff_q)
    else:
        wu_own = w_up
    grad_time, tmat, d_mod, f_wu, f_b, *small, block_out, grad_input, s_wq, s_wo, s_wu, s_wd = run_whole(
        n, plain, clip_len, time_embed, bias, raw, wu_own, frames, cotangent, w_mod, w_qkv, w_out, w_down
    )
    gwm = tn(tmat, d_mod)
    if plain:
        s_wu = f_wu.astype(f32).reshape(4, own_rows, n, units).transpose(1, 2, 0, 3).reshape(own_rows, ff)

        def own(value, like):
            size = like.shape[0]
            return lax.dynamic_slice_in_dim(value, dp_rank * size, size, 0)

        bq = f_b[:, 0, :qw].reshape(4, pairs, 3, 128).transpose(2, 0, 1, 3).reshape(-1)
        bu = f_b[:, 0, qw : qw + ff_q].reshape(4, n, units).transpose(1, 0, 2).reshape(-1)
        bo = jnp.sum(f_b[:, 0, qw + ff_q : qw + ff_q + width], axis=0)
        bd = jnp.sum(f_b[:, 0, qw + ff_q + width :], axis=0)
        bq, bo, bu = own(bq, b_qkv), own(bo, b_out), own(bu, b_up)
        bd, bm = own(bd, b_down), own(jnp.sum(d_mod.astype(f32), axis=0), b_mod)
    else:
        bq, bo, bd, bu, bm = (b.reshape(-1) for b in small)
    return (block_out, grad_input, grad_time, s_wq, bq, s_wo, bo, s_wu, bu, s_wd, bd, gwm, bm)


def solution(mesh):
    placed = (
        P(("dp", "seq"), None),
        P("dp", None),
        P("dp", None),
        P("dp", None),
        P("dp"),
        P("dp", None),
        P("dp"),
        P("dp", None),
        P("dp"),
        P("dp", None),
        P("dp"),
        P("dp", None),
        P("dp"),
        P(("dp", "seq"), None),
    )
    return jax.shard_map(
        per_device,
        mesh=mesh,
        in_specs=placed,
        out_specs=(
            P(("dp", "seq"), None),
            P(("dp", "seq"), None),
            P("dp", None),
            P("dp", None),
            P("dp"),
            P("dp", None),
            P("dp"),
            P("dp", None),
            P("dp"),
            P("dp", None),
            P("dp"),
            P("dp", None),
            P("dp"),
        ),
        check_vma=False,
    )
```

```python
import functools
import math

import jax
import jax.numpy as jnp
from jax import lax
from jax.experimental import pallas as pl
from jax.experimental.pallas import tpu as pltpu
from jax.sharding import PartitionSpec as P

HEADS = 16
MESH = pl.DeviceIdType.MESH
f32 = jnp.float32
bf16 = jnp.bfloat16
norm_eps = 1e-06


def nn(left_side, right_side):
    return lax.dot_general(left_side, right_side, (((1,), (0,)), ((), ())), preferred_element_type=f32)


def nt(left_side, right_side):
    return lax.dot_general(left_side, right_side, (((1,), (1,)), ((), ())), preferred_element_type=f32)


def merged(ref):
    shape = ref.shape
    return ref[...].reshape(shape[0] * shape[1], shape[2])


def swap_halves(values, lane):
    up = pltpu.roll(values, 96, 1)
    down = pltpu.roll(values, 32, 1)
    return jnp.where(lane % 64 < 32, up, down)


def gelu_both(h):
    c = math.sqrt(2.0 / math.pi)
    h2 = h * h
    t = jnp.tanh(c * h * (1.0 + 0.044715 * h2))
    half = 0.5 * (1.0 + t)
    return h * half, half + 0.5 * h * (1.0 - t * t) * (c * (1.0 + 3.0 * 0.044715 * h2))


def normed(values):
    mean_val = jnp.mean(values, axis=-1, keepdims=True)
    centred = values - mean_val
    rstd = lax.rsqrt(jnp.mean(centred * centred, axis=-1, keepdims=True) + norm_eps)
    return centred * rstd, rstd


def norm_back(e, n, rstd):
    return (e - jnp.mean(e, axis=-1, keepdims=True) - n * jnp.mean(e * n, axis=-1, keepdims=True)) * rstd


class Links:
    def __init__(self, n, send, recv):
        self.n = n
        self.d = lax.axis_index("dp")
        self.s = lax.axis_index("seq")
        d, s = self.d, self.s
        self.px = d + 1 - 2 * (d % 2)
        self.s1 = s + 1 - 2 * (s % 2)
        self.s2 = (s + 2) % 4
        self.s3 = 3 - s
        self.send, self.recv = send, recv
        self.n_send = self.n_recv = 0

    def sems(self, sends, recvs):
        base = (self.n_send, self.n_recv)
        self.n_send += sends
        self.n_recv += recvs
        return base

    def block(self, i):
        s = self.s
        return (s % 2 + i % 2) % 2 + 2 * ((s // 2 + i // 2) % 2)

    def copy(self, src, dst, si, ri, dev):
        return pltpu.make_async_remote_copy(
            src_ref=src, dst_ref=dst, send_sem=self.send.at[si], recv_sem=self.recv.at[ri],
            device_id=dev, device_id_type=MESH,
        )

    def greet(self):
        b = pltpu.get_barrier_semaphore()
        for k in range(1, self.n):
            pl.semaphore_signal(b, inc=1, device_id=((self.d + k) % self.n, self.s), device_id_type=MESH)
        for t in (self.s1, self.s2, self.s3):
            pl.semaphore_signal(b, inc=1, device_id=(self.d, t), device_id_type=MESH)

    def meet(self):
        pl.semaphore_wait(pltpu.get_barrier_semaphore(), self.n + 2)


class ToAll:
    def __init__(self, links, src, buf, cols=None):
        self.l, self.src, self.buf, self.cols = links, src, buf, cols
        self.si, self.ri = links.sems(links.n, links.n)

    def _at(self, slot):
        return self.buf.at[slot] if self.cols is None else self.buf.at[slot, :, self.cols]

    def _to(self, k):
        l = self.l
        peer = (l.d + k) % l.n
        src = self._at(l.d) if self.src is None else self.src(peer)
        return l.copy(src, self._at(l.d), self.si + k, self.ri + l.d, (peer, l.s))

    def start(self):
        for k in range(1, self.l.n):
            self._to(k).start()

    def wait_recv(self):
        l = self.l
        for k in range(1, l.n):
            peer = (l.d + k) % l.n
            l.copy(self._at(peer), self._at(peer), self.si + k, self.ri + peer, (peer, l.s)).wait_recv()

    def wait_send(self):
        for k in range(1, self.l.n):
            self._to(k).wait_send()


class SeqAll:
    def __init__(self, links, buf):
        self.l, self.buf = links, buf
        self.si, self.ri = links.sems(4, 4)

    def _to(self, k):
        l = self.l
        t = l.block(k)
        return l.copy(self.buf.at[l.s], self.buf.at[l.s], self.si + k, self.ri + l.s, (l.d, t))

    def start(self):
        for k in (2, 3, 1):
            self._to(k).start()

    def wait_recv(self):
        l = self.l
        for k in (1, 2, 3):
            t = l.block(k)
            l.copy(self.buf.at[t], self.buf.at[t], self.si + k, self.ri + t, (l.d, t)).wait_recv()

    def wait_send(self):
        for k in (1, 2, 3):
            self._to(k).wait_send()


class DpGather:
    def __init__(self, links, buf):
        self.l, self.buf = links, buf
        self.si, self.ri = links.sems(links.n, links.n)
        self.half = links.n // 2

    def _z(self, k):
        l = self.l
        return l.copy(self.buf.at[l.d], self.buf.at[l.d], self.si + k, self.ri + l.d, ((l.d + 2 * k) % l.n, l.s))

    def _x(self, k):
        l = self.l
        r = (l.d + 2 * k) % l.n
        return l.copy(self.buf.at[r], self.buf.at[r], self.si + self.half + k, self.ri + r, (l.px, l.s))

    def start(self):
        for k in range(1, self.half):
            self._z(k).start()
        self._x(0).start()

    def hand_on(self):
        l = self.l
        for k in range(1, self.half):
            r = (l.d + 2 * k) % l.n
            l.copy(self.buf.at[r], self.buf.at[r], self.si, self.ri + r, (r, l.s)).wait_recv()
            self._x(k).start()

    def wait_rest(self):
        l = self.l
        for k in range(self.half):
            r = (l.px + 2 * k) % l.n
            l.copy(self.buf.at[r], self.buf.at[r], self.si, self.ri + r, (l.px, l.s)).wait_recv()

    def wait_send(self):
        for k in range(1, self.half):
            self._z(k).wait_send()
        for k in range(self.half):
            self._x(k).wait_send()


class SeqGather:
    def __init__(self, links, buf, rows=None):
        self.l, self.buf, self.rows = links, buf, rows
        self.si, self.ri = links.sems(3, 4)

    def _at(self, slot):
        return self.buf.at[slot] if self.rows is None else self.buf.at[slot, self.rows]

    def _c(self, slot, k, t):
        l = self.l
        return l.copy(self._at(slot), self._at(slot), self.si + k, self.ri + slot, (l.d, t))

    def start(self):
        l = self.l
        self._c(l.s, 0, l.s2).start()
        self._c(l.s, 1, l.s1).start()

    def hand_on(self):
        l = self.l
        self.wait(l.s2)
        self._c(l.s2, 2, l.s1).start()

    def wait(self, slot):
        self._c(slot, 0, self.l.s1).wait_recv()

    def wait_send(self):
        l = self.l
        self._c(l.s, 0, l.s2).wait_send()
        self._c(l.s, 1, l.s1).wait_send()
        self._c(l.s2, 2, l.s1).wait_send()


class SeqSwap:
    def __init__(self, links, out, into):
        self.l, self.out, self.into = links, out, into
        self.si, self.ri = links.sems(4, 4)

    def copy_to(self, i):
        l = self.l
        t = l.block(i)
        return l.copy(self.out.at[t], self.into.at[l.s], self.si + i, self.ri + l.s, (l.d, t))

    def wait_one(self, i):
        l = self.l
        t = l.block(i)
        l.copy(self.into.at[t], self.into.at[t], self.si + i, self.ri + t, (l.d, t)).wait_recv()

    def wait_recv(self):
        l = self.l
        for i in (1, 2, 3):
            t = l.block(i)
            l.copy(self.into.at[t], self.into.at[t], self.si + i, self.ri + t, (l.d, t)).wait_recv()

    def wait_send(self):
        for i in (1, 2, 3):
            self.copy_to(i).wait_send()


class SeqSum:
    def __init__(self, links, held):
        self.l, self.held = links, held
        self.rows = held.shape[1]
        self.si, self.ri = links.sems(5, 5)

    def _c(self, k, h, t):
        l = self.l
        half = self.rows // 2
        at = slice(None) if k == 2 else slice(h * half, (h + 1) * half)
        sem = 4 if k == 2 else 2 * k + h
        return l.copy(self.held.at[k, at], self.held.at[3 + k, at], self.si + sem, self.ri + sem, (l.d, t))

    def far(self, term, cross=True):
        l, held, half = self.l, self.held, self.rows // 2
        for h in range(2):
            held[0, h * half : (h + 1) * half] = term(l.s3, h).astype(bf16)
            self._c(0, h, l.s1).start()
        for h in range(2):
            at = slice(h * half, (h + 1) * half)
            mine = term(l.s2, h)
            self._c(0, h, l.s1).wait_recv()
            held[1, at] = (mine + held[3, at].astype(f32)).astype(bf16)
            if cross:
                self._c(1, h, l.s2).start()

    def cross(self):
        for h in range(2):
            self._c(1, h, self.l.s2).start()

    def near(self, term):
        l = self.l
        self.held[2] = term(l.s1, None).astype(bf16)
        self._c(2, 0, l.s1).start()

    def total(self, term):
        l, held = self.l, self.held
        mine = term(l.s, None)
        self._c(2, 0, l.s1).wait_recv()
        for h in range(2):
            self._c(1, h, l.s2).wait_recv()
        return mine + held[5].astype(f32) + held[4].astype(f32)

    def wait_send(self):
        l = self.l
        for h in range(2):
            self._c(0, h, l.s1).wait_send()
            self._c(1, h, l.s2).wait_send()
        self._c(2, 0, l.s1).wait_send()


def half_of_each(one, two, odd):
    lane = lax.broadcasted_iota(jnp.int32, one.shape, 1)
    low = jnp.where(odd, pltpu.roll(one, 64, 1), one)
    high = jnp.where(odd, two, pltpu.roll(two, 64, 1))
    return jnp.where(lane < 64, low, high)


def tn(left_side, right_side):
    return lax.dot_general(left_side, right_side, (((0,), (0,)), ((), ())), preferred_element_type=f32)


class SlotGather:
    def __init__(self, links, buf):
        self.l, self.buf = links, buf
        self.half = links.n // 2
        self.si, self.ri = links.sems(3 * links.n, 3 * links.n)

    def _c(self, block, r, kind, t):
        l = self.l
        at = kind * l.n + r
        return l.copy(self.buf.at[block, r], self.buf.at[block, r], self.si + at, self.ri + at, (l.d, t))

    def _each(self, base, body):
        def one(k, carry):
            body((base + 2 * k) % self.l.n)
            return carry

        lax.fori_loop(0, self.half, one, 0)

    def send(self, base):
        l = self.l

        def body(r):
            self._c(l.s, r, 0, l.s2).start()
            self._c(l.s, r, 1, l.s1).start()

        self._each(base, body)

    def hand_on(self, base):
        l = self.l

        def body(r):
            self._c(l.s2, r, 0, l.s2).wait_recv()
            self._c(l.s2, r, 2, l.s1).start()

        self._each(base, body)

    def wait_rest(self):
        l = self.l

        def one(r, carry):
            self._c(l.s1, r, 1, l.s1).wait_recv()
            self._c(l.s3, r, 2, l.s1).wait_recv()
            return carry

        lax.fori_loop(0, l.n, one, 0)

    def wait_send(self):
        l = self.l

        def one(r, carry):
            self._c(l.s, r, 0, l.s2).wait_send()
            self._c(l.s, r, 1, l.s1).wait_send()
            self._c(l.s2, r, 2, l.s1).wait_send()
            return carry

        lax.fori_loop(0, l.n, one, 0)


class DpSum:
    def __init__(self, links, g, xin, zin):
        self.l, self.g, self.xin, self.zin = links, g, xin, zin
        self.half = links.n // 2
        self.si, self.ri = links.sems(links.n, links.n)

    def _x(self, t):
        l = self.l
        h = t // 2
        return l.copy(self.g.at[t], self.xin.at[h], self.si + h, self.ri + h, (l.px, l.s))

    def _z(self, k):
        l = self.l
        t = (l.d + 2 * k) % l.n
        at = self.half + k
        return l.copy(self.g.at[t], self.zin.at[k - 1], self.si + at, self.ri + at, (t, l.s))

    def send_x(self, first, count):
        for i in range(count // 2):
            self._x(first + 2 * i + self.l.px % 2).start()

    def fold(self):
        l = self.l

        def one(k, carry):
            t = (l.d + 2 * k) % l.n
            h = t // 2
            l.copy(self.xin.at[h], self.xin.at[h], self.si, self.ri + h, (l.px, l.s)).wait_recv()
            self.g[t] = (self.g[t].astype(f32) + self.xin[h].astype(f32)).astype(bf16)
            self._z(k).start()
            return carry

        lax.fori_loop(1, self.half, one, 0)

    def total(self):
        l = self.l
        h = l.d // 2
        l.copy(self.xin.at[h], self.xin.at[h], self.si, self.ri + h, (l.px, l.s)).wait_recv()
        out = self.g[l.d].astype(f32) + self.xin[h].astype(f32)
        for k in range(1, self.half):
            self._z(k).wait_recv()
            out = out + self.zin[k - 1].astype(f32)
        return out

    def wait_send(self):
        l = self.l
        for k in range(self.half):
            self._x((l.px + 2 * k) % l.n).wait_send()
        for k in range(1, self.half):
            self._z(k).wait_send()


def whole_kernel(
    n, plain,
    lengths, time_row, bias, b1, b2, b3, b4, b5, wu_own, frames_hbm, cot_hbm, wm_hbm, wq_hbm, wo_hbm, wd_hbm,
    grad_time, tmat, dmat, f_wu, bias_out, o_bq, o_bo, o_bd, o_bu, o_bm, out_hbm, grad_hbm, gwq_hbm, gwo_hbm, gwu_hbm, gwd_hbm,
    tbuf, dmb, frames, cot, block_out, grad_input, bmv, wu_raw, f_b, wm, wq0, wq1, wu, wd, wo, tsrc, psend, pbuf, psend2, pbuf2, bbuf, mod, n_in, attn_branch, n_mid, cos, sin, idc, idr,
    xa, dffn, xf, q, k, v, kt, vt, lse, ao_out, ao, gh, gelu, dhid, dattn, fsum, dk, dv, dproj,
    f_q0, f_q1, f_wo, f_wd, held, held_f, held_o, g_q0, x_q0, z_q0, g_q1, x_q1, z_q1, g_wo, x_wo, z_wo, g_wu, x_wu, z_wu, g_wd, x_wd, z_wd,
    em, lm, eb, ebb, lb, lbb, dts, dtb,
    send, recv, local, gone,
):
    l = Links(n, send, recv)
    l.greet()
    d, s = l.d, l.s
    rows, width = frames.shape
    item = 4 * rows
    quarter = width // 4
    own_rows = wm.shape[0]
    units = wd.shape[1]
    ff_q = wu.shape[2]
    pairs = quarter // 128
    qw = 3 * quarter
    pw = qw // pairs
    lane = lax.broadcasted_iota(jnp.int32, (rows, 128), 1)
    take = [
        pltpu.make_async_copy(wm_hbm, wm, local.at[0]),
        pltpu.make_async_copy(wd_hbm.at[pl.ds(pl.multiple_of(s * units, 8), units), :], wd.at[d], local.at[1]),
        pltpu.make_async_copy(wo_hbm.at[:, pl.ds(pl.multiple_of(s * quarter, 128), quarter)], wo.at[s, d], local.at[2]),
    ] + [
        pltpu.make_async_copy(
            wq_hbm.at[:, pl.ds(pl.multiple_of(j * width + s * quarter + 128 * p, 128), 128)],
            (wq0, wq1)[p].at[d, :, pl.ds(128 * j, 128)], local.at[3 + 3 * p + j],
        )
        for p in range(pairs) for j in range(3)
    ]
    first = [
        pltpu.make_async_copy(frames_hbm, frames, local.at[9]),
        pltpu.make_async_copy(cot_hbm, cot, local.at[10]),
    ]
    if not plain:
        wide = pl.multiple_of(s // 2 * 128, 128)
        take_wu = [
            pltpu.make_async_copy(wu_own.at[:, pl.ds(i * 4 * units + wide, 128)], wu_raw.at[i], local.at[11 + i])
            for i in range(n)
        ]
    for c in first + take:
        c.start()
    times = ToAll(l, lambda peer: tsrc.at[peer], tbuf)
    parts, parts2 = ToAll(l, lambda peer: psend.at[peer], pbuf), ToAll(l, lambda peer: psend2.at[peer], pbuf2)
    wide_b = bbuf.shape[2]
    biases = ToAll(l, None, bbuf)
    mods = SeqAll(l, mod)
    a_q0, a_q1, a_wu, a_wd, a_wo = DpGather(l, wq0), DpGather(l, wq1), DpGather(l, wu), DpGather(l, wd), DpGather(l, wo.at[s])
    s_wo = SlotGather(l, wo)
    s_a0, s_a1 = (SeqGather(l, xa, pl.ds(h * (rows // 2), rows // 2)) for h in range(2))
    s_x0, s_x1 = (SeqGather(l, xf, pl.ds(h * (rows // 2), rows // 2)) for h in range(2))
    s_d0, s_d1 = (SeqGather(l, dffn, pl.ds(h * (rows // 2), rows // 2)) for h in range(2))
    w_ao, w_do = SeqSwap(l, ao_out, ao), SeqSwap(l, ao_out, gh)
    sum_x, sum_f, sum_a = SeqSum(l, held), SeqSum(l, held_f), SeqSum(l, held)
    d_q0, d_q1, d_wo, d_wu, d_wd = (
        DpSum(l, g_q0, x_q0, z_q0), DpSum(l, g_q1, x_q1, z_q1), DpSum(l, g_wo, x_wo, z_wo),
        DpSum(l, g_wu, x_wu, z_wu), DpSum(l, g_wd, x_wd, z_wd),
    )
    o_q0, o_q1, o_wu, o_wd = (
        SeqGather(l, f_q0), SeqGather(l, f_q1), SeqGather(l, f_wu), SeqGather(l, f_wd)
    )
    sum_o, o_wo = SeqSum(l, held_o), SeqGather(l, f_wo)
    e_mod, l_mod, o_b = SeqAll(l, em), SeqAll(l, lm), SeqAll(l, f_b)
    e_all, l_all = ToAll(l, None, dmb, slice(2 * width, 6 * width)), ToAll(l, None, dmb, slice(0, 2 * width))
    eb_all, lb_all = ToAll(l, lambda peer: eb, ebb), ToAll(l, lambda peer: lb, lbb)
    t_all = ToAll(l, lambda peer: dts.at[peer], dtb)

    def at_rows(b):
        return pl.ds(pl.multiple_of(b * rows, rows), rows)

    if plain:
        bbuf[d] = bias[0, :, :wide_b]
        own_mod = bias[0, :, wide_b:]
    else:
        bbuf[d] = jnp.concatenate([b[...].astype(f32).reshape(1, -1) for b in (b1, b2, b3, b4)], axis=1)
        own_mod = b5[...].astype(f32).reshape(1, -1)
    if plain:
        bmv[...] = own_mod
    else:
        bmv[...] = jnp.concatenate([jnp.where(d == i, own_mod, jnp.zeros_like(own_mod)) for i in range(n)], axis=1)
    tv = time_row[...]
    act = (tv / (1.0 + jnp.exp(-tv))).astype(bf16).astype(f32)
    for i in range(n):
        tsrc[i] = act[:, i * own_rows : (i + 1) * own_rows]
    for c in first:
        c.wait()
    n_in[...] = normed(frames[...])[0]
    dffn[s] = cot[...].astype(bf16)
    for c in take[3:]:
        c.wait()
    l.meet()
    times.start()
    a_q0.start()
    s_d0.start()
    biases.start()
    tbuf[d] = tsrc[d]
    if plain:
        wu_copy = pltpu.make_async_copy(wu_own, wu.at[d], local.at[11])
        wu_copy.start()
        wu_copy.wait()
    else:
        for c in take_wu:
            c.start()
    for c in take[:3]:
        c.wait()
    times.wait_recv()
    lhs = jnp.concatenate([tbuf[i] for i in range(n)], axis=0).astype(bf16)
    tmat[...] = lhs
    part = nn(lhs, wm[:, : 2 * width]) + bmv[:, : 2 * width]
    for i in range(n):
        psend[i] = part[i : i + 1]
    parts.start()
    part = nn(lhs, wm[:, pl.ds(pl.multiple_of((2 + s) * width, 128), width)]) + bmv[:, pl.ds(pl.multiple_of((2 + s) * width, 128), width)]
    for i in range(n):
        psend2[i] = part[i : i + 1]
    total = psend[d]
    parts.wait_recv()
    for j in range(1, n):
        total = total + pbuf[(d + j) % n]
    shift_a, scale_a = total[:, :width], total[:, width:]
    xa[s] = (n_in[...] * (1.0 + scale_a) + shift_a).astype(bf16)
    s_a0.start()
    s_a1.start()
    parts2.start()
    a_q1.start()
    a_wo.start()

    def places(shape, dim):
        at = lax.broadcasted_iota(jnp.int32, shape, dim)
        number, first, end = jnp.zeros(shape, jnp.int32), jnp.zeros(shape, jnp.int32), 0
        for c in range(lengths.shape[1] - 1):
            end = end + lengths[0, c]
            past = at >= end
            number = number + jnp.where(past, 1, 0)
            first = jnp.where(past, end, first)
        return number, at - first

    idr[...] = places((1, item), 1)[0]
    number, position = places((item, 1), 0)
    idc[...] = number
    lanes = lax.broadcasted_iota(jnp.int32, (1, 128), 1)
    rate = jnp.exp((lanes % 32).astype(f32) * (-2.0 * math.log(10000.0) / 64))
    phase = position.astype(f32) * rate
    cos[...] = jnp.cos(phase)
    sin[...] = jnp.where(lanes % 64 < 32, -1.0, 1.0) * jnp.sin(phase)

    a_q0.hand_on()
    total = psend2[d]
    parts2.wait_recv()
    for j in range(1, n):
        total = total + pbuf2[(d + j) % n]
    mod[s] = total
    mods.start()
    biases.wait_recv()
    if plain:
        own_bias = bbuf[0]
        for j in range(1, n):
            own_bias = own_bias + bbuf[j]
        bq = own_bias[:, :qw]
        bo = own_bias[:, qw : qw + width]
        bu = own_bias[:, qw + width : qw + width + ff_q]
        bd = own_bias[:, qw + width + ff_q :]
    else:
        each = 3 * own_rows // 128
        bqs = []
        for p in range(pairs):
            for j in range(3):
                u = j * (width // 128) + s * pairs + p
                bqs.append(bbuf[u // each, :, pl.ds(pl.multiple_of(u % each * 128, 128), 128)])
        bq = jnp.concatenate(bqs, axis=1)
        c0 = 3 * own_rows
        bo = jnp.concatenate([bbuf[i, :, c0 : c0 + own_rows] for i in range(n)], axis=1)
        c0 = c0 + own_rows
        c1 = c0 + 4 * units
        bd = jnp.concatenate([bbuf[i, :, c1 : c1 + own_rows] for i in range(n)], axis=1)
        odd = s % 2 == 1
        at = pl.ds(c0 + wide, 128)
        bu = jnp.concatenate([half_of_each(bbuf[2 * i, :, at], bbuf[2 * i + 1, :, at], odd) for i in range(n // 2)], axis=1)
        for c in take_wu:
            c.wait()
        for i in range(n // 2):
            pair = half_of_each(wu_raw[2 * i].astype(f32), wu_raw[2 * i + 1].astype(f32), odd)
            wu[d, :, 128 * i : 128 * i + 128] = pair.astype(bf16)
    mods.wait_recv()
    gate_a, shift_f, scale_f, gate_f = (mod[i] for i in range(4))
    a_q0.wait_rest()

    def project_pair(p, wq, before):
        c0 = 128 * p

        def one(i, carry):
            before(i)
            b = l.block(i)
            at = at_rows(b)
            pr = nn(xa[b], merged(wq)) + bq[:, p * pw : (p + 1) * pw]
            cb, sb = cos[at, :], sin[at, :]
            qp, kp, vp = (pr[:, 128 * j : 128 * j + 128] for j in range(3))
            vp = vp.astype(bf16)
            qp = (qp * cb + swap_halves(qp, lane) * sb).astype(bf16)
            kp = (kp * cb + swap_halves(kp, lane) * sb).astype(bf16)
            q[at, c0 : c0 + 128] = qp * jnp.bfloat16(0.125)
            k[at, c0 : c0 + 128] = kp
            v[at, c0 : c0 + 128] = vp
            kt[p, :, at] = jnp.transpose(kp)
            vt[p, :, at] = jnp.transpose(vp)
            return carry

        lax.fori_loop(0, 4, one, 0)

    def attend_pair(p, after):
        def one(j, carry):
            i = (j + 2) % 4
            b = l.block(i)
            at = at_rows(b)
            same = idc[...] == idr[:, at]
            qp, kp = q[at, 128 * p : 128 * p + 128], k[:, 128 * p : 128 * p + 128]
            outs = []
            for h in range(2):
                qm = jnp.where((lane < 64) == (h == 0), qp, jnp.zeros_like(qp))
                sc = jnp.where(same, nt(kp, qm), -1e30)
                top = jnp.max(sc, axis=0, keepdims=True)
                ex = jnp.exp(sc - top)
                su = jnp.sum(ex, axis=0, keepdims=True)
                lse[2 * p + h, :, at] = top + jnp.log(su)
                pt = (ex * (1.0 / su)).astype(bf16)
                outs.append(nn(vt[p, 64 * h : 64 * h + 64, :], pt))
            ao_out[b, :, 128 * p : 128 * p + 128] = jnp.transpose(jnp.concatenate(outs, axis=0)).astype(bf16)
            after(j, i)
            return carry

        lax.fori_loop(0, 4, one, 0)

    def after_first(j, i):
        @pl.when(j == 0)
        def _():
            a_wo.hand_on()
            s_wo.send(d)

        @pl.when(j == 1)
        def _():
            a_wd.start()

        @pl.when(j == 2)
        def _():
            s_d1.hand_on()

    def after_second(j, i):
        @pl.when(j != 2)
        def _():
            w_ao.copy_to(i).start()

        @pl.when(j == 0)
        def _():
            s_wo.hand_on(d)

        @pl.when(j == 1)
        def _():
            a_wu.hand_on()

        @pl.when(j == 2)
        def _():
            ao[s] = ao_out[s]

        @pl.when(j == 3)
        def _():
            s_wo.hand_on(l.px)

    def before_first(i):
        @pl.when(i == 1)
        def _():
            s_a0.wait(l.s1)
            s_a1.wait(l.s1)

        @pl.when(i == 2)
        def _():
            s_a0.hand_on()
            s_a1.hand_on()
            s_d1.start()

        @pl.when(i == 3)
        def _():
            s_a0.wait(l.s3)
            s_a1.wait(l.s3)
            s_d0.hand_on()
            a_wu.start()

    project_pair(0, wq0, before_first)
    a_q1.hand_on()
    attend_pair(0, after_first)
    a_q1.wait_rest()
    a_wo.wait_rest()
    s_wo.send(l.px)
    project_pair(1, wq1, lambda i: None)
    attend_pair(1, after_second)
    s_wo.wait_rest()
    w_ao.wait_recv()
    left = jnp.concatenate([ao[i] for i in range(4)], axis=1)
    for c in range(4):
        cs = slice(c * quarter, (c + 1) * quarter)
        attn_branch[:, cs] = nn(left, merged(wo.at[c])) + bo[:, cs]
    xm = frames[...] + gate_a * attn_branch[...]
    block_out[...] = xm
    nm, rstd = normed(xm)
    n_mid[...] = nm
    xf[s] = (nm * (1.0 + scale_f) + shift_f).astype(bf16)
    s_x0.start()
    s_x1.start()
    a_wd.hand_on()
    for g in (s_d0, s_d1):
        g.wait(l.s1)
        g.wait(l.s3)
        g.wait_send()
    for b in range(4):
        dffn[b] = (gate_f * dffn[b].astype(f32)).astype(bf16)
    a_wu.wait_rest()
    a_wd.wait_rest()

    def run_of(b, h):
        if h is None:
            return at_rows(b)
        return pl.ds(pl.multiple_of(b * rows + h * half, half), half)

    def hidden_term(b, h):
        return nt(dhid[run_of(b, h), :], merged(wu))

    def ffn_term(b, h):
        return nn(gelu[run_of(b, h), :], merged(wd))

    def out_term(t, h):
        part = dattn[:, pl.ds(pl.multiple_of(t * quarter, 128), quarter)]
        blocks = range(4) if h is None else (2 * h, 2 * h + 1)
        return jnp.concatenate([tn(ao[i], part) for i in blocks], axis=0)

    def xa_term(b, h):
        at = run_of(b, h)
        return nt(dproj[at, :pw], merged(wq0)) + nt(dproj[at, pw:], merged(wq1))

    half = rows // 2

    def feed(j, carry):
        late = j // 4
        i = late * (2 + j % 2) + (1 - late) * (j // 2)
        h = late * (j // 2 % 2) + (1 - late) * (j % 2)

        @pl.when(j == 2)
        def _():
            s_x0.wait(l.s1)
            s_x1.wait(l.s1)

        @pl.when(j == 4)
        def _():
            sum_x.near(hidden_term)
            s_x0.hand_on()

        @pl.when(j == 5)
        def _():
            s_x0.wait(l.s3)

        @pl.when(j == 6)
        def _():
            s_x1.hand_on()

        @pl.when(j == 7)
        def _():
            s_x1.wait(l.s3)

        b = l.block(i)
        inner = pl.ds(pl.multiple_of(h * half, half), half)
        at = pl.ds(pl.multiple_of(b * rows + h * half, half), half)
        act, slope = gelu_both(nn(xf[b, inner], merged(wu)) + bu)
        gelu[at, :] = act.astype(bf16)
        dhid[at, :] = (nt(dffn[b, inner], merged(wd)) * slope).astype(bf16)
        return carry

    lax.fori_loop(0, 8, feed, 0)
    sum_x.far(hidden_term)

    def make(left_of, right, g, chain, each):
        per = 256 // each

        def one(m, carry):
            val = tn(left_of(m), right()).astype(bf16)
            g[pl.ds(m * per, per)] = val.reshape(per, each, val.shape[1])
            chain.send_x(m * per, per)
            return carry

        lax.fori_loop(0, n // per, one, 0)

    def cols_of(ref, m):
        return ref[:, :, pl.ds(pl.multiple_of(m * 256, 256), 256)].reshape(item, 256)

    make(lambda m: gelu[:, pl.ds(pl.multiple_of(m * 256, 256), 256)], lambda: merged(dffn), g_wd, d_wd, units)
    make(lambda m: cols_of(xf, m), lambda: dhid[...], g_wu, d_wu, own_rows)
    eb[:, :ff_q] = jnp.sum(dhid[...].astype(f32), axis=0, keepdims=True)
    eb[:, ff_q + width :] = jnp.sum(dffn[s].astype(f32), axis=0, keepdims=True)
    dk[...] = jnp.zeros_like(dk)
    dv[...] = jnp.zeros_like(dv)
    sum_f.far(ffn_term, False)
    sum_f.near(ffn_term)
    g = sum_x.total(hidden_term)
    nm = n_mid[...]
    fsum[0:1, :] = jnp.sum(g, axis=0, keepdims=True)
    fsum[1:2, :] = jnp.sum(g * nm, axis=0, keepdims=True)
    dm = cot[...] + norm_back(g * (1.0 + scale_f), nm, normed(block_out[...])[1])
    grad_input[...] = dm
    dattn[...] = (gate_a * dm).astype(bf16)
    per4 = n // 4
    w_ao.wait_send()

    def give(j, carry):
        i = (j + 2) % 4
        t = l.block(i)
        out = None
        for c in range(4):
            wt = wo[c, pl.ds(t * per4, per4)].reshape(quarter, quarter)
            o = nt(dattn[:, c * quarter : (c + 1) * quarter], wt)
            out = o if out is None else out + o
        ao_out[t] = out.astype(bf16)

        @pl.when(j != 2)
        def _():
            w_do.copy_to(i).start()

        @pl.when(j == 2)
        def _():
            gh[s] = ao_out[s]

        return carry

    lax.fori_loop(0, 4, give, 0)
    fsum[2:3, :] = jnp.sum(dm * attn_branch[...], axis=0, keepdims=True)
    eb[:, ff_q : ff_q + width] = jnp.sum(dattn[...].astype(f32), axis=0, keepdims=True)
    eb_all.start()

    def leave(src, dst, k):
        return pltpu.make_async_copy(src, dst, gone.at[k])

    def turned(values, at):
        val = values.astype(bf16).astype(f32)
        return (val * cos[at, :] - swap_halves(val, lane) * sin[at, :]).astype(bf16)

    def back_pair(p, before, after):
        c0, base = 128 * p, p * pw

        def one(i, carry):
            before(i)
            b = l.block(i)
            at = at_rows(b)
            same = idc[...] == idr[:, at]
            kp, vp = k[:, c0 : c0 + 128], v[:, c0 : c0 + 128]
            qp, dop = q[at, c0 : c0 + 128], gh[b, :, c0 : c0 + 128]
            dqs, pts, dsts, qms, doms = [], [], [], [], []
            for h in range(2):
                mine = (lane < 64) == (h == 0)
                qm = jnp.where(mine, qp, jnp.zeros_like(qp))
                dom = jnp.where(mine, dop, jnp.zeros_like(dop))
                pt = jnp.exp(jnp.where(same, nt(kp, qm), -1e30) - lse[2 * p + h, :, at])
                dpt = nt(vp, dom)
                mean = jnp.sum(dpt * pt, axis=0, keepdims=True)
                dst = (pt * (dpt - mean)).astype(bf16)
                pts.append(pt.astype(bf16))
                dsts.append(dst)
                qms.append(qm)
                doms.append(dom)
                dqs.append(nn(kt[p, 64 * h : 64 * h + 64, :], dst))
            dv[p] += nn(jnp.concatenate(pts, axis=1), jnp.concatenate(doms, axis=0))
            dk[p] += nn(jnp.concatenate(dsts, axis=1), jnp.concatenate(qms, axis=0))
            dq = jnp.transpose(jnp.concatenate(dqs, axis=0)) * 0.125
            dproj[at, base : base + 128] = turned(dq, at)
            after(i)
            return carry

        lax.fori_loop(0, 4, one, 0)

        def finish(b, carry):
            at = at_rows(b)
            dproj[at, base + 128 : base + 256] = turned(dk[p, at, :], at)
            dproj[at, base + 256 : base + 384] = dv[p, at, :].astype(bf16)
            return carry

        lax.fori_loop(0, 4, finish, 0)

    def before0(i):
        @pl.when(i == 1)
        def _():
            w_do.wait_one(1)

        @pl.when(i == 2)
        def _():
            w_do.wait_one(2)

        @pl.when(i == 3)
        def _():
            w_do.wait_one(3)

    def after0(i):
        @pl.when(i == 0)
        def _():
            sum_o.far(out_term)

        @pl.when(i == 1)
        def _():
            sum_o.near(out_term)

        @pl.when(i == 2)
        def _():
            d_wu.fold()

        @pl.when(i == 3)
        def _():
            sum_f.cross()

    def after1(i):
        @pl.when(i == 1)
        def _():
            g_wo[...] = sum_o.total(out_term).astype(bf16).reshape(n, own_rows, quarter)
            d_wo.send_x(0, n)

    d_wd.fold()
    back_pair(0, before0, after0)
    make(lambda m: cols_of(xa, m), lambda: dproj[:, :pw], g_q0, d_q0, own_rows)
    back_pair(1, lambda i: None, after1)
    sum_x.wait_send()
    sum_a.far(xa_term)
    d_q0.fold()
    make(lambda m: cols_of(xa, m), lambda: dproj[:, pw:], g_q1, d_q1, own_rows)
    sum_a.near(xa_term)
    ffn = sum_f.total(ffn_term) + bd
    em[s, :, 3 * width :] = jnp.sum(cot[...] * ffn, axis=0, keepdims=True)
    em[s, :, :width] = fsum[2:3, :]
    em[s, :, width : 2 * width] = fsum[0:1, :]
    em[s, :, 2 * width : 3 * width] = fsum[1:2, :]
    e_mod.start()
    block_out[...] = block_out[...] + gate_f * ffn
    leave(block_out, out_hbm, 0).start()
    d_wo.fold()
    e_mod.wait_recv()
    dmb[d, :, 2 * width :] = (em[0] + em[1] + em[2] + em[3]).astype(bf16).astype(f32)
    e_all.start()
    lb[...] = jnp.sum(dproj[...].astype(f32), axis=0, keepdims=True)
    lb_all.start()
    f_wd[s] = d_wd.total().astype(bf16)
    f_wu[s] = d_wu.total().astype(bf16)
    e_all.wait_recv()
    dm_e = jnp.concatenate([dmb[i, :, 2 * width :] for i in range(n)], axis=0).astype(bf16)
    dmat[:, 2 * width :] = dm_e
    dt = nt(dm_e, wm[:, 2 * width :])
    d_q1.fold()
    g = sum_a.total(xa_term)
    n_val = n_in[...]
    lm[s, :, :width] = jnp.sum(g, axis=0, keepdims=True)
    lm[s, :, width:] = jnp.sum(g * n_val, axis=0, keepdims=True)
    l_mod.start()
    o_wd.start()
    o_wu.start()
    grad_input[...] = grad_input[...] + norm_back(g * (1.0 + scale_a), n_val, normed(frames[...])[1])
    leave(grad_input, grad_hbm, 1).start()
    l_mod.wait_recv()
    dmb[d, :, : 2 * width] = (lm[0] + lm[1] + lm[2] + lm[3]).astype(bf16).astype(f32)
    l_all.start()
    f_wo[s] = d_wo.total().astype(bf16)
    o_wo.start()
    f_q0[s] = d_q0.total().astype(bf16)
    o_q0.start()
    eb_all.wait_recv()
    lb_all.wait_recv()
    esum, lsum = eb[...], lb[...]
    for j in range(1, n):
        esum = esum + ebb[(d + j) % n]
        lsum = lsum + lbb[(d + j) % n]
    f_b[s, :, :qw] = lsum
    f_b[s, :, qw:] = esum
    o_b.start()
    l_all.wait_recv()
    dm_l = jnp.concatenate([dmb[i, :, : 2 * width] for i in range(n)], axis=0).astype(bf16)
    dmat[:, : 2 * width] = dm_l
    dt = dt + nt(dm_l, wm[:, : 2 * width])
    for i in range(n):
        dts[i] = dt[i : i + 1]
    t_all.start()
    f_q1[s] = d_q1.total().astype(bf16)
    o_q1.start()
    o_wd.hand_on()
    o_wu.hand_on()
    o_q0.hand_on()
    o_wo.hand_on()
    t_all.wait_recv()
    dtb[d] = dts[d]
    sig = 1.0 / (1.0 + jnp.exp(-tv))
    slope = sig + tv * sig * (1.0 - sig)
    for i in range(n):
        at = slice(i * own_rows, (i + 1) * own_rows)
        grad_time[:, at] = dtb[i] * slope[:, at]
    for o in (o_wu, o_wd, o_q0, o_wo):
        o.wait(l.s1)
        o.wait(l.s3)
    for t in range(4):
        n_mid[t * units : (t + 1) * units, :] = f_wd[t].astype(f32)
    ends = [leave(n_mid.at[: 4 * units], gwd_hbm, 2)]
    ends[0].start()
    o_q1.hand_on()
    if not plain:
        for i in range(n):
            for h in range(2):
                c0 = i // 2 * 128
                pair = half_of_each(
                    f_wu[2 * h, :, c0 : c0 + 128].astype(f32), f_wu[2 * h + 1, :, c0 : c0 + 128].astype(f32), i % 2 == 1
                )
                col = i * 4 * units + 128 * h
                r0 = col // width * own_rows
                n_in[r0 : r0 + own_rows, col % width : col % width + 128] = pair
        for c in range(2):
            ends.append(leave(n_in.at[c * own_rows : (c + 1) * own_rows], gwu_hbm.at[:, c * width : (c + 1) * width], 3 + c))
            ends[-1].start()
    for t in range(4):
        attn_branch[:own_rows, t * quarter : (t + 1) * quarter] = f_wo[t].astype(f32)
    ends.append(leave(attn_branch.at[:own_rows], gwo_hbm, 5))
    ends[-1].start()
    thirds = (cot.at[:own_rows], cot.at[own_rows : 2 * own_rows], attn_branch.at[own_rows : 2 * own_rows])

    def place(p, held_p):
        for t in range(4):
            for j in range(3):
                at = t * quarter + 128 * p
                thirds[j][:, at : at + 128] = held_p[t, :, 128 * j : 128 * j + 128].astype(f32)

    place(0, f_q0)
    o_b.wait_recv()
    if plain:
        bias_out[...] = f_b[...]
    else:
        outs = []
        for i in range(each):
            u = d * each + i
            j, v = u // (width // 128), u % (width // 128)
            outs.append(f_b[v // pairs, :, pl.ds(pl.multiple_of(v % pairs * pw + j * 128, 128), 128)])
        for base in (qw + ff_q, qw + ff_q + width):
            at = pl.ds(pl.multiple_of(base + d * own_rows, 128), own_rows)
            outs.append(f_b[0, :, at] + f_b[1, :, at] + f_b[2, :, at] + f_b[3, :, at])
        at = pl.ds(pl.multiple_of(qw + d // 2 * 128, 128), 128)
        for h in range(2):
            outs.append(half_of_each(f_b[2 * h, :, at], f_b[2 * h + 1, :, at], d % 2 == 1))
        mod_each = 6 * width // n
        at = pl.ds(pl.multiple_of(d * mod_each, 128), mod_each)
        row = dmb[0, :, at]
        for i in range(1, n):
            row = row + dmb[i, :, at]
        outs.append(row)
        o_bq[...] = jnp.concatenate(outs[:each], axis=1).reshape(-1)
        o_bo[...] = outs[each].reshape(-1)
        o_bd[...] = outs[each + 1].reshape(-1)
        o_bu[...] = jnp.concatenate(outs[each + 2 : each + 4], axis=1).reshape(-1)
        o_bm[...] = outs[each + 4].reshape(-1)
    o_q1.wait(l.s1)
    o_q1.wait(l.s3)
    place(1, f_q1)
    for j in range(3):
        ends.append(leave(thirds[j], gwq_hbm.at[:, j * width : (j + 1) * width], 6 + j))
        ends[-1].start()
    leave(block_out, out_hbm, 0).wait()
    leave(grad_input, grad_hbm, 1).wait()
    for c in ends:
        c.wait()
    for c in (
        times, parts, parts2, biases, mods, s_a0, s_a1, a_q0, a_q1, a_wu, a_wd, a_wo, s_x0, s_x1, s_wo, w_do,
        sum_f, sum_o, sum_a, d_q0, d_q1, d_wo, d_wu, d_wd, o_q0, o_q1, o_wo, o_wu, o_wd, e_mod, l_mod, o_b,
        e_all, l_all, eb_all, lb_all, t_all,
    ):
        c.wait_send()


def run_whole(n, plain, clip_len, time_embed, bias, raw, wu_own, frames, cot, w_mod, w_qkv, w_out, w_down):
    rows, width = frames.shape
    item, quarter, own_rows = 4 * rows, width // 4, width // n
    ff_q = w_down.shape[0] * n // 4
    units, heads, pairs = ff_q // n, quarter // 64, quarter // 128
    qw = 3 * quarter
    pw = qw // pairs
    S, V = jax.ShapeDtypeStruct, pltpu.VMEM
    bw = qw + ff_q + 2 * width
    mod_own = 6 * width if plain else 6 * width // n
    bias_wide = bw if plain else 7 * width // n
    wide = V((rows, width), f32)
    outs = [
        S((1, width), f32), S((n, own_rows), bf16), S((n, 6 * width), bf16), S((4, own_rows, ff_q), bf16),
        S((4, 1, bw) if plain else (1, 1, 128), f32), S((3 * own_rows,), f32), S((own_rows,), f32), S((own_rows,), f32),
        S((4 * units,), f32), S((6 * own_rows,), f32), S((rows, width), f32), S((rows, width), f32),
        S((own_rows, 3 * width), f32), S((own_rows, width), f32), S((own_rows, 4 * ff_q), f32), S((4 * units, width), f32),
    ]

    def chain(a, b):
        return [V((n, a, b), bf16), V((n // 2, a, b), bf16), V((n // 2 - 1, a, b), bf16)]

    held = V((6, rows, width), bf16)
    scratch = (
        [V((n, 1, own_rows), f32), V((n, 1, 6 * width), f32)]
        + [wide] * 4
        + [
            V((1, 6 * width), f32), V((8, 128) if plain else (n, own_rows, 128), bf16), V((4, 1, bw), f32),
            V((own_rows, 6 * width), bf16), V((n, own_rows, pw), bf16), V((n, own_rows, pw), bf16),
            V((n, own_rows, ff_q), bf16), V((n, units, width), bf16), V((4, n, own_rows, quarter), bf16),
            V((n, 1, own_rows), f32), V((n, 1, 2 * width), f32), V((n, 1, 2 * width), f32), V((n, 1, width), f32),
            V((n, 1, width), f32), V((n, 1, bias_wide), f32), V((4, 1, width), f32), wide, wide, wide,
            V((item, 128), f32), V((item, 128), f32), V((item, 1), jnp.int32), V((1, item), jnp.int32),
            V((4, rows, width), bf16), V((4, rows, width), bf16), V((4, rows, width), bf16),
            V((item, quarter), bf16), V((item, quarter), bf16), V((item, quarter), bf16),
            V((pairs, 128, item), bf16), V((pairs, 128, item), bf16), V((heads, 1, item), f32),
        ]
        + [V((4, rows, quarter), bf16)] * 3
        + [
            V((item, ff_q), bf16), V((item, ff_q), bf16), V((rows, width), bf16), V((8, width), f32),
            V((pairs, item, 128), f32), V((pairs, item, 128), f32), V((item, qw), bf16),
            V((4, own_rows, pw), bf16), V((4, own_rows, pw), bf16), V((4, own_rows, quarter), bf16),
            V((4, units, width), bf16), held, held, V((6, width, quarter), bf16),
        ]
        + chain(own_rows, pw) + chain(own_rows, pw) + chain(own_rows, quarter) + chain(own_rows, ff_q) + chain(units, width)
        + [
            V((4, 1, 4 * width), f32), V((4, 1, 2 * width), f32), V((1, ff_q + 2 * width), f32),
            V((n, 1, ff_q + 2 * width), f32), V((1, qw), f32), V((n, 1, qw), f32),
            V((n, 1, own_rows), f32), V((n, 1, own_rows), f32),
            pltpu.SemaphoreType.DMA((22 * n + 90,)), pltpu.SemaphoreType.DMA((22 * n + 100,)),
            pltpu.SemaphoreType.DMA((11 + n,)), pltpu.SemaphoreType.DMA((9,)),
        ]
    )
    vm = pl.BlockSpec(memory_space=pltpu.VMEM)
    hb = pl.BlockSpec(memory_space=pl.ANY)
    return pl.pallas_call(
        functools.partial(whole_kernel, n, plain),
        out_shape=outs,
        in_specs=[pl.BlockSpec(memory_space=pltpu.SMEM)] + [vm] * 7 + [hb] * 7,
        out_specs=[vm] * 10 + [hb] * 6,
        scratch_shapes=scratch,
        compiler_params=pltpu.CompilerParams(collective_id=0, has_side_effects=True, vmem_limit_bytes=63 << 20),
    )(clip_len, time_embed, bias, *raw, wu_own, frames, cot, w_mod, w_qkv, w_out, w_down)


def per_device(
    frames, time_embed, clip_len, w_qkv, b_qkv, w_out, b_out, w_up, b_up, w_down, b_down, w_mod, b_mod, cotangent
):
    n = lax.axis_size("dp")
    seq_rank, dp_rank = lax.axis_index("seq"), lax.axis_index("dp")
    rows, width = frames.shape
    quarter = width // 4
    own_rows, ff = w_up.shape
    units = w_down.shape[0] // 4
    pairs = quarter // 128
    ff_q = ff // 4
    qw = 3 * quarter

    plain = own_rows % 128 != 0 or units != 64
    raw = [b_qkv, b_out, b_up, b_down, b_mod]
    bias = time_embed[None]
    if plain:

        def placed(b):
            return lax.dynamic_update_slice(
                jnp.zeros((b.shape[0] * n,), f32), b.astype(f32), (dp_rank * b.shape[0],)
            )

        def mine(value, axis):
            return lax.dynamic_index_in_dim(value, seq_rank, axis, keepdims=False)

        laid = [
            mine(placed(b_qkv).reshape(3, 4, pairs, 128), 1).transpose(1, 0, 2).reshape(-1),
            placed(b_out),
            mine(placed(b_up).reshape(n, 4, units), 1).reshape(-1),
            placed(b_down),
            placed(b_mod),
        ]
        bias = jnp.concatenate(laid).reshape(1, 1, -1)
        wu_own = mine(w_up.reshape(own_rows, n, 4, units), 2).reshape(own_rows, ff_q)
    else:
        wu_own = w_up
    grad_time, tmat, d_mod, f_wu, f_b, *small, block_out, grad_input, s_wq, s_wo, s_wu, s_wd = run_whole(
        n, plain, clip_len, time_embed, bias, raw, wu_own, frames, cotangent, w_mod, w_qkv, w_out, w_down
    )
    gwm = tn(tmat, d_mod)
    if plain:
        s_wu = f_wu.astype(f32).reshape(4, own_rows, n, units).transpose(1, 2, 0, 3).reshape(own_rows, ff)

        def own(value, like):
            size = like.shape[0]
            return lax.dynamic_slice_in_dim(value, dp_rank * size, size, 0)

        bq = f_b[:, 0, :qw].reshape(4, pairs, 3, 128).transpose(2, 0, 1, 3).reshape(-1)
        bu = f_b[:, 0, qw : qw + ff_q].reshape(4, n, units).transpose(1, 0, 2).reshape(-1)
        bo = jnp.sum(f_b[:, 0, qw + ff_q : qw + ff_q + width], axis=0)
        bd = jnp.sum(f_b[:, 0, qw + ff_q + width :], axis=0)
        bq, bo, bu = own(bq, b_qkv), own(bo, b_out), own(bu, b_up)
        bd, bm = own(bd, b_down), own(jnp.sum(d_mod.astype(f32), axis=0), b_mod)
    else:
        bq, bo, bd, bu, bm = small
    return (block_out, grad_input, grad_time, s_wq, bq, s_wo, bo, s_wu, bu, s_wd, bd, gwm, bm)


def solution(mesh):
    placed = (
        P(("dp", "seq"), None),
        P("dp", None),
        P("dp", None),
        P("dp", None),
        P("dp"),
        P("dp", None),
        P("dp"),
        P("dp", None),
        P("dp"),
        P("dp", None),
        P("dp"),
        P("dp", None),
        P("dp"),
        P(("dp", "seq"), None),
    )
    return jax.shard_map(
        per_device,
        mesh=mesh,
        in_specs=placed,
        out_specs=(
            P(("dp", "seq"), None),
            P(("dp", "seq"), None),
            P("dp", None),
            P("dp", None),
            P("dp"),
            P("dp", None),
            P("dp"),
            P("dp", None),
            P("dp"),
            P("dp", None),
            P("dp"),
            P("dp", None),
            P("dp"),
        ),
        check_vma=False,
    )
```
